128 devices in a mesh: dp: 2 (over y_lo), ctx: 16 (over x, z), exp: 4 (over y_hi, core).
Axes of the slice: x: 4, y: 4 (y_hi: 2, y_lo: 2; y = y_hi * 2 + y_lo), z: 4, core: 2. Of those that a mesh axis runs over, the one named last changes fastest.
Arguments:
- tokens: bfloat16 [8, 2048, 1024], P(('dp', 'exp'), 'ctx'), may hold values from -6 to 6
- places: int32 [8, 2048], P(('dp', 'exp')), may hold values from 0 to 2047, as said below
- choices: int32 [8, 2048, 8], P(('dp', 'exp'), 'ctx'), may hold values from 0 to 31, all different within a row; in each aligned block of 128 rows (0 to 127, 128 to 255, ..., all dimensions but the last counted through in order) at most 40 rows name the same one
- cotangent: bfloat16 [8, 2048, 1024], P(('dp', 'exp'), 'ctx'), may hold values from -6 to 6
- attn_gain: bfloat16 [1024], replicated, may hold values from 0.25 to 1.75
- w_query: bfloat16 [1024, 1024], replicated, may hold values from -0.1875 to 0.1875
- w_key: bfloat16 [1024, 512], replicated, may hold values from -0.1875 to 0.1875
- w_value: bfloat16 [1024, 512], replicated, may hold values from -0.1875 to 0.1875
- query_gain: bfloat16 [1024], replicated, may hold values from 0.25 to 1.75
- key_gain: bfloat16 [512], replicated, may hold values from 0.25 to 1.75
- w_out: bfloat16 [1024, 1024], replicated, may hold values from -1.5 to 1.5
- ffn_gain: bfloat16 [1024], replicated, may hold values from 0.25 to 1.75
- w_router: bfloat16 [1024, 32], replicated, may hold values from -0.09375 to 0.09375
- w_gate: bfloat16 [32, 1024, 512], P('ctx', None, 'exp'), may hold values from -0.1875 to 0.1875
- w_up: bfloat16 [32, 1024, 512], P('ctx', None, 'exp'), may hold values from -0.1875 to 0.1875
- w_down: bfloat16 [32, 512, 1024], P('ctx', 'exp'), may hold values from -2 to 2
Outputs:
- out: bfloat16 [8, 2048, 1024], P(('dp', 'exp'), 'ctx')
- input_grad: float32 [8, 2048, 1024], P(('dp', 'exp'), 'ctx')
- attn_gain_grad: float32 [1024], replicated
- w_query_grad: float32 [1024, 1024], replicated
- w_key_grad: float32 [1024, 512], replicated
- w_value_grad: float32 [1024, 512], replicated
- query_gain_grad: float32 [1024], replicated
- key_gain_grad: float32 [512], replicated
- w_out_grad: float32 [1024, 1024], replicated
- ffn_gain_grad: float32 [1024], replicated
- w_router_grad: float32 [1024, 32], replicated
- w_gate_grad: float32 [32, 1024, 512], P('ctx', None, 'exp')
- w_up_grad: float32 [32, 1024, 512], P('ctx', None, 'exp')
- w_down_grad: float32 [32, 512, 1024], P('ctx', 'exp')
The draws below stay inside these ranges and needn't reach their ends.
Inputs may be any that keep to these rules, and one draw needn't show every extreme that they name: Each row of places is a permutation of the positions of its sequence. Split a sequence into 32 runs of 64 consecutive positions; token slots 128 * c to 128 * (c + 1) - 1 hold, in slot order, run b and run 2 * 16 - 1 - b (in either order) for some b, each run ascending. `choices`: each token names 8 different experts. Among the tokens of one device (aligned blocks of 128 token slots of a sequence) no expert is named more than 40 times, a bound that some block reaches.
All inputs are finite; a program needn't handle non-finite values.
Results may differ from the reference program's by a relative error of at most 0.024.
Values may be sent and summed in bfloat16 or wider, within the bound.
No kernel may reach another device: no remote copies, remote signals or barrier semaphores. Data moves between devices by JAX's collectives and lax.ppermute only.
A program may use at most 256 MiB of HBM per device.

```python
import math
import jax
import jax.numpy as jnp
import numpy as np
from jax import lax

D = 1024
HEADS = 16
KV_HEADS = 8
HEAD_DIM = 64
FF = 512
EXPERTS = 32
TOPK = 8
SEQ = 2048
TOK_DEV = 128
SEQS = 8
CAP = 40


def draw_places(key, part):
    key = jax.random.fold_in(key, 11)
    run_count = SEQ // TOK_DEV
    run_len = TOK_DEV // 2

    def one_sequence(subkey):
        perm_key, flip_key = jax.random.split(subkey)
        shuffled = jax.random.permutation(perm_key, run_count).astype(jnp.int32)
        flipped = jax.random.randint(flip_key, (run_count,), 0, 2)
        low_run = shuffled
        high_run = 2 * run_count - 1 - shuffled
        leading = jnp.where(flipped == 1, high_run, low_run)
        trailing = jnp.where(flipped == 1, low_run, high_run)
        runs = jnp.stack([leading, trailing], axis=1).reshape(-1)
        offsets = jnp.arange(run_len, dtype=jnp.int32)
        return (runs[:, None] * run_len + offsets[None, :]).reshape(-1).astype(jnp.int32)
    return jax.vmap(one_sequence)(jax.random.split(key, SEQS))


def block_scale(own_key, shape, cuts, low, largest):
    gain = 1.0
    for dim, blocks in cuts:
        steps = jax.random.uniform(jax.random.fold_in(jax.random.fold_in(own_key, 6), dim), (blocks,), jnp.float32, low / len(cuts), largest / len(cuts))
        gain = gain * jnp.repeat(jnp.exp(steps), shape[dim] // blocks).reshape((-1,) + (1,) * (len(shape) - 1 - dim))
    return gain


def assign_block(key, own, number, rows, amount, top, reach, lean):
    ranking = jax.random.permutation(key, amount)
    crowded, common = load_shares(amount, rows * top, reach, lean, True), load_shares(amount, rows * top, reach, lean, False)
    places = jnp.arange(amount)

    def named(lengths, rotation):
        used = int((lengths > 0).sum())
        fixed = max(1, used // 4)
        moved = fixed + (places - fixed + rotation * (used - fixed)) % max(1, amount - fixed)
        return jnp.zeros((amount,), jnp.int32).at[ranking[jnp.where(places < fixed, places, moved)]].set(jnp.asarray(lengths, jnp.int32))

    lengths = jnp.where(number % 4 == 0, named(crowded, number // 4), named(common, number - number // 4 - 1))
    mixed = jax.random.permutation(jax.random.fold_in(own, 3), amount)
    giver, receiver = mixed[0:amount // 2 * 2:2], mixed[1:amount // 2 * 2:2]
    margin = jnp.minimum(lengths[giver] - 1, reach - lengths[receiver]) // 2
    margin = jnp.where((giver == ranking[0]) | (receiver == ranking[0]) | (lengths[receiver] == 0), 0, jnp.maximum(margin, 0))
    moved = jax.random.randint(jax.random.fold_in(own, 4), (amount // 2,), 0, 1 << 20) % (margin + 1)
    lengths = lengths.at[giver].add(-moved).at[receiver].add(moved)
    labels = jnp.searchsorted(jnp.cumsum(lengths), jnp.arange(rows * top), side="right").astype(jnp.int32)
    listing = labels.reshape(top, rows).T
    listing = listing[jax.random.permutation(jax.random.fold_in(own, 1), rows)]
    rotation = jax.random.randint(jax.random.fold_in(own, 2), (rows, 1), 0, top)
    return jnp.take_along_axis(listing, (jnp.arange(top)[None, :] + rotation) % top, axis=1)


def load_shares(count, total, reach, skew, full):
    weights = [(1 << 20) // math.isqrt(rank ** skew) + 1 for rank in range(1, count + 1)]
    largest = reach if full else min(reach, max(-(-total // count), total * weights[0] // sum(weights)))
    least = 1 if total - largest >= count - 1 else 0
    holding, surplus = [largest] + [least] * (count - 1), total - largest - least * (count - 1)
    while surplus > 0:
        movable = [i for i in range(1, count) if holding[i] < largest] or [i for i in range(1, count) if holding[i] < reach]
        whole, budget = sum([weights[i] for i in movable]), surplus
        for i in movable:
            addition = min(reach - holding[i], max(1, budget * weights[i] // whole), surplus)
            holding[i] = holding[i] + addition
            surplus = surplus - addition
    return np.array(holding)


def gaussian(key, extent, width, reach, cuts=(), held_as=jnp.bfloat16):
    gain = block_scale(key, extent, cuts, -0.22, 0.18) if cuts else 1.0
    values = jax.random.normal(key, extent, jnp.float32) * width * gain
    return jnp.minimum(jnp.maximum(values, -reach), reach).astype(held_as)


def setup_inputs(seed: int = 0) -> dict:
    key_list = jax.random.split(jax.random.key(seed), 17)
    tokens = gaussian(key_list[0], (SEQS, SEQ, D), 1.0, 6.0, ((0, 8), (1, 16)))
    places = draw_places(jax.random.fold_in(key_list[16], 71), 0)
    choices_keys = jax.random.split(jax.random.fold_in(key_list[2], 1), SEQS * SEQ // TOK_DEV)
    choices_turns = jax.random.permutation(jax.random.fold_in(key_list[2], 3), SEQS * SEQ // TOK_DEV)
    choices = jax.vmap(lambda own, number: assign_block(jax.random.fold_in(key_list[2], 2), own, number, TOK_DEV, EXPERTS, TOPK, CAP, 1))(choices_keys, choices_turns).reshape((SEQS, SEQ, TOPK))
    cotangent = gaussian(key_list[3], (SEQS, SEQ, D), 1.0, 6.0, ((0, 8), (1, 16)))
    attn_gain = jnp.clip(1.0 + 0.15 * jax.random.normal(key_list[4], (D,), jnp.float32), 0.25, 1.75).astype(jnp.bfloat16)
    w_query = gaussian(key_list[5], (D, HEADS * HEAD_DIM), D ** -0.5, 0.1875)
    w_key = gaussian(key_list[6], (D, KV_HEADS * HEAD_DIM), D ** -0.5, 0.1875)
    w_value = gaussian(key_list[7], (D, KV_HEADS * HEAD_DIM), D ** -0.5, 0.1875)
    query_gain = jnp.clip(1.0 + 0.15 * jax.random.normal(key_list[8], (HEADS * HEAD_DIM,), jnp.float32), 0.25, 1.75).astype(jnp.bfloat16)
    key_gain = jnp.clip(1.0 + 0.15 * jax.random.normal(key_list[9], (KV_HEADS * HEAD_DIM,), jnp.float32), 0.25, 1.75).astype(jnp.bfloat16)
    w_out = gaussian(key_list[10], (HEADS * HEAD_DIM, D), (D // 64) ** -0.5, 1.5)
    ffn_gain = jnp.clip(1.0 + 0.15 * jax.random.normal(key_list[11], (D,), jnp.float32), 0.25, 1.75).astype(jnp.bfloat16)
    w_router = gaussian(key_list[12], (D, EXPERTS), (4 * D) ** -0.5, 0.09375)
    w_gate = gaussian(key_list[13], (EXPERTS, D, FF), D ** -0.5, 0.1875, ((0, 16), (2, 4)))
    w_up = gaussian(key_list[14], (EXPERTS, D, FF), D ** -0.5, 0.1875, ((0, 16), (2, 4)))
    w_down = gaussian(key_list[15], (EXPERTS, FF, D), (FF // 64) ** -0.5, 2.0, ((0, 16), (1, 4)))
    return dict(tokens=tokens, places=places, choices=choices, cotangent=cotangent, attn_gain=attn_gain, w_query=w_query, w_key=w_key, w_value=w_value, query_gain=query_gain, key_gain=key_gain, w_out=w_out, ffn_gain=ffn_gain, w_router=w_router, w_gate=w_gate, w_up=w_up, w_down=w_down)


EPSILON = 1e-06
HIGHEST = lax.Precision.HIGHEST
MASKED = -1e+30

@jax.custom_vjp
def low(v):
    return lax.optimization_barrier(v.astype(jnp.bfloat16)).astype(jnp.float32)

@jax.custom_vjp
def low_back(v):
    return v

def low_keep(v):
    return (low(v), None)

def low_pass(kept, grad):
    return (grad,)

def back_keep(v):
    return (v, None)

def back_low(kept, grad):
    return (low(grad),)
low.defvjp(low_keep, low_pass)
low_back.defvjp(back_keep, back_low)

def rms_norm(values, gain_vec):
    return values * lax.rsqrt(lax.optimization_barrier(jnp.mean(values * values, axis=-1, keepdims=True)) + EPSILON) * gain_vec

def rotate(matrix, positions, head_count):
    row_count = matrix.shape[0]
    per_head = matrix.reshape(row_count, head_count, HEAD_DIM)
    halfway = HEAD_DIM // 2
    frequency = 10000.0 ** (-jnp.arange(halfway, dtype=jnp.float32) * 2.0 / HEAD_DIM)
    angles = positions.astype(jnp.float32)[:, None] * frequency[None, :]
    cosine = jnp.cos(angles)[:, None, :]
    sine_part = jnp.sin(angles)[:, None, :]
    leading = per_head[..., :halfway]
    trailing = per_head[..., halfway:]
    return jnp.concatenate([leading * cosine - trailing * sine_part, trailing * cosine + leading * sine_part], axis=-1)

def attend(queries, keys, values, positions):
    q_block = min(512, SEQ)
    block_count = SEQ // q_block
    group_size = HEADS // KV_HEADS
    q_split = queries.reshape(block_count, q_block, KV_HEADS, group_size, HEAD_DIM)
    p_split = positions.reshape(block_count, q_block)

    def one_block(item):
        q_part, p_part = item
        scores = jnp.einsum('qkgd,tkd->kgqt', q_part, keys, precision=HIGHEST)
        scores = low_back(scores)
        allowed = p_part[:, None] >= positions[None, :]
        scores = jnp.where(allowed, scores, MASKED)
        running_max = lax.optimization_barrier(jnp.max(scores, axis=-1, keepdims=True))
        running_sum = lax.optimization_barrier(jnp.sum(jnp.exp(scores - running_max), axis=-1, keepdims=True))
        weights = low(jnp.exp(scores - running_max - jnp.log(running_sum)))
        attended = jnp.einsum('kgqt,tkd->qkgd', weights, values, precision=HIGHEST)
        return attended.reshape(q_block, HEADS * HEAD_DIM)
    return lax.map(jax.checkpoint(one_block), (q_split, p_split)).reshape(SEQ, HEADS * HEAD_DIM)

def experts_apply(rows_in, picked, w_gate, w_up, w_down):
    block_count = SEQ // TOK_DEV
    flat_picks = picked.reshape(block_count, TOK_DEV * TOPK)
    chosen_mask = (flat_picks[..., None] == jnp.arange(EXPERTS, dtype=jnp.int32)).astype(jnp.int32)
    earlier = jnp.cumsum(chosen_mask, axis=1) - chosen_mask
    slot_index = lax.optimization_barrier(jnp.sum(earlier * chosen_mask, axis=-1))
    target = (jnp.arange(block_count, dtype=jnp.int32)[:, None] * EXPERTS + flat_picks) * CAP + slot_index
    target = target.reshape(-1).astype(jnp.int32)
    source_rows = jnp.repeat(rows_in, TOPK, axis=0)
    buffer = jnp.zeros((block_count * EXPERTS * CAP, D), jnp.float32).at[target].set(source_rows)
    buffer = buffer.reshape(block_count, EXPERTS, CAP, D)
    gate_act = low_back(jnp.einsum('becd,edf->becf', buffer, w_gate, precision=HIGHEST))
    up_act = low_back(jnp.einsum('becd,edf->becf', buffer, w_up, precision=HIGHEST))
    hidden = low(jax.nn.silu(gate_act) * up_act)
    result = low_back(jnp.einsum('becf,efd->becd', hidden, w_down, precision=HIGHEST))
    return result.reshape(-1, D)[target].reshape(SEQ, TOPK, D)

def layer(inputs, positions, picked, params):
    attn_gain, w_query, w_key, w_value, query_gain, key_gain, w_out, ffn_gain, w_router, w_gate, w_up, w_down = params
    first = low(rms_norm(inputs, attn_gain))
    q_proj = low_back(jnp.dot(first, w_query, precision=HIGHEST))
    k_proj = low_back(jnp.dot(first, w_key, precision=HIGHEST))
    v_proj = low(low_back(jnp.dot(first, w_value, precision=HIGHEST)))
    queries = low(rotate(rms_norm(q_proj, query_gain), positions, HEADS) * HEAD_DIM ** (-0.5))
    keys = low(rotate(rms_norm(k_proj, key_gain), positions, KV_HEADS))
    values = v_proj.reshape(SEQ, KV_HEADS, HEAD_DIM)
    attended = low(low_back(attend(queries, keys, values, positions)))
    branch = low_back(jnp.dot(attended, w_out, precision=HIGHEST))
    middle = inputs + branch
    second = low(rms_norm(middle, ffn_gain))
    logits = jnp.dot(second, w_router, precision=HIGHEST)
    router_probs = jax.nn.softmax(logits, axis=-1)
    gate_values = jnp.take_along_axis(router_probs, picked, axis=-1)
    expert_out = experts_apply(second, picked, w_gate, w_up, w_down)
    return middle + lax.optimization_barrier(jnp.sum(gate_values[..., None] * expert_out, axis=1))

def reference(tokens, places, choices, cotangent, attn_gain, w_query, w_key, w_value, query_gain, key_gain, w_out, ffn_gain, w_router, w_gate, w_up, w_down):
    params = tuple((item.astype(jnp.float32) for item in (attn_gain, w_query, w_key, w_value, query_gain, key_gain, w_out, ffn_gain, w_router, w_gate, w_up, w_down)))

    def per_sequence(running, item):
        seq_tokens, seq_places, seq_picks, seq_grad = item

        def forward(values_in, weights_in):
            return layer(values_in, seq_places, seq_picks, weights_in)
        result, pull = jax.vjp(forward, seq_tokens.astype(jnp.float32), params)
        grad_inputs, grad_params = pull(seq_grad.astype(jnp.float32))
        running = jax.tree.map(lambda left, right: left + right, running, grad_params)
        return (running, (result.astype(jnp.bfloat16), grad_inputs))
    start = jax.tree.map(jnp.zeros_like, params)
    totals, (outputs, input_grads) = lax.scan(per_sequence, start, (tokens, places, choices, cotangent))
    return (outputs, input_grads, totals[0], totals[1], totals[2], totals[3], totals[4], totals[5], totals[6], totals[7], totals[8], totals[9], totals[10], totals[11])
```

```python
import jax
import jax.numpy as jnp
import numpy as np
from jax import lax
from jax.experimental import pallas as pl
from jax.experimental.pallas import tpu as pltpu
from jax.sharding import PartitionSpec as P

HEADS = 16
KV_HEADS = 8
HEAD_DIM = 64
EXPERTS = 32
CAP = 40
EPSILON = 1e-06
MASKED = -1e30
BF = jnp.bfloat16
F32 = jnp.float32
RUN = 64
QB = 256
PART = 208
MISC = 24
VMEM_BYTES = 56 * 1024 * 1024
NT = ((1,), (1,))
TN = ((0,), (0,))
VM = pl.BlockSpec(memory_space=pltpu.VMEM)
SM = pl.BlockSpec(memory_space=pltpu.SMEM)


def dot(a, b, dims=((1,), (0,))):
    return lax.dot_general(a, b, (dims, ((), ())), preferred_element_type=F32)


def call(kernel, outs, ins, name, flops, moved, scratch=(), transcendentals=0):
    return pl.pallas_call(
        kernel,
        out_shape=outs,
        in_specs=ins,
        out_specs=jax.tree.map(lambda _: VM, outs),
        scratch_shapes=list(scratch),
        compiler_params=pltpu.CompilerParams(vmem_limit_bytes=VMEM_BYTES),
        cost_estimate=pl.CostEstimate(
            flops=flops, bytes_accessed=moved, transcendentals=transcendentals
        ),
        name=name,
    )


def like(shape, dtype):
    return jax.ShapeDtypeStruct(shape, dtype)


def inverse_rms(value):
    return lax.rsqrt(jnp.mean(value * value, axis=-1, keepdims=True) + EPSILON)


def row_of(ref):
    return ref[...].astype(F32).reshape(1, -1)


def lanes_of(rows):
    return lax.broadcasted_iota(jnp.int32, (rows, 128), 1)


def swap_halves(tile):
    return pltpu.roll(tile.astype(F32), 64, 1)


def pack_head(wide, head):
    tile = wide[:, 128 * (head // 2) : 128 * (head // 2 + 1)]
    low = lanes_of(RUN) < 64
    if head % 2 == 0:
        return jnp.where(low, tile[:RUN], swap_halves(tile[RUN:]))
    return jnp.where(low, swap_halves(tile[:RUN]), tile[RUN:])


def unpack_heads(even, odd):
    low = lanes_of(RUN) < 64
    even, odd = even.astype(F32), odd.astype(F32)
    return jnp.concatenate(
        [jnp.where(low, even, swap_halves(odd)), jnp.where(low, swap_halves(even), odd)], axis=0
    )


def turn_tables(seq):
    half = HEAD_DIM // 2
    frequency = (10000.0 ** (-np.arange(half) * 2.0 / HEAD_DIM)).astype(np.float32)
    angles = (np.arange(seq, dtype=np.float32)[:, None] * frequency[None, :]).astype(np.float64)
    cosine, sine = np.cos(angles), np.sin(angles)
    ones, zeros = np.ones((seq, 64)), np.zeros((seq, 64))
    return (
        np.concatenate([cosine, cosine, ones], axis=1).astype(np.float32),
        np.concatenate([-sine, sine, zeros], axis=1).astype(np.float32),
    )


def turn(tile, cosine, sine):
    other = jnp.where(lanes_of(tile.shape[0]) < 32, pltpu.roll(tile, 96, 1), pltpu.roll(tile, 32, 1))
    return tile * cosine + other * sine


def pre_kernel(x_ref, gain, wq, wk, wv, q_gain, k_gain, send, first_out, turned_out, q_out, k_out):
    x = x_ref[...].astype(F32)
    wide = x * inverse_rms(x) * row_of(gain)
    first = wide.astype(BF)
    first_out[...] = first
    q = dot(first, wq[...])
    k = dot(first, wk[...])
    v = dot(first, wv[...])
    q_out[...] = q
    k_out[...] = k
    qn = q * inverse_rms(q) * (row_of(q_gain) * HEAD_DIM ** (-0.5))
    kn = k * inverse_rms(k) * row_of(k_gain)
    low = lanes_of(x.shape[0]) < 64
    for h in range(KV_HEADS):
        cut = slice(128 * (h // 2), 128 * (h // 2 + 1))
        kt, vt = kn[:, cut], v[:, cut]
        if h % 2 == 0:
            both = jnp.where(low, kt, swap_halves(vt))
        else:
            both = jnp.where(low, swap_halves(kt), vt)
        both = both.astype(BF)
        send[2 * h, 0 : 2 * RUN, :] = both
        send[2 * h + 1, 0 : 2 * RUN, :] = both
    for d in range(HEADS):
        send[d, 2 * RUN : 3 * RUN, :] = pack_head(qn, d).astype(BF)
    turned_out[...] = jnp.transpose(first.astype(F32)).astype(BF)


def pre(x, gain, wq, wk, wv, q_gain, k_gain):
    rows, width = x.shape
    return call(
        pre_kernel,
        (
            like((HEADS, 3 * RUN, 128), BF),
            like((rows, width), BF),
            like((width, rows), BF),
            like((rows, wq.shape[1]), F32),
            like((rows, wk.shape[1]), F32),
        ),
        [VM] * 7,
        "pre",
        2 * rows * width * 2048,
        6 * 1024 * 1024,
    )(x, gain, wq, wk, wv, q_gain, k_gain)


def attend_kernel(order, inv, recv, cosine, sine, kv_out, q_out, att_out, send_out):
    seq = kv_out.shape[0]
    lane = lanes_of(RUN)

    def gather(b, carry):
        s = order[b]
        c = lax.shift_right_logical(s, 1)
        half = jnp.bitwise_and(s, 1)
        rows = pl.ds(pl.multiple_of(b * RUN, RUN), RUN)
        cos, sin = cosine[rows, :], sine[rows, :]
        kv = recv[c, pl.ds(pl.multiple_of(half * RUN, RUN), RUN), :].astype(F32)
        kv_out[rows, :] = turn(kv, cos, sin).astype(BF)
        tile = recv[c, pl.ds(2 * RUN, RUN), :].astype(F32)
        q = jnp.where(lane < 64, jnp.where(half == 0, tile, swap_halves(tile)), 0.0)
        q_out[rows, :] = turn(q, cos, sin).astype(BF)
        return carry

    lax.fori_loop(0, seq // RUN, gather, 0)
    row = lax.broadcasted_iota(jnp.int32, (QB, QB), 0)
    col = lax.broadcasted_iota(jnp.int32, (QB, QB), 1)
    wide = lanes_of(QB)
    for i in range(seq // QB):
        here = slice(i * QB, (i + 1) * QB)
        end = (i + 1) * QB
        kv = kv_out[:end, :]
        scores = dot(q_out[here, :], kv, NT)
        last = jnp.where(col <= row, scores[:, end - QB :], MASKED)
        scores = last if i == 0 else jnp.concatenate([scores[:, : end - QB], last], axis=1)
        top = jnp.max(scores, axis=1, keepdims=True)
        weights = jnp.exp(scores - top)
        total = jnp.sum(weights, axis=1, keepdims=True)
        attended = dot(weights.astype(BF), kv) / total
        att_out[here, :] = jnp.where(wide == 0, top + jnp.log(total), attended)

    def place(c, carry):
        b0, b1 = inv[2 * c], inv[2 * c + 1]
        first = att_out[pl.ds(pl.multiple_of(b0 * RUN, RUN), RUN), :]
        second = att_out[pl.ds(pl.multiple_of(b1 * RUN, RUN), RUN), :]
        send_out[c] = jnp.where(lane < 64, swap_halves(first), second).astype(BF)
        return carry

    lax.fori_loop(0, send_out.shape[0], place, 0)


def attend(order, inv, recv, cosine, sine):
    n = recv.shape[0]
    seq = n * 128
    return call(
        attend_kernel,
        (
            like((seq, 128), BF),
            like((seq, 128), BF),
            like((seq, 128), F32),
            like((n, RUN, 128), BF),
        ),
        [SM, SM, VM, VM, VM],
        "attend",
        4 * seq * seq * 128 // 2,
        14 * seq * 128,
        transcendentals=seq * seq // 2,
    )(order, inv, recv, cosine, sine)


def attend_back_kernel(
    order, inv, recv, kv_in, q_in, att_in, cosine, sine, send_out, kv_grad_out, g_all, dq_all, dkv_all
):
    seq = kv_in.shape[0]
    lane = lanes_of(RUN)

    def gather(b, carry):
        s = order[b]
        c = lax.shift_right_logical(s, 1)
        half = jnp.bitwise_and(s, 1)
        tile = recv[c].astype(F32)
        g_all[pl.ds(pl.multiple_of(b * RUN, RUN), RUN), :] = jnp.where(
            lane >= 64, jnp.where(half == 1, tile, swap_halves(tile)), 0.0
        ).astype(BF)
        return carry

    lax.fori_loop(0, seq // RUN, gather, 0)
    dkv_all[...] = jnp.zeros_like(dkv_all)
    row = lax.broadcasted_iota(jnp.int32, (QB, QB), 0)
    col = lax.broadcasted_iota(jnp.int32, (QB, QB), 1)
    for i in range(seq // QB):
        here = slice(i * QB, (i + 1) * QB)
        end = (i + 1) * QB
        kv = kv_in[:end, :]
        q = q_in[here, :]
        g = g_all[here, :]
        att = att_in[here, :]
        offset = jnp.sum(att * g.astype(F32), axis=1, keepdims=True)
        scores = dot(q, kv, NT)
        last = jnp.where(col <= row, scores[:, end - QB :], MASKED)
        scores = last if i == 0 else jnp.concatenate([scores[:, : end - QB], last], axis=1)
        weights = jnp.exp(scores - att[:, 0:1])
        grad_weights = dot(g, kv, NT)
        grad_scores = (weights * (grad_weights - offset)).astype(BF)
        dq_all[here, :] = dot(grad_scores, kv)
        dkv_all[:end, :] += dot(grad_scores, q, TN) + dot(weights.astype(BF), g, TN)

    def place(c, carry):
        b0, b1 = inv[2 * c], inv[2 * c + 1]
        r0 = pl.ds(pl.multiple_of(b0 * RUN, RUN), RUN)
        r1 = pl.ds(pl.multiple_of(b1 * RUN, RUN), RUN)
        kv0 = turn(dkv_all[r0, :], cosine[r0, :], -sine[r0, :]).astype(BF)
        kv1 = turn(dkv_all[r1, :], cosine[r1, :], -sine[r1, :]).astype(BF)
        send_out[c, 0:RUN, :] = kv0
        send_out[c, RUN : 2 * RUN, :] = kv1
        kv_grad_out[c, 0:RUN, :] = kv0
        kv_grad_out[c, RUN : 2 * RUN, :] = kv1
        q0 = turn(dq_all[r0, :], cosine[r0, :], -sine[r0, :])
        q1 = turn(dq_all[r1, :], cosine[r1, :], -sine[r1, :])
        both = jnp.where(lane < 64, q0, swap_halves(q1))
        send_out[c, 2 * RUN : 3 * RUN, :] = (both * HEAD_DIM ** (-0.5)).astype(BF)
        return carry

    lax.fori_loop(0, send_out.shape[0], place, 0)


def attend_back(order, inv, recv, kv, q, att, cosine, sine):
    n = recv.shape[0]
    seq = n * 128
    return call(
        attend_back_kernel,
        (like((n, 3 * RUN, 128), BF), like((n, 2 * RUN, 128), BF)),
        [SM, SM] + [VM] * 6,
        "attend_back",
        10 * seq * seq * 128 // 2,
        20 * seq * 128,
        [
            pltpu.VMEM((seq, 128), BF),
            pltpu.VMEM((seq, 128), F32),
            pltpu.VMEM((seq, 128), F32),
        ],
        seq * seq // 2,
    )(order, inv, recv, kv, q, att, cosine, sine)


def slot_masks(slot, pair):
    line = lax.broadcasted_iota(jnp.int32, (2 * CAP, 128), 0).astype(F32)
    left = (line < CAP) & (line == slot[2 * pair : 2 * pair + 1, :])
    right = (line >= CAP) & (line - CAP == slot[2 * pair + 1 : 2 * pair + 2, :])
    return jnp.where(left, 1.0, 0.0).astype(BF), jnp.where(right, 1.0, 0.0).astype(BF)


def expert_kernel(number, rows_ref, g_ref, router_ref, *refs):
    parts, (back_ref, out_a, out_b, kept_ref, hid_ref, ga_ref, gu_ref, gr_ref, gs_ref) = (
        refs[:12],
        refs[12:],
    )
    local = pl.program_id(0)
    e = number[0] + local
    n_ctx = g_ref.shape[0]
    picks = jnp.concatenate([g_ref[c, 128:144, 0:128].astype(F32)[None] for c in range(n_ctx)], 0)
    named = jnp.max(jnp.where(picks[:, :8, :] == e.astype(F32), 1.0, 0.0), axis=1)
    before = lax.broadcasted_iota(jnp.int32, (128, 128), 0) < lax.broadcasted_iota(
        jnp.int32, (128, 128), 1
    )
    slot = dot(named.astype(BF), jnp.where(before, 1.0, 0.0).astype(BF))
    slot = jnp.where(named > 0.0, slot, -1.0)
    for p in range(n_ctx // 2):
        left, right = slot_masks(slot, p)
        gs_ref[2 * CAP * p : 2 * CAP * (p + 1), :] = (
            dot(left, g_ref[2 * p, 0:128, :]) + dot(right, g_ref[2 * p + 1, 0:128, :])
        ).astype(BF)
    rows = jnp.concatenate([rows_ref[c, 0].astype(F32) for c in range(n_ctx)], axis=0).astype(BF)
    kept_ref[0] = rows
    grads = gs_ref[...].astype(F32)
    logits = dot(rows, router_ref[...])
    lane = lax.broadcasted_iota(jnp.int32, logits.shape, 1)
    powers = jnp.exp(logits - jnp.max(logits, axis=1, keepdims=True))
    gate = jnp.sum(jnp.where(lane == e, powers, 0.0), axis=1, keepdims=True) / jnp.sum(
        powers, axis=1, keepdims=True
    )
    w_gate = jnp.concatenate([parts[3 * j][0] for j in range(4)], axis=1)
    w_up = jnp.concatenate([parts[3 * j + 1][0] for j in range(4)], axis=1)
    w_down = jnp.concatenate([parts[3 * j + 2][0] for j in range(4)], axis=0)
    gate_act = dot(rows, w_gate)
    up_act = dot(rows, w_up)
    sig = 1.0 / (1.0 + jnp.exp(-gate_act))
    silu = gate_act * sig
    hidden = (silu * up_act).astype(BF)
    hid_ref[0] = hidden
    expert_out = dot(hidden, w_down)
    out_rows = (gate * expert_out).astype(BF)

    @pl.when(local == 0)
    def _():
        out_a[...] = out_rows

    @pl.when(local == 1)
    def _():
        out_b[...] = out_rows

    grad_gate = jnp.sum(grads * expert_out, axis=1, keepdims=True)
    grad_rows = (gate * grads).astype(BF)
    gr_ref[0] = grad_rows
    grad_hidden = dot(grad_rows, w_down, NT)
    ga = (grad_hidden * up_act * sig * (1.0 + gate_act * (1.0 - sig))).astype(BF)
    gu = (grad_hidden * silu).astype(BF)
    ga_ref[0] = ga
    gu_ref[0] = gu
    back = dot(ga, w_gate, NT) + dot(gu, w_up, NT)
    high = grad_gate.astype(BF).astype(F32)
    lane = lanes_of(rows.shape[0])
    tail = jnp.where(lane == e, high, jnp.where(lane == e + EXPERTS, grad_gate - high, 0.0))
    for c in range(n_ctx):
        cut = slice(CAP * c, CAP * (c + 1))
        back_ref[c, 0, :, 0:1024] = back[cut, :].astype(BF)
        back_ref[c, 0, :, 1024:1152] = tail[cut, :].astype(BF)


def experts(number, rows, g_all, router, parts):
    n_ctx = rows.shape[0]
    n = n_ctx * CAP
    own = lambda w: pl.BlockSpec((1,) + w.shape[1:], lambda i: (i, 0, 0))
    each = lambda width: pl.BlockSpec((1, n, width), lambda i: (i, 0, 0))
    both = lambda width: pl.BlockSpec((n_ctx, 1, CAP, width), lambda i: (0, i, 0, 0))
    once = pl.BlockSpec((n, 1024), lambda i: (0, 0))
    return pl.pallas_call(
        expert_kernel,
        grid=(2,),
        out_shape=(
            like((n_ctx, 2, CAP, 1152), BF),
            like((n, 1024), BF),
            like((n, 1024), BF),
            like((2, n, 1024), BF),
            like((2, n, 512), BF),
            like((2, n, 512), BF),
            like((2, n, 512), BF),
            like((2, n, 1024), BF),
        ),
        in_specs=[SM, both(1024), VM, VM] + [own(w) for w in parts],
        out_specs=(both(1152), once, once, each(1024), each(512), each(512), each(512), each(1024)),
        scratch_shapes=[pltpu.VMEM((n, 1024), BF)],
        compiler_params=pltpu.CompilerParams(vmem_limit_bytes=VMEM_BYTES),
        cost_estimate=pl.CostEstimate(
            flops=24 * n * 1024 * 512, bytes_accessed=32 * 1024 * 1024, transcendentals=2 * n * 512
        ),
        name="experts",
    )(number, rows, g_all, router, *parts)


def weight_grad_kernel(rows_ref, hid_ref, ga_ref, gu_ref, gr_ref, keep, near, far):
    rows = rows_ref[0]
    gate = dot(rows, ga_ref[0], TN)
    up = dot(rows, gu_ref[0], TN)
    down = dot(hid_ref[0], gr_ref[0], TN)
    for j, (ref, at) in enumerate([(keep, 0), (far, 0), (near, 0), (far, 1)]):
        cut = slice(128 * j, 128 * (j + 1))
        ref[at, 0, 0:1024, :] = gate[:, cut].astype(BF)
        ref[at, 0, 1024:2048, :] = up[:, cut].astype(BF)
        for n in range(8):
            ref[at, 0, 2048 + 128 * n : 2176 + 128 * n, :] = down[
                cut, 128 * n : 128 * (n + 1)
            ].astype(BF)


def weight_grads(rows, hid, ga, gu, gr):
    n = rows.shape[1]
    each = lambda v: pl.BlockSpec((1,) + v.shape[1:], lambda i: (i, 0, 0))
    put = lambda k: pl.BlockSpec((k, 1, 3072, 128), lambda i: (0, i, 0, 0))
    return pl.pallas_call(
        weight_grad_kernel,
        grid=(2,),
        out_shape=(
            like((1, 2, 3072, 128), BF),
            like((1, 2, 3072, 128), BF),
            like((2, 2, 3072, 128), BF),
        ),
        in_specs=[each(v) for v in (rows, hid, ga, gu, gr)],
        out_specs=(put(1), put(1), put(2)),
        compiler_params=pltpu.CompilerParams(vmem_limit_bytes=VMEM_BYTES),
        cost_estimate=pl.CostEstimate(
            flops=12 * n * 1024 * 512, bytes_accessed=16 * 1024 * 1024, transcendentals=0
        ),
        name="weight_grads",
    )(rows, hid, ga, gu, gr)


def middle_kernel(heads, x_ref, w_out, gain, spot, attended_out, middle_out, second_out, send_out):
    attended = jnp.concatenate(
        [unpack_heads(heads[2 * t], heads[2 * t + 1]) for t in range(HEADS // 2)], axis=1
    ).astype(BF)
    attended_out[...] = attended
    middle = x_ref[...].astype(F32) + dot(attended, w_out[...])
    middle_out[...] = middle
    second = (middle * inverse_rms(middle) * row_of(gain)).astype(BF)
    second_out[...] = second
    send_out[...] = dot(spot[...], second, TN).astype(BF)


def middle_forward(heads, x, w_out, gain, spot):
    rows, width = x.shape
    return call(
        middle_kernel,
        (
            like((rows, width), BF),
            like((rows, width), F32),
            like((rows, width), BF),
            like((spot.shape[1], width), BF),
        ),
        [VM] * 5,
        "middle",
        2 * rows * width * (1024 + 1280),
        6 * 1024 * 1024,
    )(heads, x, w_out, gain, spot)


def middle_back_kernel(
    spot, back, middle_ref, second, router, gain, g_ref, w_out,
    send, grad_out, branch_out, misc_out,
):
    summed = dot(spot[...], back[...])
    logits = dot(second[...], router[...])
    powers = jnp.exp(logits - jnp.max(logits, axis=1, keepdims=True))
    probs = powers / jnp.sum(powers, axis=1, keepdims=True)
    last = summed[:, 1024:1152]
    grad_sel = (last + pltpu.roll(last, 128 - EXPERTS, 1))[:, :EXPERTS]
    grad_logits = probs * (grad_sel - jnp.sum(probs * grad_sel, axis=1, keepdims=True))
    high = grad_logits.astype(BF)
    rest = (grad_logits - high.astype(F32)).astype(BF)
    upstream = summed[:, :1024] + dot(high, router[...], NT) + dot(rest, router[...], NT)
    middle = middle_ref[...]
    r = inverse_rms(middle)
    hat = middle * r
    gain_part = jnp.sum(upstream * hat, axis=0, keepdims=True)
    router_part = dot(high, second[...], TN) + dot(rest, second[...], TN)
    first = router_part[0:MISC, :]
    last = jnp.concatenate(
        [router_part[MISC:EXPERTS, :], gain_part, jnp.zeros((2 * MISC - EXPERTS - 1, 1024), F32)],
        axis=0,
    )
    low = lanes_of(MISC) < 64
    for d in range(HEADS):
        cut = slice(128 * (d // 2), 128 * (d // 2 + 1))
        a, b = first[:, cut], last[:, cut]
        misc_out[d] = (
            jnp.where(low, a, swap_halves(b)) if d % 2 == 0 else jnp.where(low, swap_halves(a), b)
        )
    scaled = upstream * row_of(gain)
    grad = (
        r * (scaled - hat * jnp.mean(scaled * hat, axis=1, keepdims=True)) + g_ref[...].astype(F32)
    )
    grad_out[...] = grad
    branch = grad.astype(BF)
    branch_out[...] = branch
    att = dot(branch, w_out[...], NT)
    for d in range(HEADS):
        send[d] = pack_head(att, d).astype(BF)


def middle_back(spot, back, middle, second, router, gain, g_low, w_out):
    rows, width = middle.shape
    return call(
        middle_back_kernel,
        (
            like((HEADS, RUN, 128), BF),
            like((rows, width), F32),
            like((rows, width), BF),
            like((HEADS, MISC, 128), F32),
        ),
        [VM] * 8,
        "middle_back",
        2 * rows * width * (1280 + 1024),
        6 * 1024 * 1024,
    )(spot, back, middle, second, router, gain, g_low, w_out)


def out_grad_kernel(packed, branch, out_ref):
    low = lanes_of(128) < 64
    heads = []
    for c in range(packed.shape[0]):
        tile = packed[c].astype(F32)
        tile = jnp.concatenate([tile, swap_halves(tile)], axis=0)
        heads.append(jnp.where(low, tile, 0.0).astype(BF))
    out_ref[...] = dot(jnp.concatenate(heads, axis=0), branch[...], TN)[0:64, :].astype(BF)


def out_grads(packed, branch):
    return call(
        out_grad_kernel,
        like((64, 1024), BF),
        [VM] * 2,
        "out_grads",
        2 * 2048 * 1024 * 128,
        5 * 1024 * 1024,
    )(packed, branch)


def queries_of(recv):
    return jnp.concatenate(
        [
            unpack_heads(recv[2 * t, 2 * RUN : 3 * RUN, :], recv[2 * t + 1, 2 * RUN : 3 * RUN, :])
            for t in range(HEADS // 2)
        ],
        axis=1,
    )


def keys_values_of(recv):
    low = lanes_of(2 * RUN) < 64
    both = [
        recv[2 * j, 0 : 2 * RUN, :].astype(F32) + recv[2 * j + 1, 0 : 2 * RUN, :].astype(F32)
        for j in range(KV_HEADS)
    ]
    keys, values = [], []
    for t in range(KV_HEADS // 2):
        keys.append(jnp.where(low, both[2 * t], swap_halves(both[2 * t + 1])))
        values.append(jnp.where(low, swap_halves(both[2 * t]), both[2 * t + 1]))
    return jnp.concatenate(keys, axis=1), jnp.concatenate(values, axis=1)


def means_kernel(recv, q_ref, k_ref, q_gain, k_gain, misc, out_ref):
    uq = queries_of(recv)
    uk, _ = keys_values_of(recv)
    q, k = q_ref[...], k_ref[...]
    rq, rk = inverse_rms(q), inverse_rms(k)
    mq = jnp.mean(uq * row_of(q_gain) * q, axis=1, keepdims=True) * rq
    mk = jnp.mean(uk * row_of(k_gain) * k, axis=1, keepdims=True) * rk
    lane = lanes_of(q.shape[0])
    columns = jnp.where(lane == 0, rq, jnp.where(lane == 1, mq, jnp.where(lane == 2, rk, mk)))
    rows = jnp.transpose(columns)[0:8, :]
    for d in range(HEADS):
        out_ref[d, 0:8, :] = rows
        out_ref[d, 8 : 8 + MISC, :] = misc[d]


def means(recv, q, k, q_gain, k_gain, misc):
    return call(
        means_kernel,
        like((HEADS, 8 + MISC, 128), F32),
        [VM] * 6,
        "means",
        1 << 20,
        2 * 1024 * 1024,
    )(recv, q, k, q_gain, k_gain, misc)


def input_kernel(
    recv, q_ref, k_ref, x_ref, middle, q_gain, k_gain, gain, wq, wk, wv, out_ref, gains_ref
):
    uq = queries_of(recv)
    uk, dv = keys_values_of(recv)
    q, k = q_ref[...], k_ref[...]
    rq, rk = inverse_rms(q), inverse_rms(k)
    qh, kh = q * rq, k * rk
    q_part = jnp.sum(uq * qh, axis=0, keepdims=True)
    k_part = jnp.sum(uk * kh, axis=0, keepdims=True)
    uq, uk = uq * row_of(q_gain), uk * row_of(k_gain)
    gq = (rq * (uq - qh * jnp.mean(uq * qh, axis=1, keepdims=True))).astype(BF)
    gk = (rk * (uk - kh * jnp.mean(uk * kh, axis=1, keepdims=True))).astype(BF)
    upstream = dot(gq, wq[...], NT) + dot(gk, wk[...], NT) + dot(dv.astype(BF), wv[...], NT)
    x = x_ref[...].astype(F32)
    r = inverse_rms(x)
    hat = x * r
    x_part = jnp.sum(upstream * hat, axis=0, keepdims=True)
    scaled = upstream * row_of(gain)
    out_ref[...] = middle[...] + r * (scaled - hat * jnp.mean(scaled * hat, axis=1, keepdims=True))
    pad = jnp.zeros((1, 64), F32)
    none = jnp.zeros((5, 128), F32)
    for s in range(8):
        cut = slice(128 * s, 128 * (s + 1))
        pair = k_part[:, 128 * (s // 2) : 128 * (s // 2 + 1)]
        if s % 2 == 1:
            pair = swap_halves(jnp.broadcast_to(pair, (8, 128)))[0:1, :]
        third = jnp.concatenate([pair[:, :64], pad], axis=1)
        gains_ref[s] = jnp.concatenate([x_part[:, cut], q_part[:, cut], third, none], axis=0)


def input_back(recv, q, k, x, middle, q_gain, k_gain, gain, wq, wk, wv):
    rows, width = x.shape
    return call(
        input_kernel,
        (like((rows, width), F32), like((8, 8, 128), F32)),
        [VM] * 11,
        "input_back",
        2 * rows * width * 2048,
        8 * 1024 * 1024,
    )(recv, q, k, x, middle, q_gain, k_gain, gain, wq, wk, wv)


def head_grad_kernel(
    even, turned, own, kv_own, kv_other, normed, stats, gain_ref, out_rows, gains, out_ref
):
    n = own.shape[0]
    low = lanes_of(128) < 64
    gain = gain_ref[...]
    total = None
    for p in range(n // 2):
        grads = []
        for c in (2 * p, 2 * p + 1):
            packed = own[c, 2 * RUN : 3 * RUN, :].astype(F32)
            uq = jnp.concatenate([packed, swap_halves(packed)], axis=0)
            both = kv_own[c].astype(F32) + kv_other[c].astype(F32)
            keys = swap_halves(both)
            upstream = jnp.where(low, uq, keys)
            packed = normed[c, 2 * RUN : 3 * RUN, :].astype(F32)
            qn = jnp.concatenate([packed, swap_halves(packed)], axis=0) * HEAD_DIM**0.5
            hat = jnp.where(low, qn, swap_halves(normed[c, 0 : 2 * RUN, :])) / gain
            cols = jnp.transpose(jnp.concatenate([stats[c, 0:8, :]] * 16, axis=0))
            r = jnp.where(low, cols[:, 0:1], cols[:, 2:3])
            m = jnp.where(low, cols[:, 1:2], cols[:, 3:4])
            grad = r * (upstream * gain - hat * m)
            grads.append(jnp.where(low | (even[0] == 1), grad, both).astype(BF))
        left = jnp.concatenate([turned[2 * p], turned[2 * p + 1]], axis=1)
        step = dot(left, jnp.concatenate(grads, axis=0))
        total = step if total is None else total + step
    misc = stats[0, 8 : 8 + MISC, :]
    for c in range(1, n):
        misc = misc + stats[c, 8 : 8 + MISC, :]
    third = MISC // 8
    for s in range(8):
        out_ref[s, 0:128, :] = total[128 * s : 128 * (s + 1), :].astype(BF)
        out_ref[s, 128:192, :] = out_rows[:, 128 * s : 128 * (s + 1)]
        some = jnp.concatenate(
            [misc[third * s : third * (s + 1), :], jnp.zeros((8 - third, 128), F32)], axis=0
        )
        out_ref[s, 192:208, :] = jnp.concatenate([some, gains[s]], axis=0).astype(BF)


def head_grads(even, turned, own, kv_own, kv_other, normed, stats, gain, out_rows, gains):
    return call(
        head_grad_kernel,
        like((8, PART, 128), BF),
        [SM] + [VM] * 9,
        "head_grads",
        2 * 2048 * 1024 * 128,
        8 * 1024 * 1024,
    )(even, turned, own, kv_own, kv_other, normed, stats, gain, out_rows, gains)


def spread_kernel(core, own_ref, other_ref, wq, wk, wv, wo, misc, gains):
    first = core[0] == 0
    n = own_ref.shape[1]
    low = lanes_of(128) < 64
    sums = [None, None]
    for c in range(0, n, 2):
        blocks = []
        for d in (c, c + 1):
            own, other = own_ref[0, d, 0].astype(F32), other_ref[0, d, 0].astype(F32)
            blocks.append((jnp.where(first, own, other), jnp.where(first, other, own)))
        for i in range(2):
            even, odd = blocks[0][i], blocks[1][i]
            down = slice(128 * i, 128 * (i + 1))
            wq[down, 64 * c : 64 * c + 128] = jnp.where(low, even[:128], swap_halves(odd[:128]))
            half = slice(32 * c - 32 * (c % 4), 32 * c - 32 * (c % 4) + 128)
            key, value = even[:128], odd[:128]
            if c % 4 == 0:
                kept = (swap_halves(key), swap_halves(value))
                blocks_kept = kept if i == 0 else blocks_kept + kept
            else:
                before = last_kept[2 * i : 2 * i + 2]
                wk[down, half] = jnp.where(low, before[0], key)
                wv[down, half] = jnp.where(low, before[1], value)
            for d, block in ((c, even), (c + 1, odd)):
                wo[64 * d : 64 * d + 64, down] = block[128:192, :]
                misc[0, i, :, 128 * d : 128 * (d + 1)] = block[192:200, :]
                sums[i] = block[200:208, :] if sums[i] is None else sums[i] + block[200:208, :]
        if c % 4 == 0:
            last_kept = blocks_kept
    gains[0, 0] = sums[0]
    gains[0, 1] = sums[1]


def spread(core, own, other):
    dp, n, y = own.shape[:3]
    block = pl.BlockSpec((1, n, 1, PART, 128), lambda i: (i // y, 0, i % y, 0, 0))
    return pl.pallas_call(
        spread_kernel,
        grid=(dp * y,),
        out_shape=(
            like((1024, 1024), F32),
            like((1024, 512), F32),
            like((1024, 512), F32),
            like((1024, 1024), F32),
            like((dp * y, 2, 8, 128 * n), F32),
            like((dp * y, 2, 8, 128), F32),
        ),
        in_specs=[SM, block, block],
        out_specs=(
            pl.BlockSpec((256, 1024), lambda i: (i, 0)),
            pl.BlockSpec((256, 512), lambda i: (i, 0)),
            pl.BlockSpec((256, 512), lambda i: (i, 0)),
            pl.BlockSpec((1024, 256), lambda i: (0, i)),
            pl.BlockSpec((1, 2, 8, 128 * n), lambda i: (i, 0, 0, 0)),
            pl.BlockSpec((1, 2, 8, 128), lambda i: (i, 0, 0, 0)),
        ),
        compiler_params=pltpu.CompilerParams(vmem_limit_bytes=VMEM_BYTES),
        name="spread",
    )(core, own, other)


def by_ctx(value):
    return lax.all_to_all(value, "ctx", split_axis=0, concat_axis=0, tiled=True)


def swap(value, axis, bit):
    n = lax.axis_size(axis)
    return lax.ppermute(value, axis, [(i, i ^ bit) for i in range(n)])


def held(value):
    return lax.optimization_barrier(value)


def across_chips(value):
    axes = ("dp", "ctx", "exp")
    dp, ctx, exp = (lax.axis_size(a) for a in axes)
    groups = [
        [(d * ctx + c) * exp + 2 * y + core for d in range(dp) for c in range(ctx) for y in range(exp // 2)]
        for core in range(2)
    ]
    return lax.all_to_all(
        value, axes, split_axis=0, concat_axis=0, tiled=True, axis_index_groups=groups
    )


def per_device(
    tokens,
    places,
    choices,
    cotangent,
    attn_gain,
    w_query,
    w_key,
    w_value,
    query_gain,
    key_gain,
    w_out,
    ffn_gain,
    w_router,
    w_gate,
    w_up,
    w_down,
):
    x_low = tokens[0]
    rows = x_low.shape[0]
    ctx = lax.axis_index("ctx")
    exp = lax.axis_index("exp")
    n_ctx = lax.axis_size("ctx")
    n_dp = lax.axis_size("dp")
    core = jnp.bitwise_and(exp, 1).astype(jnp.int32)
    picked = choices[0]
    g_low = cotangent[0]

    inv = places[0, ::RUN] // RUN
    runs = jnp.arange(inv.shape[0], dtype=jnp.int32)
    order = jnp.sum(jnp.where(inv[None, :] == runs[:, None], runs[None, :], 0), axis=1)
    cosine, sine = (jnp.asarray(t) for t in turn_tables(places.shape[1]))

    chosen = jnp.any(picked[:, :, None] == jnp.arange(EXPERTS, dtype=jnp.int32), axis=1)
    tri = jnp.asarray(np.tril(np.ones((rows, rows), np.float32), -1), BF)
    slot = dot(tri, chosen.astype(BF))
    slot = jnp.where(chosen, slot, -1.0).astype(BF)
    column = np.arange(EXPERTS * CAP)
    named = (np.arange(EXPERTS)[:, None] == (column // CAP)[None, :]).astype(np.float32)
    at = dot(slot, jnp.asarray(named, BF))
    spot = (at == jnp.asarray(column % CAP, F32)[None, :]).astype(BF)

    send, first_low, first_turned, q_proj, k_proj = pre(
        x_low, attn_gain, w_query, w_key, w_value, query_gain, key_gain
    )
    mine = (w_gate, w_up, w_down)
    over_y = tuple(swap(w, "exp", 2) for w in mine)
    over_core = tuple(swap(w, "exp", 1) for w in mine)
    g_then, send = held((g_low, send))
    extra = jnp.zeros((16, 1024), BF).at[:8, :128].set(picked.T.astype(BF))
    g_all = lax.all_gather(jnp.concatenate([g_then, extra], axis=0), "ctx")
    recv = by_ctx(send)
    kv_all, q_all, att_all, att_send = attend(order, inv, recv, cosine, sine)
    att_send, over_y, over_core = held((att_send, over_y, over_core))
    over_both = tuple(swap(w, "exp", 1) for w in over_y)
    parts = mine + over_core + over_y + over_both
    heads = by_ctx(att_send)
    attended, middle, second_low, rows_send = middle_forward(heads, x_low, w_out, ffn_gain, spot)
    sent = by_ctx(rows_send.reshape(n_ctx, 2, CAP, -1))
    sent, parts, g_all, first_turned = held((sent, parts, g_all, first_turned))
    turned_all = lax.all_gather(first_turned, "ctx")
    number = jnp.reshape(2 * ctx, (1,)).astype(jnp.int32)
    back, out_a, out_b, *kept = experts(number, sent, g_all, w_router, parts)
    back = by_ctx(back).reshape(EXPERTS * CAP, -1)
    keep, near, far = weight_grads(*kept)
    back, keep, near, far, turned_all = held((back, keep, near, far, turned_all))
    far = swap(far, "exp", 1)
    att_grad_send, grad_middle, branch, misc_part = middle_back(
        spot, back, middle, second_low, w_router, ffn_gain, g_low, w_out
    )
    branch_all = lax.all_gather(branch, "ctx", axis=0, tiled=True)
    grad_recv = by_ctx(att_grad_send)
    near = (near[0].astype(F32) + far[1].astype(F32)).astype(BF)
    keep = (keep[0].astype(F32) + far[0].astype(F32)).astype(BF)
    grad_recv, near, keep, out_a = held((grad_recv, near, keep, out_a))
    near = swap(near, "exp", 2)
    out_a = by_ctx(out_a.reshape(n_ctx, CAP, -1))
    grad_send, kv_own = attend_back(order, inv, grad_recv, kv_all, q_all, att_all, cosine, sine)
    grad_send, out_a = held((grad_send, out_a))
    grads = by_ctx(grad_send)
    kv_other = swap(kv_own, "ctx", 1)
    keep = (keep.astype(F32) + near.astype(F32)).astype(BF)
    grads, keep = held((grads, keep))
    over_dp = swap(keep, "dp", 1)
    stats = by_ctx(means(grads, q_proj, k_proj, query_gain, key_gain, misc_part))
    out_rows = out_grads(att_send, branch_all)
    stats, out_rows = held((stats, out_rows))
    input_grad, gains = input_back(
        grads, q_proj, k_proj, x_low, grad_middle, query_gain, key_gain, attn_gain, w_query, w_key, w_value
    )
    own_gain = jnp.concatenate(
        [
            lax.dynamic_slice_in_dim(query_gain, ctx * HEAD_DIM, HEAD_DIM),
            lax.dynamic_slice_in_dim(key_gain, ctx // 2 * HEAD_DIM, HEAD_DIM),
        ]
    ).astype(F32)[None]
    even = jnp.reshape(1 - jnp.bitwise_and(ctx, 1), (1,)).astype(jnp.int32)
    shares = head_grads(
        even, turned_all, grad_send, kv_own, kv_other, recv, stats, own_gain, out_rows, gains
    )
    shares = lax.all_to_all(shares, ("dp", "exp"), split_axis=0, concat_axis=0, tiled=True)
    share = jnp.sum(shares.astype(F32), axis=0).astype(BF)
    share, over_dp = held((share, over_dp))
    expert_sum = keep.astype(F32) + over_dp.astype(F32)
    grad_gate_w = expert_sum[:, :1024]
    grad_up_w = expert_sum[:, 1024:2048]
    grad_down_w = (
        expert_sum[:, 2048:].reshape(2, 8, 128, 128).transpose(0, 2, 1, 3).reshape(2, 128, 1024)
    )
    chips = n_dp * n_ctx * 2
    whole = across_chips(jnp.broadcast_to(share[None], (chips,) + share.shape))
    spot = spot.reshape(rows, n_ctx, 2, CAP)
    spot_a, spot_b = (spot[:, :, a].reshape(rows, -1) for a in range(2))
    outputs = middle + dot(spot_a, out_a.reshape(n_ctx * CAP, -1))
    whole, outputs, out_b, grad_gate_w, grad_up_w, grad_down_w = held(
        (whole, outputs, out_b, grad_gate_w, grad_up_w, grad_down_w)
    )
    other = swap(whole, "exp", 1)
    out_b = by_ctx(out_b.reshape(n_ctx, CAP, -1))
    shape = (n_dp, n_ctx, 2, PART, 128)
    wq, wk, wv, wo, misc, gain_sums = spread(
        jnp.reshape(core, (1,)), whole.reshape(shape), other.reshape(shape)
    )
    gain_sums = gain_sums.reshape(8, 8, 128)
    misc = misc.reshape(8, 8, n_ctx, 2, 64)[:, : MISC // 8]
    misc = misc.transpose(3, 0, 1, 2, 4).reshape(2 * MISC, 1024)
    outputs = outputs + dot(spot_b, out_b.reshape(n_ctx * CAP, -1))
    return (
        outputs.astype(BF)[None],
        input_grad[None],
        gain_sums[:, 0].reshape(1024),
        wq,
        wk,
        wv,
        gain_sums[:, 1].reshape(1024),
        gain_sums[:, 2, :64].reshape(512),
        wo,
        misc[EXPERTS],
        misc[:EXPERTS].T,
        grad_gate_w,
        grad_up_w,
        grad_down_w,
    )


def solution(mesh):
    seqs = ("dp", "exp")
    row_spec = P(seqs, "ctx", None)
    in_specs = (row_spec, P(seqs, None), row_spec, row_spec) + (P(),) * 9
    in_specs += (P("ctx", None, "exp"), P("ctx", None, "exp"), P("ctx", "exp", None))
    out_specs = (row_spec, row_spec) + (P(),) * 9
    out_specs += (P("ctx", None, "exp"), P("ctx", None, "exp"), P("ctx", "exp", None))
    return jax.shard_map(
        per_device, mesh=mesh, in_specs=in_specs, out_specs=out_specs, check_vma=False
    )
```

```python
import jax
import jax.numpy as jnp
import numpy as np
from jax import lax
from jax.experimental import pallas as pl
from jax.experimental.pallas import tpu as pltpu
from jax.sharding import PartitionSpec as P

HEADS = 16
KV_HEADS = 8
HEAD_DIM = 64
EXPERTS = 32
CAP = 40
EPSILON = 1e-06
MASKED = -1e30
BF = jnp.bfloat16
F32 = jnp.float32
RUN = 64
QB = 256
PART = 208
MIB = 1024 * 1024
NT = ((1,), (1,))
TN = ((0,), (0,))
VM = pl.BlockSpec(memory_space=pltpu.VMEM)
SM = pl.BlockSpec(memory_space=pltpu.SMEM)


def dot(a, b, dims=((1,), (0,))):
    return lax.dot_general(a, b, (dims, ((), ())), preferred_element_type=F32)


def call(kernel, outs, ins, name, flops, moved, scratch=(), transcendentals=0, vmem=56):
    return pl.pallas_call(
        kernel,
        out_shape=outs,
        in_specs=ins,
        out_specs=jax.tree.map(lambda _: VM, outs),
        scratch_shapes=list(scratch),
        compiler_params=pltpu.CompilerParams(vmem_limit_bytes=vmem * MIB),
        cost_estimate=pl.CostEstimate(
            flops=flops, bytes_accessed=moved, transcendentals=transcendentals
        ),
        name=name,
    )


def like(shape, dtype):
    return jax.ShapeDtypeStruct(shape, dtype)


def inverse_rms(value):
    return lax.rsqrt(jnp.mean(value * value, axis=-1, keepdims=True) + EPSILON)


def row_of(ref):
    return ref[...].astype(F32).reshape(1, -1)


def lanes_of(rows):
    return lax.broadcasted_iota(jnp.int32, (rows, 128), 1)


def swap_halves(tile):
    return pltpu.roll(tile.astype(F32), 64, 1)


def pack_head(wide, head):
    tile = wide[:, 128 * (head // 2) : 128 * (head // 2 + 1)]
    low = lanes_of(RUN) < 64
    if head % 2 == 0:
        return jnp.where(low, tile[:RUN], swap_halves(tile[RUN:]))
    return jnp.where(low, swap_halves(tile[:RUN]), tile[RUN:])


def unpack_heads(even, odd):
    low = lanes_of(RUN) < 64
    even, odd = even.astype(F32), odd.astype(F32)
    return jnp.concatenate(
        [jnp.where(low, even, swap_halves(odd)), jnp.where(low, swap_halves(even), odd)], axis=0
    )


def turn_tables(seq):
    half = HEAD_DIM // 2
    frequency = (10000.0 ** (-np.arange(half) * 2.0 / HEAD_DIM)).astype(np.float32)
    angles = (np.arange(seq, dtype=np.float32)[:, None] * frequency[None, :]).astype(np.float64)
    cosine, sine = np.cos(angles), np.sin(angles)
    ones, zeros = np.ones((seq, 64)), np.zeros((seq, 64))
    return (
        np.concatenate([cosine, cosine, ones], axis=1).astype(np.float32),
        np.concatenate([-sine, sine, zeros], axis=1).astype(np.float32),
    )


def turn(tile, cosine, sine):
    other = jnp.where(lanes_of(tile.shape[0]) < 32, pltpu.roll(tile, 96, 1), pltpu.roll(tile, 32, 1))
    return tile * cosine + other * sine


def pre_kernel(x_ref, gain, wq, wk, wv, q_gain, k_gain, picks, send, first_out, turned_out, q_out, k_out):
    x = x_ref[...].astype(F32)
    wide = x * inverse_rms(x) * row_of(gain)
    first = wide.astype(BF)
    first_out[...] = first
    q = dot(first, wq[...])
    k = dot(first, wk[...])
    v = dot(first, wv[...])
    q_out[...] = q
    k_out[...] = k
    qn = q * inverse_rms(q) * (row_of(q_gain) * HEAD_DIM ** (-0.5))
    kn = k * inverse_rms(k) * row_of(k_gain)
    low = lanes_of(x.shape[0]) < 64
    for h in range(KV_HEADS):
        cut = slice(128 * (h // 2), 128 * (h // 2 + 1))
        kt, vt = kn[:, cut], v[:, cut]
        if h % 2 == 0:
            both = jnp.where(low, kt, swap_halves(vt))
        else:
            both = jnp.where(low, swap_halves(kt), vt)
        both = both.astype(BF)
        send[2 * h, 0 : 2 * RUN, :] = both
        send[2 * h + 1, 0 : 2 * RUN, :] = both
    named = jnp.concatenate([picks[...].astype(F32), jnp.zeros((8, 128), F32)], axis=0).astype(BF)
    for d in range(HEADS):
        send[d, 2 * RUN : 3 * RUN, :] = pack_head(qn, d).astype(BF)
        send[d, 3 * RUN : 3 * RUN + 16, :] = named
    turned_out[...] = jnp.transpose(first.astype(F32)).astype(BF)


def pre(x, gain, wq, wk, wv, q_gain, k_gain, picks):
    rows, width = x.shape
    return call(
        pre_kernel,
        (
            like((HEADS, 3 * RUN + 16, 128), BF),
            like((rows, width), BF),
            like((width, rows), BF),
            like((rows, wq.shape[1]), F32),
            like((rows, wk.shape[1]), F32),
        ),
        [VM] * 8,
        "pre",
        2 * rows * width * 2048,
        6 * 1024 * 1024,
    )(x, gain, wq, wk, wv, q_gain, k_gain, picks)


def attend_kernel(order, inv, recv, cosine, sine, kv_out, q_out, att_out, send_out):
    seq = kv_out.shape[0]
    lane = lanes_of(RUN)

    def gather(b, carry):
        s = order[b]
        c = lax.shift_right_logical(s, 1)
        half = jnp.bitwise_and(s, 1)
        rows = pl.ds(pl.multiple_of(b * RUN, RUN), RUN)
        cos, sin = cosine[rows, :], sine[rows, :]
        kv = recv[c, pl.ds(pl.multiple_of(half * RUN, RUN), RUN), :].astype(F32)
        kv_out[rows, :] = turn(kv, cos, sin).astype(BF)
        tile = recv[c, pl.ds(2 * RUN, RUN), :].astype(F32)
        q = jnp.where(lane < 64, jnp.where(half == 0, tile, swap_halves(tile)), 0.0)
        q_out[rows, :] = turn(q, cos, sin).astype(BF)
        return carry

    lax.fori_loop(0, seq // RUN, gather, 0)
    row = lax.broadcasted_iota(jnp.int32, (QB, QB), 0)
    col = lax.broadcasted_iota(jnp.int32, (QB, QB), 1)
    wide = lanes_of(QB)
    for i in range(seq // QB):
        here = slice(i * QB, (i + 1) * QB)
        end = (i + 1) * QB
        kv = kv_out[:end, :]
        scores = dot(q_out[here, :], kv, NT)
        last = jnp.where(col <= row, scores[:, end - QB :], MASKED)
        scores = last if i == 0 else jnp.concatenate([scores[:, : end - QB], last], axis=1)
        top = jnp.max(scores, axis=1, keepdims=True)
        weights = jnp.exp(scores - top)
        total = jnp.sum(weights, axis=1, keepdims=True)
        attended = dot(weights.astype(BF), kv) / total
        att_out[here, :] = jnp.where(wide == 0, top + jnp.log(total), attended)

    def place(c, carry):
        b0, b1 = inv[2 * c], inv[2 * c + 1]
        first = att_out[pl.ds(pl.multiple_of(b0 * RUN, RUN), RUN), :]
        second = att_out[pl.ds(pl.multiple_of(b1 * RUN, RUN), RUN), :]
        send_out[c] = jnp.where(lane < 64, swap_halves(first), second).astype(BF)
        return carry

    lax.fori_loop(0, send_out.shape[0], place, 0)


def attend(order, inv, recv, cosine, sine):
    n = recv.shape[0]
    seq = n * 128
    return call(
        attend_kernel,
        (
            like((seq, 128), BF),
            like((seq, 128), BF),
            like((seq, 128), F32),
            like((n, RUN, 128), BF),
        ),
        [SM, SM, VM, VM, VM],
        "attend",
        4 * seq * seq * 128 // 2,
        14 * seq * 128,
        transcendentals=seq * seq // 2,
    )(order, inv, recv, cosine, sine)


def attend_back_kernel(
    order, inv, recv, kv_in, q_in, att_in, cosine, sine, send_out, kv_grad_out, g_all, dq_all, dkv_all
):
    seq = kv_in.shape[0]
    lane = lanes_of(RUN)

    def gather(b, carry):
        s = order[b]
        c = lax.shift_right_logical(s, 1)
        half = jnp.bitwise_and(s, 1)
        tile = recv[c].astype(F32)
        g_all[pl.ds(pl.multiple_of(b * RUN, RUN), RUN), :] = jnp.where(
            lane >= 64, jnp.where(half == 1, tile, swap_halves(tile)), 0.0
        ).astype(BF)
        return carry

    lax.fori_loop(0, seq // RUN, gather, 0)
    dkv_all[...] = jnp.zeros_like(dkv_all)
    row = lax.broadcasted_iota(jnp.int32, (QB, QB), 0)
    col = lax.broadcasted_iota(jnp.int32, (QB, QB), 1)
    for i in range(seq // QB):
        here = slice(i * QB, (i + 1) * QB)
        end = (i + 1) * QB
        kv = kv_in[:end, :]
        q = q_in[here, :]
        g = g_all[here, :]
        att = att_in[here, :]
        offset = jnp.sum(att * g.astype(F32), axis=1, keepdims=True)
        scores = dot(q, kv, NT)
        last = jnp.where(col <= row, scores[:, end - QB :], MASKED)
        scores = last if i == 0 else jnp.concatenate([scores[:, : end - QB], last], axis=1)
        weights = jnp.exp(scores - att[:, 0:1])
        grad_weights = dot(g, kv, NT)
        grad_scores = (weights * (grad_weights - offset)).astype(BF)
        dq_all[here, :] = dot(grad_scores, kv)
        dkv_all[:end, :] += dot(grad_scores, q, TN) + dot(weights.astype(BF), g, TN)

    def place(c, carry):
        b0, b1 = inv[2 * c], inv[2 * c + 1]
        r0 = pl.ds(pl.multiple_of(b0 * RUN, RUN), RUN)
        r1 = pl.ds(pl.multiple_of(b1 * RUN, RUN), RUN)
        kv0 = turn(dkv_all[r0, :], cosine[r0, :], -sine[r0, :]).astype(BF)
        kv1 = turn(dkv_all[r1, :], cosine[r1, :], -sine[r1, :]).astype(BF)
        send_out[c, 0:RUN, :] = kv0
        send_out[c, RUN : 2 * RUN, :] = kv1
        kv_grad_out[c, 0:RUN, :] = kv0
        kv_grad_out[c, RUN : 2 * RUN, :] = kv1
        q0 = turn(dq_all[r0, :], cosine[r0, :], -sine[r0, :])
        q1 = turn(dq_all[r1, :], cosine[r1, :], -sine[r1, :])
        both = jnp.where(lane < 64, q0, swap_halves(q1))
        send_out[c, 2 * RUN : 3 * RUN, :] = (both * HEAD_DIM ** (-0.5)).astype(BF)
        return carry

    lax.fori_loop(0, send_out.shape[0], place, 0)


def attend_back(order, inv, recv, kv, q, att, cosine, sine):
    n = recv.shape[0]
    seq = n * 128
    return call(
        attend_back_kernel,
        (like((n, 3 * RUN, 128), BF), like((n, 2 * RUN, 128), BF)),
        [SM, SM] + [VM] * 6,
        "attend_back",
        10 * seq * seq * 128 // 2,
        20 * seq * 128,
        [
            pltpu.VMEM((seq, 128), BF),
            pltpu.VMEM((seq, 128), F32),
            pltpu.VMEM((seq, 128), F32),
        ],
        seq * seq // 2,
    )(order, inv, recv, kv, q, att, cosine, sine)


def slot_masks(slot, pair):
    line = lax.broadcasted_iota(jnp.int32, (2 * CAP, 128), 0).astype(F32)
    left = (line < CAP) & (line == slot[2 * pair : 2 * pair + 1, :])
    right = (line >= CAP) & (line - CAP == slot[2 * pair + 1 : 2 * pair + 2, :])
    return jnp.where(left, 1.0, 0.0).astype(BF), jnp.where(right, 1.0, 0.0).astype(BF)


def expert_kernel(number, rows_ref, picks_ref, g_ref, router_ref, *refs):
    parts, (back_ref, out_ref, kept_ref, hid_ref, ga_ref, gu_ref, gr_ref, slot_ref, gs_ref) = (
        refs[:4],
        refs[4:],
    )
    local = pl.program_id(0)
    e = number[0] + local
    n_ctx = g_ref.shape[0]
    picks = picks_ref[...].astype(F32)[:, :8, :]
    named = jnp.max(jnp.where(picks == e.astype(F32), 1.0, 0.0), axis=1)
    before = lax.broadcasted_iota(jnp.int32, (128, 128), 0) < lax.broadcasted_iota(
        jnp.int32, (128, 128), 1
    )
    slot = dot(named.astype(BF), jnp.where(before, 1.0, 0.0).astype(BF))
    slot = jnp.where(named > 0.0, slot, -1.0)
    slot_ref[0] = slot
    for p in range(n_ctx // 2):
        left, right = slot_masks(slot, p)
        gs_ref[2 * CAP * p : 2 * CAP * (p + 1), :] = (
            dot(left, g_ref[2 * p]) + dot(right, g_ref[2 * p + 1])
        ).astype(BF)
    rows = jnp.concatenate([rows_ref[c, 0].astype(F32) for c in range(n_ctx)], axis=0).astype(BF)
    kept_ref[0] = rows
    grads = gs_ref[...].astype(F32)
    logits = dot(rows, router_ref[...], NT)
    lane = lax.broadcasted_iota(jnp.int32, logits.shape, 1)
    powers = jnp.exp(logits - jnp.max(logits, axis=1, keepdims=True))
    gate = jnp.sum(jnp.where(lane == e, powers, 0.0), axis=1, keepdims=True) / jnp.sum(
        powers, axis=1, keepdims=True
    )
    w_gate = jnp.concatenate([w[0, 0:1024, :] for w in parts], axis=1)
    w_up = jnp.concatenate([w[0, 1024:2048, :] for w in parts], axis=1)
    w_down = jnp.concatenate(
        [
            jnp.concatenate([w[0, 2048 + 128 * n : 2176 + 128 * n, :] for n in range(8)], axis=1)
            for w in parts
        ],
        axis=0,
    )
    gate_act = dot(rows, w_gate)
    up_act = dot(rows, w_up)
    sig = 1.0 / (1.0 + jnp.exp(-gate_act))
    silu = gate_act * sig
    hidden = (silu * up_act).astype(BF)
    hid_ref[0] = hidden
    expert_out = dot(hidden, w_down)
    out_rows = gate * expert_out
    for c in range(n_ctx):
        out_ref[c, 0] = out_rows[CAP * c : CAP * (c + 1), :].astype(BF)
    grad_gate = jnp.sum(grads * expert_out, axis=1, keepdims=True)
    grad_rows = (gate * grads).astype(BF)
    gr_ref[0] = grad_rows
    grad_hidden = dot(grad_rows, w_down, NT)
    ga = (grad_hidden * up_act * sig * (1.0 + gate_act * (1.0 - sig))).astype(BF)
    gu = (grad_hidden * silu).astype(BF)
    ga_ref[0] = ga
    gu_ref[0] = gu
    back = dot(ga, w_gate, NT) + dot(gu, w_up, NT)
    high = grad_gate.astype(BF).astype(F32)
    lane = lanes_of(rows.shape[0])
    tail = jnp.where(lane == e, high, jnp.where(lane == e + EXPERTS, grad_gate - high, 0.0))
    for c in range(n_ctx):
        cut = slice(CAP * c, CAP * (c + 1))
        back_ref[c, 0, :, 0:1024] = back[cut, :].astype(BF)
        back_ref[c, 0, :, 1024:1152] = tail[cut, :].astype(BF)


def experts(number, rows, recv, g_all, router, parts):
    n_ctx = rows.shape[0]
    n = n_ctx * CAP
    own = lambda w: pl.BlockSpec((1,) + w.shape[1:], lambda i: (i, 0, 0))
    each = lambda width: pl.BlockSpec((1, n, width), lambda i: (i, 0, 0))
    both = lambda width: pl.BlockSpec((n_ctx, 1, CAP, width), lambda i: (0, i, 0, 0))
    return pl.pallas_call(
        expert_kernel,
        grid=(2,),
        out_shape=(
            like((n_ctx, 2, CAP, 1152), BF),
            like((n_ctx, 2, CAP, 1024), BF),
            like((2, n, 1024), BF),
            like((2, n, 512), BF),
            like((2, n, 512), BF),
            like((2, n, 512), BF),
            like((2, n, 1024), BF),
            like((2, n_ctx, 128), F32),
        ),
        in_specs=[SM, both(1024), pl.BlockSpec((n_ctx, 16, 128), lambda i: (0, 3 * RUN // 16, 0)), VM, VM]
        + [own(w) for w in parts],
        out_specs=(
            both(1152),
            both(1024),
            each(1024),
            each(512),
            each(512),
            each(512),
            each(1024),
            pl.BlockSpec((1, n_ctx, 128), lambda i: (i, 0, 0)),
        ),
        scratch_shapes=[pltpu.VMEM((n, 1024), BF)],
        compiler_params=pltpu.CompilerParams(vmem_limit_bytes=56 * MIB),
        cost_estimate=pl.CostEstimate(
            flops=24 * n * 1024 * 512, bytes_accessed=32 * 1024 * 1024, transcendentals=2 * n * 512
        ),
        name="experts",
    )(number, rows, recv, g_all, router, *parts)


def weight_grad_kernel(rows_ref, hid_ref, ga_ref, gu_ref, gr_ref, keep, near, far):
    rows = rows_ref[0]
    gate = dot(rows, ga_ref[0], TN)
    up = dot(rows, gu_ref[0], TN)
    down = dot(hid_ref[0], gr_ref[0], TN)
    for j, (ref, at) in enumerate([(keep, 0), (far, 0), (near, 0), (far, 1)]):
        cut = slice(128 * j, 128 * (j + 1))
        ref[at, 0, 0:1024, :] = gate[:, cut].astype(BF)
        ref[at, 0, 1024:2048, :] = up[:, cut].astype(BF)
        for n in range(8):
            ref[at, 0, 2048 + 128 * n : 2176 + 128 * n, :] = down[
                cut, 128 * n : 128 * (n + 1)
            ].astype(BF)


def weight_grads(rows, hid, ga, gu, gr):
    n = rows.shape[1]
    each = lambda v: pl.BlockSpec((1,) + v.shape[1:], lambda i: (i, 0, 0))
    put = lambda k: pl.BlockSpec((k, 1, 3072, 128), lambda i: (0, i, 0, 0))
    return pl.pallas_call(
        weight_grad_kernel,
        grid=(2,),
        out_shape=(
            like((1, 2, 3072, 128), BF),
            like((1, 2, 3072, 128), BF),
            like((2, 2, 3072, 128), BF),
        ),
        in_specs=[each(v) for v in (rows, hid, ga, gu, gr)],
        out_specs=(put(1), put(1), put(2)),
        compiler_params=pltpu.CompilerParams(vmem_limit_bytes=56 * MIB),
        cost_estimate=pl.CostEstimate(
            flops=1 << 20, bytes_accessed=1 << 20, transcendentals=0
        ),
        name="weight_grads",
    )(rows, hid, ga, gu, gr)


def scatter_kernel(slot_ref, rows_ref, out_ref):
    line = lax.broadcasted_iota(jnp.int32, (CAP, 128), 0).astype(F32)
    for c in range(out_ref.shape[0]):
        total = None
        for a in range(2):
            mask = jnp.where(line == slot_ref[a, c : c + 1, :], 1.0, 0.0).astype(BF)
            part = dot(mask, rows_ref[c, a], TN)
            total = part if total is None else total + part
        out_ref[c] = total.astype(BF)


def scatter_rows(slot, rows):
    n = rows.shape[0]
    return call(
        scatter_kernel,
        like((n, 128, 1024), BF),
        [VM] * 2,
        "scatter_rows",
        1 << 20,
        1 << 20,
    )(slot, rows)


def middle_kernel(heads, x_ref, w_out, gain, spot, attended_out, middle_out, second_out, send_out):
    attended = jnp.concatenate(
        [unpack_heads(heads[2 * t], heads[2 * t + 1]) for t in range(HEADS // 2)], axis=1
    ).astype(BF)
    attended_out[...] = attended
    middle = x_ref[...].astype(F32) + dot(attended, w_out[...])
    middle_out[...] = middle
    second = (middle * inverse_rms(middle) * row_of(gain)).astype(BF)
    second_out[...] = second
    send_out[...] = dot(spot[...], second, TN).astype(BF)


def middle_forward(heads, x, w_out, gain, spot):
    rows, width = x.shape
    return call(
        middle_kernel,
        (
            like((rows, width), BF),
            like((rows, width), F32),
            like((rows, width), BF),
            like((spot.shape[1], width), BF),
        ),
        [VM] * 5,
        "middle",
        2 * rows * width * (1024 + 1280),
        6 * 1024 * 1024,
    )(heads, x, w_out, gain, spot)


def middle_back_kernel(
    spot, back, middle_ref, second, router, gain, g_ref, w_out,
    send, grad_out, branch_out, misc_out, gain_out,
):
    summed = dot(spot[...], back[...])
    logits = dot(second[...], router[...], NT)
    powers = jnp.exp(logits - jnp.max(logits, axis=1, keepdims=True))
    probs = powers / jnp.sum(powers, axis=1, keepdims=True)
    last = summed[:, 1024:1152]
    grad_sel = (last + pltpu.roll(last, 128 - EXPERTS, 1))[:, :EXPERTS]
    grad_logits = probs * (grad_sel - jnp.sum(probs * grad_sel, axis=1, keepdims=True))
    high = grad_logits.astype(BF)
    rest = (grad_logits - high.astype(F32)).astype(BF)
    upstream = summed[:, :1024] + dot(high, router[...]) + dot(rest, router[...])
    middle = middle_ref[...]
    r = inverse_rms(middle)
    hat = middle * r
    gain_out[...] = jnp.sum(upstream * hat, axis=0, keepdims=True)
    router_part = dot(high, second[...], TN) + dot(rest, second[...], TN)
    low = lanes_of(EXPERTS) < 64
    for d in range(HEADS):
        tile = router_part[:, 128 * (d // 2) : 128 * (d // 2 + 1)]
        misc_out[d] = jnp.where(low, tile if d % 2 == 0 else swap_halves(tile), 0.0)
    scaled = upstream * row_of(gain)
    grad = (
        r * (scaled - hat * jnp.mean(scaled * hat, axis=1, keepdims=True)) + g_ref[...].astype(F32)
    )
    grad_out[...] = grad
    branch = grad.astype(BF)
    branch_out[...] = branch
    att = dot(branch, w_out[...], NT)
    for d in range(HEADS):
        send[d] = pack_head(att, d).astype(BF)


def middle_back(spot, back, middle, second, router, gain, g_low, w_out):
    rows, width = middle.shape
    return call(
        middle_back_kernel,
        (
            like((HEADS, RUN, 128), BF),
            like((rows, width), F32),
            like((rows, width), BF),
            like((HEADS, EXPERTS, 128), F32),
            like((1, width), F32),
        ),
        [VM] * 8,
        "middle_back",
        2 * rows * width * (1280 + 1024),
        6 * 1024 * 1024,
    )(spot, back, middle, second, router, gain, g_low, w_out)


def out_grad_kernel(packed, branch, out_ref):
    low = lanes_of(128) < 64
    heads = []
    for c in range(packed.shape[0]):
        tile = packed[c].astype(F32)
        tile = jnp.concatenate([tile, swap_halves(tile)], axis=0)
        heads.append(jnp.where(low, tile, 0.0).astype(BF))
    out_ref[...] = dot(jnp.concatenate(heads, axis=0), branch[...], TN)[0:64, :].astype(BF)


def out_grads(packed, branch):
    return call(
        out_grad_kernel,
        like((64, 1024), BF),
        [VM] * 2,
        "out_grads",
        1 << 20,
        1 << 18,
    )(packed, branch)


def queries_of(recv):
    return jnp.concatenate(
        [
            unpack_heads(recv[2 * t, 2 * RUN : 3 * RUN, :], recv[2 * t + 1, 2 * RUN : 3 * RUN, :])
            for t in range(HEADS // 2)
        ],
        axis=1,
    )


def keys_values_of(recv):
    low = lanes_of(2 * RUN) < 64
    both = [
        recv[2 * j, 0 : 2 * RUN, :].astype(F32) + recv[2 * j + 1, 0 : 2 * RUN, :].astype(F32)
        for j in range(KV_HEADS)
    ]
    keys, values = [], []
    for t in range(KV_HEADS // 2):
        keys.append(jnp.where(low, both[2 * t], swap_halves(both[2 * t + 1])))
        values.append(jnp.where(low, swap_halves(both[2 * t]), both[2 * t + 1]))
    return jnp.concatenate(keys, axis=1), jnp.concatenate(values, axis=1)


def means_kernel(recv, q_ref, k_ref, q_gain, k_gain, misc, out_ref):
    uq = queries_of(recv)
    uk, _ = keys_values_of(recv)
    q, k = q_ref[...], k_ref[...]
    rq, rk = inverse_rms(q), inverse_rms(k)
    mq = jnp.mean(uq * row_of(q_gain) * q, axis=1, keepdims=True) * rq
    mk = jnp.mean(uk * row_of(k_gain) * k, axis=1, keepdims=True) * rk
    lane = lanes_of(q.shape[0])
    columns = jnp.where(lane == 0, rq, jnp.where(lane == 1, mq, jnp.where(lane == 2, rk, mk)))
    rows = jnp.transpose(columns)[0:8, :]
    high = rows.astype(BF).astype(F32)
    rows = jnp.concatenate([high, rows - high], axis=0).astype(BF)
    for d in range(HEADS):
        out_ref[d, 0:16, :] = rows
        out_ref[d, 16:48, :] = misc[d].astype(BF)


def means(recv, q, k, q_gain, k_gain, misc):
    return call(
        means_kernel,
        like((HEADS, 48, 128), BF),
        [VM] * 6,
        "means",
        1 << 20,
        2 * 1024 * 1024,
    )(recv, q, k, q_gain, k_gain, misc)


def input_kernel(
    recv, q_ref, k_ref, x_ref, middle, q_gain, k_gain, gain, wq, wk, wv, ffn_part, out_ref, gains_ref
):
    uq = queries_of(recv)
    uk, dv = keys_values_of(recv)
    q, k = q_ref[...], k_ref[...]
    rq, rk = inverse_rms(q), inverse_rms(k)
    qh, kh = q * rq, k * rk
    q_part = jnp.sum(uq * qh, axis=0, keepdims=True)
    k_part = jnp.sum(uk * kh, axis=0, keepdims=True)
    uq, uk = uq * row_of(q_gain), uk * row_of(k_gain)
    gq = (rq * (uq - qh * jnp.mean(uq * qh, axis=1, keepdims=True))).astype(BF)
    gk = (rk * (uk - kh * jnp.mean(uk * kh, axis=1, keepdims=True))).astype(BF)
    upstream = dot(gq, wq[...], NT) + dot(gk, wk[...], NT) + dot(dv.astype(BF), wv[...], NT)
    x = x_ref[...].astype(F32)
    r = inverse_rms(x)
    hat = x * r
    x_part = jnp.sum(upstream * hat, axis=0, keepdims=True)
    scaled = upstream * row_of(gain)
    out_ref[...] = middle[...] + r * (scaled - hat * jnp.mean(scaled * hat, axis=1, keepdims=True))
    none = jnp.zeros((4, 128), F32)
    for s in range(8):
        cut = slice(128 * s, 128 * (s + 1))
        third = k_part[:, cut] if s < 4 else none[0:1, :]
        gains_ref[s] = jnp.concatenate(
            [x_part[:, cut], q_part[:, cut], third, ffn_part[:, cut], none], axis=0
        )


def input_back(recv, q, k, x, middle, q_gain, k_gain, gain, wq, wk, wv, ffn_part):
    rows, width = x.shape
    return call(
        input_kernel,
        (like((rows, width), F32), like((8, 8, 128), F32)),
        [VM] * 12,
        "input_back",
        2 * rows * width * 2048,
        8 * 1024 * 1024,
    )(recv, q, k, x, middle, q_gain, k_gain, gain, wq, wk, wv, ffn_part)


def head_grad_kernel(
    even, turned, own, kv_own, kv_other, normed, stats, gain_ref, gains, out_rows, out_ref
):
    n = own.shape[0]
    low = lanes_of(128) < 64
    gain = gain_ref[...]
    total = None
    for p in range(n // 2):
        grads = []
        for c in (2 * p, 2 * p + 1):
            packed = own[c, 2 * RUN : 3 * RUN, :].astype(F32)
            uq = jnp.concatenate([packed, swap_halves(packed)], axis=0)
            both = kv_own[c].astype(F32) + kv_other[c].astype(F32)
            keys = swap_halves(both)
            upstream = jnp.where(low, uq, keys)
            packed = normed[c, 2 * RUN : 3 * RUN, :].astype(F32)
            qn = jnp.concatenate([packed, swap_halves(packed)], axis=0) * HEAD_DIM**0.5
            hat = jnp.where(low, qn, swap_halves(normed[c, 0 : 2 * RUN, :])) / gain
            scalars = stats[c, 0:16, :].astype(F32)
            scalars = scalars[0:8, :] + scalars[8:16, :]
            cols = jnp.transpose(jnp.concatenate([scalars] * 16, axis=0))
            r = jnp.where(low, cols[:, 0:1], cols[:, 2:3])
            m = jnp.where(low, cols[:, 1:2], cols[:, 3:4])
            grad = r * (upstream * gain - hat * m)
            grads.append(jnp.where(low | (even[0] == 1), grad, both).astype(BF))
        left = jnp.concatenate([turned[2 * p], turned[2 * p + 1]], axis=1)
        step = dot(left, jnp.concatenate(grads, axis=0))
        total = step if total is None else total + step
    others = stats[0, 16:48, :].astype(F32)
    for c in range(1, n):
        others = others + stats[c, 16:48, :].astype(F32)
    for s in range(8):
        out_ref[s, 0:128, :] = total[128 * s : 128 * (s + 1), :].astype(BF)
        out_ref[s, 128:144, :] = jnp.concatenate(
            [others[8 * (s // 2) : 8 * (s // 2) + 8, :], gains[s]], axis=0
        ).astype(BF)
        out_ref[s, 144:PART, :] = out_rows[:, 128 * s : 128 * (s + 1)]


def head_grads(even, turned, own, kv_own, kv_other, normed, stats, gain, gains, out_rows):
    return call(
        head_grad_kernel,
        like((8, PART, 128), BF),
        [SM] + [VM] * 9,
        "head_grads",
        2 * 2048 * 1024 * 128,
        8 * 1024 * 1024,
    )(even, turned, own, kv_own, kv_other, normed, stats, gain, gains, out_rows)


def share_kernel(shares, out_ref):
    total = shares[0].astype(F32)
    for s in range(1, shares.shape[0]):
        total = total + shares[s].astype(F32)
    total = total.astype(BF)
    for c in range(out_ref.shape[0]):
        out_ref[c] = total


def share_out(shares, chips):
    return call(
        share_kernel,
        like((chips, PART, 128), BF),
        [VM],
        "share_out",
        1 << 18,
        4 * 1024 * 1024,
    )(shares)


def spread_kernel(place, block_ref, *refs):
    wq, wk, wv, x_gain, q_gain, k_gain, f_gain, wo, router = refs[-9:]
    n = block_ref.shape[1]
    low = lanes_of(128) < 64
    some = lanes_of(8) < 64
    total = None
    kept = None
    for c in range(0, n, 2):
        even, odd = block_ref[0, c, 0].astype(F32), block_ref[0, c + 1, 0].astype(F32)
        wide = slice(64 * c, 64 * c + 128)
        wq[0, 0, :, wide] = jnp.where(low, even[:128], swap_halves(odd[:128]))
        key, value = even[:128], odd[:128]
        if c % 4 == 0:
            kept = (swap_halves(key), swap_halves(value))
        else:
            half = slice(32 * c - 64, 32 * c + 64)
            wk[0, 0, :, half] = jnp.where(low, kept[0], key)
            wv[0, 0, :, half] = jnp.where(low, kept[1], value)
        router[:, wide] = jnp.where(some, even[128:136], swap_halves(odd[128:136]))
        sums = even[136:144] + odd[136:144]
        total = sums if total is None else total + sums
        for d, block in ((c, even), (c + 1, odd)):
            wo[64 * d : 64 * d + 64, :] = block[144:PART]
    x_gain[0, 0] = total[0:1]
    q_gain[0, 0] = total[1:2]
    k_gain[0, 0] = total[2:3]
    f_gain[0, 0] = total[3:4]


def spread(place, block, before=None):
    dp, n, y = block.shape[:3]
    steps = dp * y
    put = lambda rows, width: pl.BlockSpec((1, 1, rows, width), lambda i, at: (i, at[0], 0, 0))
    sizes = [(128, 1024), (128, 512), (128, 512)] + [(1, 128)] * 4
    given = () if before is None else tuple(before)
    return pl.pallas_call(
        spread_kernel,
        grid_spec=pltpu.PrefetchScalarGridSpec(
            num_scalar_prefetch=1,
            grid=(steps,),
            in_specs=[pl.BlockSpec((1, n, 1, PART, 128), lambda i, at: (i // y, 0, i % y, 0, 0))]
            + [pl.BlockSpec(memory_space=pl.ANY)] * len(given),
            out_specs=[put(*size) for size in sizes]
            + [
                pl.BlockSpec((1024, 128), lambda i, at: (0, 2 * i + at[0])),
                pl.BlockSpec((8, 1024), lambda i, at: (i, 0)),
            ],
        ),
        out_shape=[like((steps, 2) + size, F32) for size in sizes]
        + [like((1024, 256 * steps), F32), like((8 * steps, 1024), F32)],
        input_output_aliases={2 + i: i for i in range(len(given))},
        compiler_params=pltpu.CompilerParams(vmem_limit_bytes=56 * MIB),
        name="spread",
    )(place, block, *given)


def by_ctx(value):
    return lax.all_to_all(value, "ctx", split_axis=0, concat_axis=0, tiled=True)


def swap(value, axis, bit):
    n = lax.axis_size(axis)
    return lax.ppermute(value, axis, [(i, i ^ bit) for i in range(n)])


def held(value):
    return lax.optimization_barrier(value)


def across_chips(value):
    axes = ("dp", "ctx", "exp")
    dp, ctx, exp = (lax.axis_size(a) for a in axes)
    groups = [
        [(d * ctx + c) * exp + 2 * y + core for d in range(dp) for c in range(ctx) for y in range(exp // 2)]
        for core in range(2)
    ]
    return lax.all_to_all(
        value, axes, split_axis=0, concat_axis=0, tiled=True, axis_index_groups=groups
    )


def per_device(
    tokens,
    places,
    choices,
    cotangent,
    attn_gain,
    w_query,
    w_key,
    w_value,
    query_gain,
    key_gain,
    w_out,
    ffn_gain,
    w_router,
    w_gate,
    w_up,
    w_down,
):
    x_low = tokens[0]
    rows = x_low.shape[0]
    ctx = lax.axis_index("ctx")
    exp = lax.axis_index("exp")
    n_ctx = lax.axis_size("ctx")
    n_dp = lax.axis_size("dp")
    core = jnp.bitwise_and(exp, 1).astype(jnp.int32)
    picked = choices[0]
    g_low = cotangent[0]

    inv = places[0, ::RUN] // RUN
    runs = jnp.arange(inv.shape[0], dtype=jnp.int32)
    order = jnp.sum(jnp.where(inv[None, :] == runs[:, None], runs[None, :], 0), axis=1)
    cosine, sine = (jnp.asarray(t) for t in turn_tables(places.shape[1]))

    chosen = jnp.any(picked[:, :, None] == jnp.arange(EXPERTS, dtype=jnp.int32), axis=1)
    tri = jnp.asarray(np.tril(np.ones((rows, rows), np.float32), -1), BF)
    slot = dot(tri, chosen.astype(BF))
    slot = jnp.where(chosen, slot, -1.0).astype(BF)
    column = np.arange(EXPERTS * CAP)
    named = (np.arange(EXPERTS)[:, None] == (column // CAP)[None, :]).astype(np.float32)
    at = dot(slot, jnp.asarray(named, BF))
    spot = (at == jnp.asarray(column % CAP, F32)[None, :]).astype(BF)

    send, first_low, first_turned, q_proj, k_proj = pre(
        x_low, attn_gain, w_query, w_key, w_value, query_gain, key_gain, picked.T
    )
    g_all = lax.all_gather(g_low, "ctx")
    recv = by_ctx(send)
    kv_all, q_all, att_all, att_send = attend(order, inv, recv, cosine, sine)
    att_send, w_gate, w_up, w_down = held((att_send, w_gate, w_up, w_down))
    down_blocks = w_down.reshape(2, 128, 8, 128).transpose(0, 2, 1, 3).reshape(2, 1024, 128)
    mine = held(jnp.concatenate([w_gate, w_up, down_blocks], axis=1))
    over_y = swap(mine, "exp", 2)
    over_core = swap(mine, "exp", 1)
    heads = by_ctx(att_send)
    heads, mine = held((heads, mine))
    over_both = swap(over_y, "exp", 1)
    router = w_router.T
    attended, middle, second_low, rows_send = middle_forward(heads, x_low, w_out, ffn_gain, spot)
    rows_send, g_all, first_turned = held((rows_send, g_all, first_turned))
    turned_all = lax.all_gather(first_turned, "ctx")
    sent = by_ctx(rows_send.reshape(n_ctx, 2, CAP, -1))
    sent, over_core, over_both = held((sent, over_core, over_both))
    parts = (mine, over_core, over_y, over_both)
    number = jnp.reshape(2 * ctx, (1,)).astype(jnp.int32)
    back, out_rows, *kept, slots = experts(number, sent, recv, g_all, router, parts)
    back = by_ctx(back).reshape(EXPERTS * CAP, -1)
    add = lambda *parts: sum(p.astype(F32) for p in parts).astype(BF)
    keep, near, far = weight_grads(*kept)
    out_part = scatter_rows(slots, out_rows)
    back, near, keep, far, out_part, turned_all = held((back, near, keep, far, out_part, turned_all))
    far = swap(far, "exp", 1)
    att_grad_send, grad_middle, branch, misc_part, ffn_part = middle_back(
        spot, back, middle, second_low, router, ffn_gain, g_low, w_out
    )
    branch_all = lax.all_gather(branch, "ctx", axis=0, tiled=True)
    grad_recv = by_ctx(att_grad_send)
    near, keep = add(near[0], far[1]), add(keep[0], far[0])
    grad_recv, near, keep = held((grad_recv, near, keep))
    near = swap(near, "exp", 2)
    grad_send, kv_own = attend_back(order, inv, grad_recv, kv_all, q_all, att_all, cosine, sine)
    grads = by_ctx(grad_send)
    kv_other = swap(kv_own, "ctx", 1)
    keep = add(keep, near)
    grads, keep = held((grads, keep))
    over_dp = swap(keep, "dp", 1)
    stats = by_ctx(means(grads, q_proj, k_proj, query_gain, key_gain, misc_part))
    branch_all, out_part = held((branch_all, out_part))
    out_rows = out_grads(att_send, branch_all)
    out_part = lax.psum_scatter(out_part, "ctx", scatter_dimension=0, tiled=False)
    stats, out_rows = held((stats, out_rows))
    input_grad, gains = input_back(
        grads, q_proj, k_proj, x_low, grad_middle, query_gain, key_gain, attn_gain, w_query, w_key, w_value,
        ffn_part,
    )
    own_gain = jnp.concatenate(
        [
            lax.dynamic_slice_in_dim(query_gain, ctx * HEAD_DIM, HEAD_DIM),
            lax.dynamic_slice_in_dim(key_gain, ctx // 2 * HEAD_DIM, HEAD_DIM),
        ]
    ).astype(F32)[None]
    even = jnp.reshape(1 - jnp.bitwise_and(ctx, 1), (1,)).astype(jnp.int32)
    shares = head_grads(
        even, turned_all, grad_send, kv_own, kv_other, recv, stats, own_gain, gains, out_rows
    )
    shares = lax.all_to_all(shares, ("dp", "exp"), split_axis=0, concat_axis=0, tiled=True)
    shares, over_dp = held((shares, over_dp))
    chips = n_dp * n_ctx * 2
    whole = across_chips(share_out(shares, chips))
    expert_sum = keep.astype(F32) + over_dp.astype(F32)
    grad_gate_w = expert_sum[:, :1024]
    grad_up_w = expert_sum[:, 1024:2048]
    grad_down_w = (
        expert_sum[:, 2048:].reshape(2, 8, 128, 128).transpose(0, 2, 1, 3).reshape(2, 128, 1024)
    )
    whole, grad_gate_w, grad_up_w, grad_down_w = held(
        (whole, grad_gate_w, grad_up_w, grad_down_w)
    )
    other = swap(whole, "exp", 1)
    shape = (n_dp, n_ctx, 2, PART, 128)
    done = spread(jnp.reshape(core, (1,)), whole.reshape(shape))
    done = spread(jnp.reshape(1 - core, (1,)), other.reshape(shape), done)
    wq, wk, wv = (v.reshape(1024, -1) for v in done[:3])
    wo, router_grad = done[7], done[8].T
    outputs = (middle + out_part.astype(F32)).astype(BF)
    gain_sums = [v.reshape(1024) for v in done[3:7]]
    return (
        outputs[None],
        input_grad[None],
        gain_sums[0],
        wq,
        wk,
        wv,
        gain_sums[1],
        gain_sums[2][:512],
        wo,
        gain_sums[3],
        router_grad,
        grad_gate_w,
        grad_up_w,
        grad_down_w,
    )


def solution(mesh):
    seqs = ("dp", "exp")
    row_spec = P(seqs, "ctx", None)
    in_specs = (row_spec, P(seqs, None), row_spec, row_spec) + (P(),) * 9
    in_specs += (P("ctx", None, "exp"), P("ctx", None, "exp"), P("ctx", "exp", None))
    out_specs = (row_spec, row_spec) + (P(),) * 9
    out_specs += (P("ctx", None, "exp"), P("ctx", None, "exp"), P("ctx", "exp", None))
    return jax.shard_map(
        per_device, mesh=mesh, in_specs=in_specs, out_specs=out_specs, check_vma=False
    )
```

```python
import jax
import jax.numpy as jnp
import numpy as np
from jax import lax
from jax.experimental import pallas as pl
from jax.experimental.pallas import tpu as pltpu
from jax.sharding import PartitionSpec as P

HEADS = 16
KV_HEADS = 8
HEAD_DIM = 64
EXPERTS = 32
CAP = 40
EPSILON = 1e-06
MASKED = -1e30
BF = jnp.bfloat16
F32 = jnp.float32
RUN = 64
QB = 512
QB_BACK = 256
PART = 208
BASE = 256
MIB = 1024 * 1024
NT = ((1,), (1,))
TN = ((0,), (0,))
VM = pl.BlockSpec(memory_space=pltpu.VMEM)
SM = pl.BlockSpec(memory_space=pltpu.SMEM)


def dot(a, b, dims=((1,), (0,))):
    return lax.dot_general(a, b, (dims, ((), ())), preferred_element_type=F32)


def call(kernel, outs, ins, name, flops, moved, scratch=(), transcendentals=0, vmem=56):
    return pl.pallas_call(
        kernel,
        out_shape=outs,
        in_specs=ins,
        out_specs=jax.tree.map(lambda _: VM, outs),
        scratch_shapes=list(scratch),
        compiler_params=pltpu.CompilerParams(vmem_limit_bytes=vmem * MIB),
        cost_estimate=pl.CostEstimate(
            flops=flops, bytes_accessed=moved, transcendentals=transcendentals
        ),
        name=name,
    )


def like(shape, dtype):
    return jax.ShapeDtypeStruct(shape, dtype)


def inverse_rms(value):
    return lax.rsqrt(jnp.mean(value * value, axis=-1, keepdims=True) + EPSILON)


def row_of(ref):
    return ref[...].astype(F32).reshape(1, -1)


def lanes_of(rows):
    return lax.broadcasted_iota(jnp.int32, (rows, 128), 1)


def swap_halves(tile):
    return pltpu.roll(tile.astype(F32), 64, 1)


def pack_head(wide, head):
    tile = wide[:, 128 * (head // 2) : 128 * (head // 2 + 1)]
    low = lanes_of(RUN) < 64
    if head % 2 == 0:
        return jnp.where(low, tile[:RUN], swap_halves(tile[RUN:]))
    return jnp.where(low, swap_halves(tile[:RUN]), tile[RUN:])


def unpack_heads(even, odd):
    low = lanes_of(RUN) < 64
    even, odd = even.astype(F32), odd.astype(F32)
    return jnp.concatenate(
        [jnp.where(low, even, swap_halves(odd)), jnp.where(low, swap_halves(even), odd)], axis=0
    )


def turn_tables(seq):
    half = HEAD_DIM // 2
    frequency = (10000.0 ** (-np.arange(half) * 2.0 / HEAD_DIM)).astype(np.float32)
    angles = (np.arange(seq, dtype=np.float32)[:, None] * frequency[None, :]).astype(np.float64)
    cosine, sine = np.cos(angles), np.sin(angles)
    ones, zeros = np.ones((seq, 64)), np.zeros((seq, 64))
    return (
        np.concatenate([cosine, cosine, ones], axis=1).astype(np.float32),
        np.concatenate([-sine, sine, zeros], axis=1).astype(np.float32),
    )


def turn(tile, cosine, sine):
    other = jnp.where(lanes_of(tile.shape[0]) < 32, pltpu.roll(tile, 96, 1), pltpu.roll(tile, 32, 1))
    return tile * cosine + other * sine


def pre_kernel(x_ref, gain, wq, wk, wv, q_gain, k_gain, picks, send, first_out, turned_out, q_out, k_out):
    x = x_ref[...].astype(F32)
    wide = x * inverse_rms(x) * row_of(gain)
    first = wide.astype(BF)
    first_out[...] = first
    q = dot(first, wq[...])
    k = dot(first, wk[...])
    v = dot(first, wv[...])
    q_out[...] = q
    k_out[...] = k
    qn = q * inverse_rms(q) * (row_of(q_gain) * HEAD_DIM ** (-0.5))
    kn = k * inverse_rms(k) * row_of(k_gain)
    low = lanes_of(x.shape[0]) < 64
    for h in range(KV_HEADS):
        cut = slice(128 * (h // 2), 128 * (h // 2 + 1))
        kt, vt = kn[:, cut], v[:, cut]
        if h % 2 == 0:
            both = jnp.where(low, kt, swap_halves(vt))
        else:
            both = jnp.where(low, swap_halves(kt), vt)
        both = both.astype(BF)
        send[2 * h, 0 : 2 * RUN, :] = both
        send[2 * h + 1, 0 : 2 * RUN, :] = both
    lane = lanes_of(x.shape[0])
    rows = jnp.transpose(jnp.where(lane == 0, inverse_rms(q), inverse_rms(k)))[0:2, :]
    high = rows.astype(BF).astype(F32)
    named = jnp.concatenate(
        [picks[...].astype(F32), high, rows - high, jnp.zeros((4, 128), F32)], axis=0
    ).astype(BF)
    for d in range(HEADS):
        send[d, 2 * RUN : 3 * RUN, :] = pack_head(qn, d).astype(BF)
        send[d, 3 * RUN : 3 * RUN + 16, :] = named
    turned_out[...] = jnp.transpose(first.astype(F32)).astype(BF)


def pre(x, gain, wq, wk, wv, q_gain, k_gain, picks):
    rows, width = x.shape
    return call(
        pre_kernel,
        (
            like((HEADS, 3 * RUN + 16, 128), BF),
            like((rows, width), BF),
            like((width, rows), BF),
            like((rows, wq.shape[1]), F32),
            like((rows, wk.shape[1]), F32),
        ),
        [VM] * 8,
        "pre",
        2 * rows * width * 2048,
        6 * 1024 * 1024,
    )(x, gain, wq, wk, wv, q_gain, k_gain, picks)


def turn_over(source, target):
    for i in range(source.shape[0] // 128):
        cut = slice(128 * i, 128 * (i + 1))
        target[:, cut] = jnp.transpose(source[cut, :].astype(F32)).astype(BF)


def masked_scores(kv, q, block):
    scores = dot(kv, q, NT)
    end = scores.shape[0]
    row = lax.broadcasted_iota(jnp.int32, (block, block), 0)
    col = lax.broadcasted_iota(jnp.int32, (block, block), 1)
    last = jnp.where(row <= col, scores[end - block :, :], MASKED)
    return last if end == block else jnp.concatenate([scores[: end - block, :], last], axis=0)


def attend_kernel(order, inv, recv, cosine, sine, kv_out, q_out, att_out, lse_out, send_out, turned):
    seq = kv_out.shape[0]
    lane = lanes_of(RUN)

    def gather(b, carry):
        s = order[b]
        c = lax.shift_right_logical(s, 1)
        half = jnp.bitwise_and(s, 1)
        rows = pl.ds(pl.multiple_of(b * RUN, RUN), RUN)
        cos, sin = cosine[rows, :], sine[rows, :]
        kv = recv[c, pl.ds(pl.multiple_of(half * RUN, RUN), RUN), :].astype(F32)
        kv_out[rows, :] = turn(kv, cos, sin).astype(BF)
        tile = recv[c, pl.ds(2 * RUN, RUN), :].astype(F32)
        q = jnp.where(lane < 64, jnp.where(half == 0, tile, swap_halves(tile)), 0.0)
        q_out[rows, :] = turn(q, cos, sin).astype(BF)
        return carry

    lax.fori_loop(0, seq // RUN, gather, 0, unroll=32)
    turn_over(kv_out, turned)
    for i in range(seq // QB):
        here = slice(i * QB, (i + 1) * QB)
        end = (i + 1) * QB
        scores = masked_scores(kv_out[:end, :], q_out[here, :], QB)
        top = jnp.max(scores, axis=0, keepdims=True)
        weights = jnp.exp(scores - top)
        total = jnp.sum(weights, axis=0, keepdims=True)
        att_out[here, :] = jnp.transpose(dot(turned[:, :end], weights.astype(BF)) / total)
        lse_out[:, here] = jnp.broadcast_to(top + jnp.log(total), (8, QB))

    def place(c, carry):
        b0, b1 = inv[2 * c], inv[2 * c + 1]
        first = att_out[pl.ds(pl.multiple_of(b0 * RUN, RUN), RUN), :]
        second = att_out[pl.ds(pl.multiple_of(b1 * RUN, RUN), RUN), :]
        send_out[c] = jnp.where(lane < 64, swap_halves(first), second).astype(BF)
        return carry

    lax.fori_loop(0, send_out.shape[0], place, 0, unroll=16)


def attend(order, inv, recv, cosine, sine):
    n = recv.shape[0]
    seq = n * 128
    return call(
        attend_kernel,
        (
            like((seq, 128), BF),
            like((seq, 128), BF),
            like((seq, 128), F32),
            like((8, seq), F32),
            like((n, RUN, 128), BF),
        ),
        [SM, SM, VM, VM, VM],
        "attend",
        4 * seq * seq * 128 // 2,
        14 * seq * 128,
        [pltpu.VMEM((128, seq), BF)],
        transcendentals=seq * seq // 2,
    )(order, inv, recv, cosine, sine)


def attend_back_kernel(
    order, inv, even, recv, kv_in, q_in, att_in, lse_in, cosine, sine,
    send_out, kv_grad_out, g_all, dq_all, dkv_all, sums, turned,
):
    seq = kv_in.shape[0]
    lane = lanes_of(RUN)

    def gather(b, carry):
        s = order[b]
        c = lax.shift_right_logical(s, 1)
        half = jnp.bitwise_and(s, 1)
        tile = recv[c, 0:RUN, :].astype(F32)
        g_all[pl.ds(pl.multiple_of(b * RUN, RUN), RUN), :] = jnp.where(
            lane >= 64, jnp.where(half == 1, tile, swap_halves(tile)), 0.0
        ).astype(BF)
        return carry

    lax.fori_loop(0, seq // RUN, gather, 0, unroll=32)
    turn_over(kv_in, turned)
    steps = seq // QB_BACK
    for i in reversed(range(steps)):
        here = slice(i * QB_BACK, (i + 1) * QB_BACK)
        end = (i + 1) * QB_BACK
        kv, q, g = kv_in[:end, :], q_in[here, :], g_all[here, :]
        offset = jnp.sum(jnp.transpose(att_in[here, :] * g.astype(F32)), axis=0, keepdims=True)
        weights = jnp.exp(masked_scores(kv, q, QB_BACK) - lse_in[0:1, here])
        grad_scores = (weights * (dot(kv, g, NT) - offset)).astype(BF)
        dq_all[here, :] = jnp.transpose(dot(turned[:, :end], grad_scores))
        step = dot(grad_scores, q) + dot(weights.astype(BF), g)
        if i == steps - 1:
            dkv_all[...] = step
        else:
            dkv_all[:end, :] += step

    def place(c, carry):
        b0, b1 = inv[2 * c], inv[2 * c + 1]
        r0 = pl.ds(pl.multiple_of(b0 * RUN, RUN), RUN)
        r1 = pl.ds(pl.multiple_of(b1 * RUN, RUN), RUN)
        kv0 = turn(dkv_all[r0, :], cosine[r0, :], -sine[r0, :]).astype(BF)
        kv1 = turn(dkv_all[r1, :], cosine[r1, :], -sine[r1, :]).astype(BF)
        send_out[c, BASE : BASE + RUN, :] = kv0
        send_out[c, BASE + RUN : BASE + 2 * RUN, :] = kv1
        kv0, kv1 = kv0.astype(F32), kv1.astype(F32)
        values = jnp.where(lane < 64, swap_halves(kv0), kv1)
        keys = jnp.where(lane < 64, kv0, swap_halves(kv1))
        kv_grad_out[c] = jnp.where(even[0] == 1, values, keys).astype(BF)
        both_q = jnp.concatenate([dq_all[r0, :], dq_all[r1, :]], axis=0)
        both_q = both_q * jnp.concatenate([q_in[r0, :], q_in[r1, :]], axis=0).astype(F32)
        both_k = jnp.concatenate([dkv_all[r0, :], dkv_all[r1, :]], axis=0)
        both_k = both_k * jnp.concatenate([kv_in[r0, :], kv_in[r1, :]], axis=0).astype(F32)
        some = jnp.where(lanes_of(8) < 64, 1.0, 0.0).astype(BF)
        sums[pl.ds(c, 1), :] = dot(some, both_q.astype(BF), NT)[0:1, :]
        sums[pl.ds(n + c, 1), :] = dot(some, both_k.astype(BF), NT)[0:1, :]
        q0 = turn(dq_all[r0, :], cosine[r0, :], -sine[r0, :])
        q1 = turn(dq_all[r1, :], cosine[r1, :], -sine[r1, :])
        both = jnp.where(lane < 64, q0, swap_halves(q1))
        send_out[c, BASE + 2 * RUN : BASE + 3 * RUN, :] = (both * HEAD_DIM ** (-0.5)).astype(BF)
        return carry

    n = send_out.shape[0]
    lax.fori_loop(0, n, place, 0, unroll=16)
    for c in range(n):
        send_out[c, BASE + 3 * RUN : BASE + 3 * RUN + 2 * n, :] = sums[...].astype(BF)


def attend_back(order, inv, even, recv, kv, q, att, lse, cosine, sine):
    n = recv.shape[0]
    seq = n * 128
    return call(
        attend_back_kernel,
        (like((n, BASE + 3 * RUN + 2 * n, 128), BF), like((n, RUN, 128), BF)),
        [SM, SM, SM] + [VM] * 7,
        "attend_back",
        10 * seq * seq * 128 // 2,
        20 * seq * 128,
        [
            pltpu.VMEM((seq, 128), BF),
            pltpu.VMEM((seq, 128), F32),
            pltpu.VMEM((seq, 128), F32),
            pltpu.VMEM((2 * n, 128), F32),
            pltpu.VMEM((128, seq), BF),
        ],
        seq * seq // 2,
    )(order, inv, even, recv, kv, q, att, lse, cosine, sine)


def join_kernel(send, mine, far, out_ref):
    for c in range(out_ref.shape[0]):
        for j in range(4):
            rows = slice(8 * c, 8 * c + 8)
            both = mine[j, rows, :].astype(F32) + far[j, rows, :].astype(F32)
            for m in range(0, 8, 2):
                at = 64 * j + 8 * m
                pair = (both[:, 128 * m : 128 * m + 128], both[:, 128 * m + 128 : 128 * m + 256])
                out_ref[c, at : at + 16, :] = jnp.concatenate(pair, axis=0).astype(BF)


def join(send, mine, far):
    whole = pl.BlockSpec(mine.shape, lambda i: (0, 0, 0))
    return pl.pallas_call(
        join_kernel,
        grid=(1,),
        out_shape=like(send.shape, BF),
        in_specs=[pl.BlockSpec(memory_space=pl.ANY), whole, whole],
        out_specs=pl.BlockSpec((send.shape[0], BASE, 128), lambda i: (0, 0, 0)),
        input_output_aliases={0: 0},
        compiler_params=pltpu.CompilerParams(vmem_limit_bytes=56 * MIB),
        cost_estimate=pl.CostEstimate(flops=1 << 20, bytes_accessed=1 << 20, transcendentals=0),
        name="join",
    )(send, mine, far)


def slot_masks(slot, pair):
    line = lax.broadcasted_iota(jnp.int32, (2 * CAP, 128), 0).astype(F32)
    left = (line < CAP) & (line == slot[2 * pair : 2 * pair + 1, :])
    right = (line >= CAP) & (line - CAP == slot[2 * pair + 1 : 2 * pair + 2, :])
    return jnp.where(left, 1.0, 0.0).astype(BF), jnp.where(right, 1.0, 0.0).astype(BF)


def expert_kernel(number, rows_ref, picks_ref, g_ref, router_ref, *refs):
    parts, (back_ref, out_ref, kept_ref, hid_ref, ga_ref, gu_ref, gr_ref, slot_ref, gs_ref) = (
        refs[:4],
        refs[4:],
    )
    local = pl.program_id(0)
    e = number[0] + local
    n_ctx = g_ref.shape[0]
    picks = picks_ref[...].astype(F32)[:, :8, :]
    named = jnp.max(jnp.where(picks == e.astype(F32), 1.0, 0.0), axis=1)
    before = lax.broadcasted_iota(jnp.int32, (128, 128), 0) < lax.broadcasted_iota(
        jnp.int32, (128, 128), 1
    )
    slot = dot(named.astype(BF), jnp.where(before, 1.0, 0.0).astype(BF))
    slot = jnp.where(named > 0.0, slot, -1.0)
    slot_ref[0] = slot
    for p in range(n_ctx // 2):
        left, right = slot_masks(slot, p)
        gs_ref[2 * CAP * p : 2 * CAP * (p + 1), :] = (
            dot(left, g_ref[2 * p]) + dot(right, g_ref[2 * p + 1])
        ).astype(BF)
    rows = jnp.concatenate([rows_ref[c, 0].astype(F32) for c in range(n_ctx)], axis=0).astype(BF)
    kept_ref[0] = rows
    grads = gs_ref[...].astype(F32)
    logits = dot(rows, router_ref[...], NT)
    lane = lax.broadcasted_iota(jnp.int32, logits.shape, 1)
    powers = jnp.exp(logits - jnp.max(logits, axis=1, keepdims=True))
    gate = jnp.sum(jnp.where(lane == e, powers, 0.0), axis=1, keepdims=True) / jnp.sum(
        powers, axis=1, keepdims=True
    )
    w_gate = jnp.concatenate([w[0, 0:1024, :] for w in parts], axis=1)
    w_up = jnp.concatenate([w[0, 1024:2048, :] for w in parts], axis=1)
    w_down = jnp.concatenate(
        [
            jnp.concatenate([w[0, 2048 + 128 * n : 2176 + 128 * n, :] for n in range(8)], axis=1)
            for w in parts
        ],
        axis=0,
    )
    gate_act = dot(rows, w_gate)
    up_act = dot(rows, w_up)
    sig = 1.0 / (1.0 + jnp.exp(-gate_act))
    silu = gate_act * sig
    hidden = (silu * up_act).astype(BF)
    hid_ref[0] = hidden
    expert_out = dot(hidden, w_down)
    out_rows = gate * expert_out
    for c in range(n_ctx):
        out_ref[c, 0] = out_rows[CAP * c : CAP * (c + 1), :].astype(BF)
    grad_gate = jnp.sum(grads * expert_out, axis=1, keepdims=True)
    grad_rows = (gate * grads).astype(BF)
    gr_ref[0] = grad_rows
    grad_hidden = dot(grad_rows, w_down, NT)
    ga = (grad_hidden * up_act * sig * (1.0 + gate_act * (1.0 - sig))).astype(BF)
    gu = (grad_hidden * silu).astype(BF)
    ga_ref[0] = ga
    gu_ref[0] = gu
    back = dot(ga, w_gate, NT) + dot(gu, w_up, NT)
    high = grad_gate.astype(BF).astype(F32)
    lane = lanes_of(rows.shape[0])
    tail = jnp.where(lane == e, high, jnp.where(lane == e + EXPERTS, grad_gate - high, 0.0))
    for c in range(n_ctx):
        cut = slice(CAP * c, CAP * (c + 1))
        back_ref[c, 0, :, 0:1024] = back[cut, :].astype(BF)
        back_ref[c, 0, :, 1024:1152] = tail[cut, :].astype(BF)


def experts(number, rows, recv, g_all, router, parts):
    n_ctx = rows.shape[0]
    n = n_ctx * CAP
    own = lambda w: pl.BlockSpec((1,) + w.shape[1:], lambda i: (i, 0, 0))
    each = lambda width: pl.BlockSpec((1, n, width), lambda i: (i, 0, 0))
    both = lambda width: pl.BlockSpec((n_ctx, 1, CAP, width), lambda i: (0, i, 0, 0))
    return pl.pallas_call(
        expert_kernel,
        grid=(2,),
        out_shape=(
            like((n_ctx, 2, CAP, 1152), BF),
            like((n_ctx, 2, CAP, 1024), BF),
            like((2, n, 1024), BF),
            like((2, n, 512), BF),
            like((2, n, 512), BF),
            like((2, n, 512), BF),
            like((2, n, 1024), BF),
            like((2, n_ctx, 128), F32),
        ),
        in_specs=[SM, both(1024), pl.BlockSpec((n_ctx, 16, 128), lambda i: (0, 3 * RUN // 16, 0)), VM, VM]
        + [own(w) for w in parts],
        out_specs=(
            both(1152),
            both(1024),
            each(1024),
            each(512),
            each(512),
            each(512),
            each(1024),
            pl.BlockSpec((1, n_ctx, 128), lambda i: (i, 0, 0)),
        ),
        scratch_shapes=[pltpu.VMEM((n, 1024), BF)],
        compiler_params=pltpu.CompilerParams(vmem_limit_bytes=56 * MIB),
        cost_estimate=pl.CostEstimate(
            flops=24 * n * 1024 * 512, bytes_accessed=32 * 1024 * 1024, transcendentals=2 * n * 512
        ),
        name="experts",
    )(number, rows, recv, g_all, router, *parts)


def weight_grad_kernel(rows_ref, hid_ref, ga_ref, gu_ref, gr_ref, keep, near, far):
    rows = rows_ref[0]
    gate = dot(rows, ga_ref[0], TN)
    up = dot(rows, gu_ref[0], TN)
    down = dot(hid_ref[0], gr_ref[0], TN)
    for j, (ref, at) in enumerate([(keep, 0), (far, 0), (near, 0), (far, 1)]):
        cut = slice(128 * j, 128 * (j + 1))
        ref[at, 0, 0:1024, :] = gate[:, cut].astype(BF)
        ref[at, 0, 1024:2048, :] = up[:, cut].astype(BF)
        for n in range(8):
            ref[at, 0, 2048 + 128 * n : 2176 + 128 * n, :] = down[
                cut, 128 * n : 128 * (n + 1)
            ].astype(BF)


def weight_grads(rows, hid, ga, gu, gr):
    n = rows.shape[1]
    each = lambda v: pl.BlockSpec((1,) + v.shape[1:], lambda i: (i, 0, 0))
    put = lambda k: pl.BlockSpec((k, 1, 3072, 128), lambda i: (0, i, 0, 0))
    return pl.pallas_call(
        weight_grad_kernel,
        grid=(2,),
        out_shape=(
            like((1, 2, 3072, 128), BF),
            like((1, 2, 3072, 128), BF),
            like((2, 2, 3072, 128), BF),
        ),
        in_specs=[each(v) for v in (rows, hid, ga, gu, gr)],
        out_specs=(put(1), put(1), put(2)),
        compiler_params=pltpu.CompilerParams(vmem_limit_bytes=56 * MIB),
        cost_estimate=pl.CostEstimate(
            flops=12 * n * 1024 * 512, bytes_accessed=16 * 1024 * 1024, transcendentals=0
        ),
        name="weight_grads",
    )(rows, hid, ga, gu, gr)


def scatter_kernel(slot_ref, rows_ref, out_ref):
    line = lax.broadcasted_iota(jnp.int32, (CAP, 128), 0).astype(F32)
    for c in range(out_ref.shape[0]):
        total = None
        for a in range(2):
            mask = jnp.where(line == slot_ref[a, c : c + 1, :], 1.0, 0.0).astype(BF)
            part = dot(mask, rows_ref[c, a], TN)
            total = part if total is None else total + part
        out_ref[c] = total.astype(BF)


def scatter_rows(slot, rows):
    n = rows.shape[0]
    return call(
        scatter_kernel,
        like((n, 128, 1024), BF),
        [VM] * 2,
        "scatter_rows",
        1 << 33,
        16 * 1024 * 1024,
    )(slot, rows)


def middle_kernel(heads, x_ref, w_out, gain, spot, attended_out, middle_out, second_out, send_out):
    attended = jnp.concatenate(
        [unpack_heads(heads[2 * t], heads[2 * t + 1]) for t in range(HEADS // 2)], axis=1
    ).astype(BF)
    attended_out[...] = attended
    middle = x_ref[...].astype(F32) + dot(attended, w_out[...])
    middle_out[...] = middle
    second = (middle * inverse_rms(middle) * row_of(gain)).astype(BF)
    second_out[...] = second
    send_out[...] = dot(spot[...], second, TN).astype(BF)


def middle_forward(heads, x, w_out, gain, spot):
    rows, width = x.shape
    return call(
        middle_kernel,
        (
            like((rows, width), BF),
            like((rows, width), F32),
            like((rows, width), BF),
            like((spot.shape[1], width), BF),
        ),
        [VM] * 5,
        "middle",
        2 * rows * width * (1024 + 1280),
        6 * 1024 * 1024,
    )(heads, x, w_out, gain, spot)


def middle_back_kernel(
    spot, back, middle_ref, second, router, gain, g_ref, w_out,
    send, grad_out, branch_out,
):
    summed = dot(spot[...], back[...])
    logits = dot(second[...], router[...], NT)
    powers = jnp.exp(logits - jnp.max(logits, axis=1, keepdims=True))
    probs = powers / jnp.sum(powers, axis=1, keepdims=True)
    last = summed[:, 1024:1152]
    grad_sel = (last + pltpu.roll(last, 128 - EXPERTS, 1))[:, :EXPERTS]
    grad_logits = probs * (grad_sel - jnp.sum(probs * grad_sel, axis=1, keepdims=True))
    high = grad_logits.astype(BF)
    rest = (grad_logits - high.astype(F32)).astype(BF)
    upstream = summed[:, :1024] + dot(high, router[...]) + dot(rest, router[...])
    middle = middle_ref[...]
    r = inverse_rms(middle)
    hat = middle * r
    gain_part = jnp.sum(upstream * hat, axis=0, keepdims=True)
    router_part = dot(high, second[...], TN) + dot(rest, second[...], TN)
    low = lanes_of(EXPERTS) < 64
    first_row = lax.broadcasted_iota(jnp.int32, (EXPERTS, 128), 0) == 0
    for d in range(HEADS):
        cut = slice(128 * (d // 2), 128 * (d // 2 + 1))
        tile = router_part[:, cut]
        part = jnp.where(first_row, jnp.broadcast_to(gain_part[:, cut], (EXPERTS, 128)), 0.0)
        if d % 2 == 0:
            misc = jnp.where(low, tile, swap_halves(part))
        else:
            misc = jnp.where(low, swap_halves(tile), part)
        send[d, RUN : RUN + EXPERTS, :] = misc.astype(BF)
    scaled = upstream * row_of(gain)
    grad = (
        r * (scaled - hat * jnp.mean(scaled * hat, axis=1, keepdims=True)) + g_ref[...].astype(F32)
    )
    grad_out[...] = grad
    branch = grad.astype(BF)
    branch_out[...] = branch
    att = dot(branch, w_out[...], NT)
    for d in range(HEADS):
        send[d, 0:RUN, :] = pack_head(att, d).astype(BF)


def middle_back(spot, back, middle, second, router, gain, g_low, w_out):
    rows, width = middle.shape
    return call(
        middle_back_kernel,
        (
            like((HEADS, RUN + EXPERTS, 128), BF),
            like((rows, width), F32),
            like((rows, width), BF),
        ),
        [VM] * 8,
        "middle_back",
        2 * rows * width * (1280 + 1024),
        6 * 1024 * 1024,
    )(spot, back, middle, second, router, gain, g_low, w_out)


def out_grad_kernel(place, attended, branch, mine, far):
    for j in range(8):
        c, y, d = j // 4, j // 2 % 2, j % 2
        block = (
            jnp.bitwise_xor(place[0], d) * 4 + jnp.bitwise_xor(place[1], y) * 2 + jnp.bitwise_xor(place[2], c)
        )
        part = attended[:, pl.ds(pl.multiple_of(block * 128, 128), 128)]
        (far if c else mine)[j % 4] = dot(part, branch[...], TN).astype(BF)


def out_grads(place, attended, branch):
    return call(
        out_grad_kernel,
        (like((4, 128, 1024), BF), like((4, 128, 1024), BF)),
        [SM, VM, VM],
        "out_grads",
        1 << 20,
        1 << 18,
    )(place, attended, branch)


def queries_of(recv):
    return jnp.concatenate(
        [
            unpack_heads(
                recv[2 * t, BASE + 2 * RUN : BASE + 3 * RUN, :],
                recv[2 * t + 1, BASE + 2 * RUN : BASE + 3 * RUN, :],
            )
            for t in range(HEADS // 2)
        ],
        axis=1,
    )


def keys_values_of(recv):
    low = lanes_of(2 * RUN) < 64
    both = [
        recv[2 * j, BASE : BASE + 2 * RUN, :].astype(F32)
        + recv[2 * j + 1, BASE : BASE + 2 * RUN, :].astype(F32)
        for j in range(KV_HEADS)
    ]
    keys, values = [], []
    for t in range(KV_HEADS // 2):
        keys.append(jnp.where(low, both[2 * t], swap_halves(both[2 * t + 1])))
        values.append(jnp.where(low, swap_halves(both[2 * t]), both[2 * t + 1]))
    return jnp.concatenate(keys, axis=1), jnp.concatenate(values, axis=1)


def input_kernel(
    recv, q_ref, k_ref, x_ref, middle, q_gain, k_gain, gain, wq, wk, wv, out_ref, gain_ref
):
    uq = queries_of(recv)
    uk, dv = keys_values_of(recv)
    q, k = q_ref[...], k_ref[...]
    rq, rk = inverse_rms(q), inverse_rms(k)
    qh, kh = q * rq, k * rk
    uq, uk = uq * row_of(q_gain), uk * row_of(k_gain)
    gq = (rq * (uq - qh * jnp.mean(uq * qh, axis=1, keepdims=True))).astype(BF)
    gk = (rk * (uk - kh * jnp.mean(uk * kh, axis=1, keepdims=True))).astype(BF)
    upstream = dot(gq, wq[...], NT) + dot(gk, wk[...], NT) + dot(dv.astype(BF), wv[...], NT)
    x = x_ref[...].astype(F32)
    r = inverse_rms(x)
    hat = x * r
    x_part = jnp.sum(upstream * hat, axis=0, keepdims=True)
    scaled = upstream * row_of(gain)
    out_ref[...] = middle[...] + r * (scaled - hat * jnp.mean(scaled * hat, axis=1, keepdims=True))
    half = jnp.zeros((1, 64), F32)
    rows = [jnp.concatenate([half, x_part[:, 64 * i : 64 * (i + 1)]], axis=1) for i in range(8)]
    none = jnp.zeros((2, 128), F32)
    more = [x_part[:, 512 + 128 * i : 640 + 128 * i] for i in range(4)]
    gain_ref[...] = jnp.concatenate(rows + [none] + more + [none], axis=0)


def input_back(recv, q, k, x, middle, q_gain, k_gain, gain, wq, wk, wv):
    rows, width = x.shape
    return call(
        input_kernel,
        (like((rows, width), F32), like((16, 128), F32)),
        [VM] * 11,
        "input_back",
        2 * rows * width * 2048,
        8 * 1024 * 1024,
    )(recv, q, k, x, middle, q_gain, k_gain, gain, wq, wk, wv)


def head_grad_kernel(
    place, turned, own, kv_other, normed, grads, branch, gain_ref, out_ref
):
    n = own.shape[0]
    low = lanes_of(128) < 64
    gain = gain_ref[...]
    sums = grads[0, BASE + 3 * RUN : BASE + 3 * RUN + 2 * n, :].astype(F32)
    others = branch[0, RUN : RUN + EXPERTS, :].astype(F32)
    for c in range(1, n):
        sums = sums + grads[c, BASE + 3 * RUN : BASE + 3 * RUN + 2 * n, :].astype(F32)
        others = others + branch[c, RUN : RUN + EXPERTS, :].astype(F32)
    out_rows = grads[0, 0:BASE, :].astype(F32)
    for c in range(1, n):
        out_rows = out_rows + grads[c, 0:BASE, :].astype(F32)
    q_means = sums[0:n, :] / (HEADS * HEAD_DIM)
    k_means = sums[n : 2 * n, :] / (KV_HEADS * HEAD_DIM)
    total = None
    gains = None
    for p in range(n // 2):
        parts = []
        for c in (2 * p, 2 * p + 1):
            packed = own[c, BASE + 2 * RUN : BASE + 3 * RUN, :].astype(F32)
            uq = jnp.concatenate([packed, swap_halves(packed)], axis=0)
            both = own[c, BASE : BASE + 2 * RUN, :].astype(F32)
            other = kv_other[c].astype(F32)
            other = jnp.concatenate([swap_halves(other), other], axis=0)
            keys = swap_halves(both) + other
            upstream = jnp.where(low, uq, keys)
            packed = normed[c, 2 * RUN : 3 * RUN, :].astype(F32)
            qn = jnp.concatenate([packed, swap_halves(packed)], axis=0) * HEAD_DIM**0.5
            hat = jnp.where(low, qn, swap_halves(normed[c, 0 : 2 * RUN, :])) / gain
            factors = normed[c, 3 * RUN : 3 * RUN + 16, :].astype(F32)
            factors = factors[8:10, :] + factors[10:12, :]
            rows = jnp.concatenate(
                [factors, q_means[c : c + 1, :], k_means[c : c + 1, :], jnp.zeros((4, 128), F32)], axis=0
            )
            cols = jnp.transpose(jnp.concatenate([rows] * 16, axis=0))
            r = jnp.where(low, cols[:, 0:1], cols[:, 1:2])
            m = jnp.where(low, cols[:, 2:3], cols[:, 3:4])
            grad = r * (upstream * gain - hat * m)
            part = jnp.sum(upstream * hat, axis=0, keepdims=True)
            gains = part if gains is None else gains + part
            parts.append(jnp.where(low | (place[3] == 1), grad, both + other).astype(BF))
        left = jnp.concatenate([turned[2 * p], turned[2 * p + 1]], axis=1)
        step = dot(left, jnp.concatenate(parts, axis=0))
        total = step if total is None else total + step
    low_row = low[0:1, :]
    gains = jnp.where(low_row | (place[3] == 1), gains, 0.0)
    ffn = jnp.where(low_row, swap_halves(others[0:8, :])[0:1, :], 0.0)
    rows = jnp.concatenate([gains, ffn, jnp.zeros((6, 128), F32)], axis=0)
    some = lanes_of(8) < 64
    for s in range(8):
        out_ref[s, 0:128, :] = total[128 * s : 128 * (s + 1), :].astype(BF)
        kept = jnp.where(some, others[8 * (s // 2) : 8 * (s // 2) + 8, :], 0.0)
        out_ref[s, 128:144, :] = jnp.concatenate(
            [kept, rows if s == 0 else jnp.zeros((8, 128), F32)], axis=0
        ).astype(BF)
        out_ref[s, 144:PART, :] = jnp.zeros((64, 128), BF)
    for j in range(4):
        at = jnp.bitwise_xor(place[0], j % 2) * 4 + jnp.bitwise_xor(place[1], j // 2) * 2 + place[2]
        out_ref[pl.ds(at, 1), 144:PART, :] = out_rows[64 * j : 64 * j + 64, :].astype(BF)[None]


def head_grads(place, turned, own, kv_other, normed, grads, branch, gain):
    return call(
        head_grad_kernel,
        like((8, PART, 128), BF),
        [SM] + [VM] * 7,
        "head_grads",
        2 * 2048 * 1024 * 128,
        8 * 1024 * 1024,
    )(place, turned, own, kv_other, normed, grads, branch, gain)


def share_kernel(shares, gain_ref, out_ref):
    total = shares[0].astype(F32)
    for s in range(1, shares.shape[0]):
        total = total + shares[s].astype(F32)
    total = jnp.concatenate([total[0:128], total[128:144] + gain_ref[...], total[144:PART]], axis=0)
    total = total.astype(BF)
    for c in range(out_ref.shape[0]):
        out_ref[c] = total


def share_out(shares, gain, chips):
    return call(
        share_kernel,
        like((chips, PART, 128), BF),
        [VM, VM],
        "share_out",
        1 << 18,
        4 * 1024 * 1024,
    )(shares, gain)


def spread_kernel(place, block_ref, *refs):
    wq, wk, wv, wo, small, router = refs[-6:]
    n = block_ref.shape[1]
    low = lanes_of(128) < 64
    some = lanes_of(8) < 64
    total = None
    kept = None
    for c in range(0, n, 2):
        even, odd = block_ref[0, c, 0].astype(F32), block_ref[0, c + 1, 0].astype(F32)
        wide = slice(64 * c, 64 * c + 128)
        wq[0, 0, :, wide] = jnp.where(low, even[:128], swap_halves(odd[:128]))
        key, value = even[:128], odd[:128]
        if c % 4 == 0:
            kept = (swap_halves(key), swap_halves(value))
        else:
            half = slice(32 * c - 64, 32 * c + 64)
            wk[0, 0, :, half] = jnp.where(low, kept[0], key)
            wv[0, 0, :, half] = jnp.where(low, kept[1], value)
        router[:, wide] = jnp.where(some, even[128:136], swap_halves(odd[128:136]))
        sums = even[128:144] + odd[128:144]
        total = sums if total is None else total + sums
        pairs = jnp.where(some, even[136:144], swap_halves(odd[136:144]))
        small[0, 0, 0:1, wide] = pairs[0:1]
        small[0, 0, 1:2, wide] = pairs[1:2]
        if c % 4 == 0:
            key_gain = swap_halves(even[136:144])
        else:
            small[0, 0, 2:3, half] = jnp.where(some, key_gain, even[136:144])[0:1]
        for d, block in ((c, even), (c + 1, odd)):
            for m in range(8):
                wo[0, 0, 8 * d : 8 * d + 8, 128 * m : 128 * (m + 1)] = block[144 + 8 * m : 152 + 8 * m]
    turned = swap_halves(total)
    for t in range(4):
        cut = slice(128 * t, 128 * (t + 1))
        pair = jnp.where(some[0:1], turned[2 * t : 2 * t + 1], total[2 * t + 1 : 2 * t + 2])
        small[0, 0, 3:4, cut] = pair
        small[0, 0, 3:4, 512 + 128 * t : 640 + 128 * t] = total[10 + t : 11 + t]
    small[0, 0, 2:3, 512:1024] = jnp.zeros((1, 512), F32)
    small[0, 0, 4:8, :] = jnp.zeros((4, 1024), F32)


def spread(place, block, before=None):
    dp, n, y = block.shape[:3]
    steps = dp * y
    put = lambda rows, width: pl.BlockSpec((1, 1, rows, width), lambda i, at: (i, at[0], 0, 0))
    sizes = [(128, 1024), (128, 512), (128, 512), (128, 1024), (8, 1024)]
    given = () if before is None else tuple(before)
    return pl.pallas_call(
        spread_kernel,
        grid_spec=pltpu.PrefetchScalarGridSpec(
            num_scalar_prefetch=1,
            grid=(steps,),
            in_specs=[pl.BlockSpec((1, n, 1, PART, 128), lambda i, at: (i // y, 0, i % y, 0, 0))]
            + [pl.BlockSpec(memory_space=pl.ANY)] * len(given),
            out_specs=[put(*size) for size in sizes]
            + [
                pl.BlockSpec((8, 1024), lambda i, at: (i, 0)),
            ],
        ),
        out_shape=[like((steps, 2) + size, F32) for size in sizes]
        + [like((8 * steps, 1024), F32)],
        input_output_aliases={2 + i: i for i in range(len(given))},
        compiler_params=pltpu.CompilerParams(vmem_limit_bytes=56 * MIB),
        name="spread",
    )(place, block, *given)


def by_ctx(value):
    return lax.all_to_all(value, "ctx", split_axis=0, concat_axis=0, tiled=True)


def swap(value, axis, bit):
    n = lax.axis_size(axis)
    return lax.ppermute(value, axis, [(i, i ^ bit) for i in range(n)])


def swap_y(value):
    n = lax.axis_size("dp") * lax.axis_size("exp")
    return lax.ppermute(value, ("dp", "exp"), [(i, i ^ 6) for i in range(n)])


def held(value):
    return lax.optimization_barrier(value)


def across_chips(value):
    axes = ("dp", "ctx", "exp")
    dp, ctx, exp = (lax.axis_size(a) for a in axes)
    groups = [
        [(d * ctx + c) * exp + 2 * y + core for d in range(dp) for c in range(ctx) for y in range(exp // 2)]
        for core in range(2)
    ]
    return lax.all_to_all(
        value, axes, split_axis=0, concat_axis=0, tiled=True, axis_index_groups=groups
    )


def per_device(
    tokens,
    places,
    choices,
    cotangent,
    attn_gain,
    w_query,
    w_key,
    w_value,
    query_gain,
    key_gain,
    w_out,
    ffn_gain,
    w_router,
    w_gate,
    w_up,
    w_down,
):
    x_low = tokens[0]
    rows = x_low.shape[0]
    ctx = lax.axis_index("ctx")
    exp = lax.axis_index("exp")
    n_ctx = lax.axis_size("ctx")
    n_dp = lax.axis_size("dp")
    core = jnp.bitwise_and(exp, 1).astype(jnp.int32)
    picked = choices[0]
    g_low = cotangent[0]

    inv = places[0, ::RUN] // RUN
    runs = jnp.arange(inv.shape[0], dtype=jnp.int32)
    order = jnp.sum(jnp.where(inv[None, :] == runs[:, None], runs[None, :], 0), axis=1)
    cosine, sine = (jnp.asarray(t) for t in turn_tables(places.shape[1]))

    chosen = jnp.any(picked[:, :, None] == jnp.arange(EXPERTS, dtype=jnp.int32), axis=1)
    tri = jnp.asarray(np.tril(np.ones((rows, rows), np.float32), -1), BF)
    slot = dot(tri, chosen.astype(BF))
    slot = jnp.where(chosen, slot, -1.0).astype(BF)
    column = np.arange(EXPERTS * CAP)
    named = (np.arange(EXPERTS)[:, None] == (column // CAP)[None, :]).astype(np.float32)
    at = dot(slot, jnp.asarray(named, BF))
    spot = (at == jnp.asarray(column % CAP, F32)[None, :]).astype(BF)

    send, first_low, first_turned, q_proj, k_proj = pre(
        x_low, attn_gain, w_query, w_key, w_value, query_gain, key_gain, picked.T
    )
    g_all = lax.all_gather(g_low, "ctx")
    recv = by_ctx(send)
    kv_all, q_all, att_all, lse_all, att_send = attend(order, inv, recv, cosine, sine)
    att_send, w_gate, w_up, w_down = held((att_send, w_gate, w_up, w_down))
    down_blocks = w_down.reshape(2, 128, 8, 128).transpose(0, 2, 1, 3).reshape(2, 1024, 128)
    mine = held(jnp.concatenate([w_gate, w_up, down_blocks], axis=1))
    over_y = swap_y(mine)
    over_core = swap(mine, "exp", 1)
    heads = by_ctx(att_send)
    heads, mine, first_turned = held((heads, mine, first_turned))
    turned_all = lax.all_gather(first_turned, "ctx")
    over_both = swap(over_y, "exp", 1)
    router = w_router.T
    attended, middle, second_low, rows_send = middle_forward(heads, x_low, w_out, ffn_gain, spot)
    sent = by_ctx(rows_send.reshape(n_ctx, 2, CAP, -1))
    sent, over_core, over_both, g_all = held((sent, over_core, over_both, g_all))
    parts = (mine, over_core, over_y, over_both)
    number = jnp.reshape(2 * ctx, (1,)).astype(jnp.int32)
    back, out_rows, *kept, slots = experts(number, sent, recv, g_all, router, parts)
    back = by_ctx(back).reshape(EXPERTS * CAP, -1)
    out_part = scatter_rows(slots, out_rows)
    add = lambda *parts: sum(p.astype(F32) for p in parts).astype(BF)
    keep, near, far = weight_grads(*kept)
    back, near, keep, far, out_part, turned_all = held((back, near, keep, far, out_part, turned_all))
    out_part = lax.psum_scatter(out_part, "ctx", scatter_dimension=0, tiled=False)
    far = swap(far, "exp", 1)
    att_grad_send, grad_middle, branch = middle_back(
        spot, back, middle, second_low, router, ffn_gain, g_low, w_out
    )
    grad_recv = by_ctx(att_grad_send)
    even = 1 - jnp.bitwise_and(ctx, 1).astype(jnp.int32)
    place = jnp.stack([lax.axis_index("dp"), exp // 2, core, even]).astype(jnp.int32)
    out_mine, out_far = out_grads(place, attended, branch)
    near_a, near_b = (add(near[0, a], far[1, a]) for a in range(2))
    keep_a, keep_b = (add(keep[0, a], far[0, a]) for a in range(2))
    grad_recv, near_a, near_b, keep_a, keep_b, out_mine, out_far = held(
        (grad_recv, near_a, near_b, keep_a, keep_b, out_mine, out_far)
    )
    near_a = swap_y(near_a)
    near_b = swap_y(near_b)
    out_far = swap(out_far, "exp", 1)
    grad_send, kv_own = attend_back(
        order, inv, place[3:], grad_recv, kv_all, q_all, att_all, lse_all, cosine, sine
    )
    kv_other = swap(kv_own, "ctx", 1)
    grad_send = join(grad_send, out_mine, out_far)
    grads = by_ctx(grad_send)
    keep_a = held(add(keep_a, near_a))
    dp_a = swap(keep_a, "dp", 1)
    keep_b = held(add(keep_b, near_b))
    dp_b = swap(keep_b, "dp", 1)
    grads, keep_a, keep_b, kv_other = held((grads, keep_a, keep_b, kv_other))
    own_gain = jnp.concatenate(
        [
            lax.dynamic_slice_in_dim(query_gain, ctx * HEAD_DIM, HEAD_DIM),
            lax.dynamic_slice_in_dim(key_gain, ctx // 2 * HEAD_DIM, HEAD_DIM),
        ]
    ).astype(F32)[None]
    shares = head_grads(
        place, turned_all, grad_send, kv_other, recv, grads, grad_recv, own_gain
    )
    shares = lax.all_to_all(shares, ("dp", "exp"), split_axis=0, concat_axis=0, tiled=True)
    input_grad, gain_part = input_back(
        grads, q_proj, k_proj, x_low, grad_middle, query_gain, key_gain, attn_gain, w_query, w_key, w_value
    )
    shares, gain_part, input_grad = held((shares, gain_part, input_grad))
    chips = n_dp * n_ctx * 2
    shares, dp_a, dp_b = held((share_out(shares, gain_part, chips), dp_a, dp_b))
    whole = across_chips(shares)
    sums = [k.astype(F32) + d.astype(F32) for k, d in ((keep_a, dp_a), (keep_b, dp_b))]
    grad_gate_w = jnp.stack([v[:1024] for v in sums])
    grad_up_w = jnp.stack([v[1024:2048] for v in sums])
    grad_down_w = jnp.stack(
        [v[2048:].reshape(8, 128, 128).transpose(1, 0, 2).reshape(128, 1024) for v in sums]
    )
    outputs = (middle + out_part.astype(F32)).astype(BF)
    whole, outputs, grad_gate_w, grad_up_w, grad_down_w = held(
        (whole, outputs, grad_gate_w, grad_up_w, grad_down_w)
    )
    other = swap(whole, "exp", 1)
    shape = (n_dp, n_ctx, 2, PART, 128)
    done = spread(jnp.reshape(core, (1,)), whole.reshape(shape))
    done = spread(jnp.reshape(1 - core, (1,)), other.reshape(shape), done)
    wq, wk, wv, wo = (v.reshape(1024, -1) for v in done[:4])
    router_grad, small = done[5].T, done[4]
    return (
        outputs[None],
        input_grad[None],
        jnp.sum(small[:, :, 3], axis=(0, 1)),
        wq,
        wk,
        wv,
        small[0, 0, 0],
        small[0, 0, 2, :512],
        wo,
        small[0, 0, 1],
        router_grad,
        grad_gate_w,
        grad_up_w,
        grad_down_w,
    )


def solution(mesh):
    seqs = ("dp", "exp")
    row_spec = P(seqs, "ctx", None)
    in_specs = (row_spec, P(seqs, None), row_spec, row_spec) + (P(),) * 9
    in_specs += (P("ctx", None, "exp"), P("ctx", None, "exp"), P("ctx", "exp", None))
    out_specs = (row_spec, row_spec) + (P(),) * 9
    out_specs += (P("ctx", None, "exp"), P("ctx", None, "exp"), P("ctx", "exp", None))
    return jax.shard_map(
        per_device, mesh=mesh, in_specs=in_specs, out_specs=out_specs, check_vma=False
    )
```

```python
import jax
import jax.numpy as jnp
import numpy as np
from jax import lax
from jax.experimental import pallas as pl
from jax.experimental.pallas import tpu as pltpu
from jax.sharding import PartitionSpec as P

HEADS = 16
KV_HEADS = 8
HEAD_DIM = 64
EXPERTS = 32
CAP = 40
EPSILON = 1e-06
MASKED = -1e30
BF = jnp.bfloat16
F32 = jnp.float32
RUN = 64
QB = 512
QB_BACK = 256
PART = 208
BASE = 256
MIB = 1024 * 1024
NT = ((1,), (1,))
TN = ((0,), (0,))
VM = pl.BlockSpec(memory_space=pltpu.VMEM)
SM = pl.BlockSpec(memory_space=pltpu.SMEM)


def dot(a, b, dims=((1,), (0,))):
    return lax.dot_general(a, b, (dims, ((), ())), preferred_element_type=F32)


def call(kernel, outs, ins, name, flops, moved, scratch=(), transcendentals=0, vmem=56):
    return pl.pallas_call(
        kernel,
        out_shape=outs,
        in_specs=ins,
        out_specs=jax.tree.map(lambda _: VM, outs),
        scratch_shapes=list(scratch),
        compiler_params=pltpu.CompilerParams(vmem_limit_bytes=vmem * MIB),
        cost_estimate=pl.CostEstimate(
            flops=flops, bytes_accessed=moved, transcendentals=transcendentals
        ),
        name=name,
    )


def like(shape, dtype):
    return jax.ShapeDtypeStruct(shape, dtype)


def inverse_rms(value):
    return lax.rsqrt(jnp.mean(value * value, axis=-1, keepdims=True) + EPSILON)


def row_of(ref):
    return ref[...].astype(F32).reshape(1, -1)


def lanes_of(rows):
    return lax.broadcasted_iota(jnp.int32, (rows, 128), 1)


def swap_halves(tile):
    return pltpu.roll(tile.astype(F32), 64, 1)


def pack_head(wide, head):
    tile = wide[:, 128 * (head // 2) : 128 * (head // 2 + 1)]
    low = lanes_of(RUN) < 64
    if head % 2 == 0:
        return jnp.where(low, tile[:RUN], swap_halves(tile[RUN:]))
    return jnp.where(low, swap_halves(tile[:RUN]), tile[RUN:])


def unpack_heads(even, odd):
    low = lanes_of(RUN) < 64
    even, odd = even.astype(F32), odd.astype(F32)
    return jnp.concatenate(
        [jnp.where(low, even, swap_halves(odd)), jnp.where(low, swap_halves(even), odd)], axis=0
    )


def turn_tables(seq):
    half = HEAD_DIM // 2
    frequency = (10000.0 ** (-np.arange(half) * 2.0 / HEAD_DIM)).astype(np.float32)
    angles = (np.arange(seq, dtype=np.float32)[:, None] * frequency[None, :]).astype(np.float64)
    cosine, sine = np.cos(angles), np.sin(angles)
    return np.concatenate([cosine, cosine, -sine, sine], axis=1).astype(np.float32)


def split_table(table):
    low = lanes_of(table.shape[0]) < 64
    return jnp.where(low, table, 1.0), jnp.where(low, pltpu.roll(table, 64, 1), 0.0)


def turn(tile, cosine, sine):
    other = jnp.where(lanes_of(tile.shape[0]) < 32, pltpu.roll(tile, 96, 1), pltpu.roll(tile, 32, 1))
    return tile * cosine + other * sine


def pre_kernel(x_ref, gain, wq, wk, wv, q_gain, k_gain, picks, send, first_out, turned_out, q_out, k_out):
    x = x_ref[...].astype(F32)
    wide = x * inverse_rms(x) * row_of(gain)
    first = wide.astype(BF)
    first_out[...] = first
    q = dot(first, wq[...])
    k = dot(first, wk[...])
    v = dot(first, wv[...])
    q_out[...] = q
    k_out[...] = k
    qn = q * inverse_rms(q) * (row_of(q_gain) * HEAD_DIM ** (-0.5))
    kn = k * inverse_rms(k) * row_of(k_gain)
    low = lanes_of(x.shape[0]) < 64
    for h in range(KV_HEADS):
        cut = slice(128 * (h // 2), 128 * (h // 2 + 1))
        kt, vt = kn[:, cut], v[:, cut]
        if h % 2 == 0:
            both = jnp.where(low, kt, swap_halves(vt))
        else:
            both = jnp.where(low, swap_halves(kt), vt)
        both = both.astype(BF)
        send[2 * h, 0 : 2 * RUN, :] = both
        send[2 * h + 1, 0 : 2 * RUN, :] = both
    lane = lanes_of(x.shape[0])
    rows = jnp.transpose(jnp.where(lane == 0, inverse_rms(q), inverse_rms(k)))[0:2, :]
    high = rows.astype(BF).astype(F32)
    named = jnp.concatenate(
        [picks[...].astype(F32), high, rows - high, jnp.zeros((4, 128), F32)], axis=0
    ).astype(BF)
    for d in range(HEADS):
        send[d, 2 * RUN : 3 * RUN, :] = pack_head(qn, d).astype(BF)
        send[d, 3 * RUN : 3 * RUN + 16, :] = named
    turned_out[...] = jnp.transpose(first.astype(F32)).astype(BF)


def pre(x, gain, wq, wk, wv, q_gain, k_gain, picks):
    rows, width = x.shape
    return call(
        pre_kernel,
        (
            like((HEADS, 3 * RUN + 16, 128), BF),
            like((rows, width), BF),
            like((width, rows), BF),
            like((rows, wq.shape[1]), F32),
            like((rows, wk.shape[1]), F32),
        ),
        [VM] * 8,
        "pre",
        2 * rows * width * 2048,
        6 * 1024 * 1024,
    )(x, gain, wq, wk, wv, q_gain, k_gain, picks)


def turn_over(source, target):
    for i in range(source.shape[0] // 128):
        cut = slice(128 * i, 128 * (i + 1))
        target[:, cut] = jnp.transpose(source[cut, :].astype(F32)).astype(BF)


def masked_scores(kv, q, block):
    scores = dot(kv, q, NT)
    end = scores.shape[0]
    row = lax.broadcasted_iota(jnp.int32, (block, block), 0)
    col = lax.broadcasted_iota(jnp.int32, (block, block), 1)
    last = jnp.where(row <= col, scores[end - block :, :], MASKED)
    return last if end == block else jnp.concatenate([scores[: end - block, :], last], axis=0)


def attend_kernel(order, inv, recv, table, kv_out, q_out, att_out, lse_out, send_out, turned):
    seq = kv_out.shape[0]
    lane = lanes_of(RUN)

    def gather(b, carry):
        s = order[b]
        c = lax.shift_right_logical(s, 1)
        half = jnp.bitwise_and(s, 1)
        rows = pl.ds(pl.multiple_of(b * RUN, RUN), RUN)
        cos, sin = split_table(table[rows, :])
        kv = recv[c, pl.ds(pl.multiple_of(half * RUN, RUN), RUN), :].astype(F32)
        kv_out[rows, :] = turn(kv, cos, sin).astype(BF)
        tile = recv[c, pl.ds(2 * RUN, RUN), :].astype(F32)
        q = jnp.where(lane < 64, jnp.where(half == 0, tile, swap_halves(tile)), 0.0)
        q_out[rows, :] = turn(q, cos, sin).astype(BF)
        return carry

    lax.fori_loop(0, seq // RUN, gather, 0, unroll=32)
    turn_over(kv_out, turned)
    for i in range(seq // QB):
        here = slice(i * QB, (i + 1) * QB)
        end = (i + 1) * QB
        scores = masked_scores(kv_out[:end, :], q_out[here, :], QB)
        top = jnp.max(scores, axis=0, keepdims=True)
        weights = jnp.exp(scores - top)
        total = jnp.sum(weights, axis=0, keepdims=True)
        att = jnp.transpose(dot(turned[:, :end], weights.astype(BF)) / total)
        att_out[here, :] = att.astype(BF)
        lse_out[:, here] = jnp.broadcast_to(top + jnp.log(total), (8, QB))

    def place(c, carry):
        b0, b1 = inv[2 * c], inv[2 * c + 1]
        first = att_out[pl.ds(pl.multiple_of(b0 * RUN, RUN), RUN), :]
        second = att_out[pl.ds(pl.multiple_of(b1 * RUN, RUN), RUN), :]
        send_out[c] = jnp.where(lane < 64, swap_halves(first), second.astype(F32)).astype(BF)
        return carry

    lax.fori_loop(0, send_out.shape[0], place, 0, unroll=16)


def attend(order, inv, recv, table):
    n = recv.shape[0]
    seq = n * 128
    return call(
        attend_kernel,
        (
            like((seq, 128), BF),
            like((seq, 128), BF),
            like((seq, 128), BF),
            like((8, seq), F32),
            like((n, RUN, 128), BF),
        ),
        [SM, SM, VM, VM],
        "attend",
        4 * seq * seq * 128 // 2,
        14 * seq * 128,
        [pltpu.VMEM((128, seq), BF)],
        transcendentals=seq * seq // 2,
    )(order, inv, recv, table)


def attend_back_kernel(
    order, inv, even, recv, kv_in, q_in, att_in, lse_in, table,
    send_out, kv_grad_out, g_all, dq_all, dkv_all, sums, turned,
):
    seq = kv_in.shape[0]
    lane = lanes_of(RUN)

    def gather(b, carry):
        s = order[b]
        c = lax.shift_right_logical(s, 1)
        half = jnp.bitwise_and(s, 1)
        tile = recv[c, 0:RUN, :].astype(F32)
        g_all[pl.ds(pl.multiple_of(b * RUN, RUN), RUN), :] = jnp.where(
            lane >= 64, jnp.where(half == 1, tile, swap_halves(tile)), 0.0
        ).astype(BF)
        return carry

    lax.fori_loop(0, seq // RUN, gather, 0, unroll=32)
    turn_over(kv_in, turned)
    steps = seq // QB_BACK
    for i in reversed(range(steps)):
        here = slice(i * QB_BACK, (i + 1) * QB_BACK)
        end = (i + 1) * QB_BACK
        kv, q, g = kv_in[:end, :], q_in[here, :], g_all[here, :]
        offset = jnp.sum(jnp.transpose(att_in[here, :].astype(F32) * g.astype(F32)), axis=0, keepdims=True)
        weights = jnp.exp(masked_scores(kv, q, QB_BACK) - lse_in[0:1, here])
        grad_scores = (weights * (dot(kv, g, NT) - offset)).astype(BF)
        dq_all[here, :] = jnp.transpose(dot(turned[:, :end], grad_scores))
        step = dot(grad_scores, q) + dot(weights.astype(BF), g)
        if i == steps - 1:
            dkv_all[...] = step
        else:
            dkv_all[:end, :] += step

    def place(c, carry):
        b0, b1 = inv[2 * c], inv[2 * c + 1]
        r0 = pl.ds(pl.multiple_of(b0 * RUN, RUN), RUN)
        r1 = pl.ds(pl.multiple_of(b1 * RUN, RUN), RUN)
        cos0, sin0 = split_table(table[r0, :])
        cos1, sin1 = split_table(table[r1, :])
        kv0 = turn(dkv_all[r0, :], cos0, -sin0).astype(BF)
        kv1 = turn(dkv_all[r1, :], cos1, -sin1).astype(BF)
        send_out[c, 0 : RUN, :] = kv0
        send_out[c, RUN : 2 * RUN, :] = kv1
        kv0, kv1 = kv0.astype(F32), kv1.astype(F32)
        values = jnp.where(lane < 64, swap_halves(kv0), kv1)
        keys = jnp.where(lane < 64, kv0, swap_halves(kv1))
        kv_grad_out[c] = jnp.where(even[0] == 1, values, keys).astype(BF)
        both_q = jnp.concatenate([dq_all[r0, :], dq_all[r1, :]], axis=0)
        both_q = both_q * jnp.concatenate([q_in[r0, :], q_in[r1, :]], axis=0).astype(F32)
        both_k = jnp.concatenate([dkv_all[r0, :], dkv_all[r1, :]], axis=0)
        both_k = both_k * jnp.concatenate([kv_in[r0, :], kv_in[r1, :]], axis=0).astype(F32)
        some = jnp.where(lanes_of(8) < 64, 1.0, 0.0).astype(BF)
        sums[pl.ds(c, 1), :] = dot(some, both_q.astype(BF), NT)[0:1, :]
        sums[pl.ds(n + c, 1), :] = dot(some, both_k.astype(BF), NT)[0:1, :]
        q0 = turn(dq_all[r0, :], cos0, -sin0)
        q1 = turn(dq_all[r1, :], cos1, -sin1)
        both = jnp.where(lane < 64, q0, swap_halves(q1))
        send_out[c, 2 * RUN : 3 * RUN, :] = (both * HEAD_DIM ** (-0.5)).astype(BF)
        return carry

    n = send_out.shape[0]
    lax.fori_loop(0, n, place, 0, unroll=16)
    for c in range(n):
        send_out[c, 3 * RUN : 3 * RUN + 2 * n, :] = sums[...].astype(BF)


def attend_back(order, inv, even, recv, kv, q, att, lse, table):
    n = recv.shape[0]
    seq = n * 128
    whole = lambda v: pl.BlockSpec(v.shape, lambda i: (0,) * v.ndim)
    return pl.pallas_call(
        attend_back_kernel,
        grid=(1,),
        out_shape=(like((n, BASE + 3 * RUN + 2 * n, 128), BF), like((n, RUN, 128), BF)),
        in_specs=[SM, SM, SM] + [whole(v) for v in (recv, kv, q, att, lse, table)],
        out_specs=(
            pl.BlockSpec((n, BASE, 128), lambda i: (0, 1, 0)),
            pl.BlockSpec((n, RUN, 128), lambda i: (0, 0, 0)),
        ),
        scratch_shapes=[
            pltpu.VMEM((seq, 128), BF),
            pltpu.VMEM((seq, 128), F32),
            pltpu.VMEM((seq, 128), F32),
            pltpu.VMEM((2 * n, 128), F32),
            pltpu.VMEM((128, seq), BF),
        ],
        compiler_params=pltpu.CompilerParams(vmem_limit_bytes=56 * MIB),
        cost_estimate=pl.CostEstimate(
            flops=10 * seq * seq * 128 // 2, bytes_accessed=20 * seq * 128, transcendentals=seq * seq // 2
        ),
        name="attend_back",
    )(order, inv, even, recv, kv, q, att, lse, table)


def join_kernel(send, mine, far, out_ref):
    for c in range(out_ref.shape[0]):
        for j in range(4):
            rows = slice(8 * c, 8 * c + 8)
            both = mine[j, rows, :].astype(F32) + far[j, rows, :].astype(F32)
            for m in range(0, 8, 2):
                at = 64 * j + 8 * m
                pair = (both[:, 128 * m : 128 * m + 128], both[:, 128 * m + 128 : 128 * m + 256])
                out_ref[c, at : at + 16, :] = jnp.concatenate(pair, axis=0).astype(BF)


def join(send, mine, far):
    whole = pl.BlockSpec(mine.shape, lambda i: (0, 0, 0))
    return pl.pallas_call(
        join_kernel,
        grid=(1,),
        out_shape=like(send.shape, BF),
        in_specs=[pl.BlockSpec(memory_space=pl.ANY), whole, whole],
        out_specs=pl.BlockSpec((send.shape[0], BASE, 128), lambda i: (0, 0, 0)),
        input_output_aliases={0: 0},
        compiler_params=pltpu.CompilerParams(vmem_limit_bytes=56 * MIB),
        cost_estimate=pl.CostEstimate(flops=1 << 20, bytes_accessed=1 << 20, transcendentals=0),
        name="join",
    )(send, mine, far)


def slot_masks(slot, pair):
    line = lax.broadcasted_iota(jnp.int32, (2 * CAP, 128), 0).astype(F32)
    left = (line < CAP) & (line == slot[2 * pair : 2 * pair + 1, :])
    right = (line >= CAP) & (line - CAP == slot[2 * pair + 1 : 2 * pair + 2, :])
    return jnp.where(left, 1.0, 0.0).astype(BF), jnp.where(right, 1.0, 0.0).astype(BF)


def cotangent_kernel(number, picks_ref, g_ref, rows_ref, slot_ref):
    n_ctx = g_ref.shape[0]
    picks = picks_ref[...].astype(F32)[:, :8, :]
    before = lax.broadcasted_iota(jnp.int32, (128, 128), 0) < lax.broadcasted_iota(
        jnp.int32, (128, 128), 1
    )
    before = jnp.where(before, 1.0, 0.0).astype(BF)
    for a in range(2):
        e = (number[0] + a).astype(F32)
        named = jnp.max(jnp.where(picks == e, 1.0, 0.0), axis=1)
        slot = jnp.where(named > 0.0, dot(named.astype(BF), before), -1.0)
        slot_ref[a] = slot
        for p in range(n_ctx // 2):
            left, right = slot_masks(slot, p)
            rows_ref[a, 2 * CAP * p : 2 * CAP * (p + 1), :] = (
                dot(left, g_ref[2 * p]) + dot(right, g_ref[2 * p + 1])
            ).astype(BF)


def cotangent_rows(number, recv, g_all):
    n_ctx = g_all.shape[0]
    whole = lambda *shape: pl.BlockSpec(shape, lambda i: (0,) * len(shape))
    return pl.pallas_call(
        cotangent_kernel,
        grid=(1,),
        out_shape=(like((2, n_ctx * CAP, 1024), BF), like((2, n_ctx, 128), F32)),
        in_specs=[
            SM,
            pl.BlockSpec((n_ctx, 16, 128), lambda i: (0, 3 * RUN // 16, 0)),
            whole(*g_all.shape),
        ],
        out_specs=(whole(2, n_ctx * CAP, 1024), whole(2, n_ctx, 128)),
        compiler_params=pltpu.CompilerParams(vmem_limit_bytes=56 * MIB),
        cost_estimate=pl.CostEstimate(
            flops=8 * n_ctx * 80 * 128 * 1024, bytes_accessed=8 * 1024 * 1024, transcendentals=0
        ),
        name="cotangent_rows",
    )(number, recv, g_all)


def expert_steps(e, rows_ref, g_ref, router_ref, parts):
    n_ctx = rows_ref.shape[0]
    rows = jnp.concatenate([rows_ref[c, 0].astype(F32) for c in range(n_ctx)], axis=0).astype(BF)
    grads = g_ref[0].astype(F32)
    logits = dot(rows, router_ref[...], NT)
    lane = lax.broadcasted_iota(jnp.int32, logits.shape, 1)
    powers = jnp.exp(logits - jnp.max(logits, axis=1, keepdims=True))
    gate = jnp.sum(jnp.where(lane == e, powers, 0.0), axis=1, keepdims=True) / jnp.sum(
        powers, axis=1, keepdims=True
    )
    w_gate = jnp.concatenate([w[0, 0:1024, :] for w in parts], axis=1)
    w_up = jnp.concatenate([w[0, 1024:2048, :] for w in parts], axis=1)
    w_down = jnp.concatenate(
        [
            jnp.concatenate([w[0, 2048 + 128 * n : 2176 + 128 * n, :] for n in range(8)], axis=1)
            for w in parts
        ],
        axis=0,
    )
    gate_act = dot(rows, w_gate)
    up_act = dot(rows, w_up)
    sig = 1.0 / (1.0 + jnp.exp(-gate_act))
    silu = gate_act * sig
    hidden = (silu * up_act).astype(BF)
    expert_out = dot(hidden, w_down)
    grad_rows = (gate * grads).astype(BF)
    grad_hidden = dot(grad_rows, w_down, NT)
    ga = (grad_hidden * up_act * sig * (1.0 + gate_act * (1.0 - sig))).astype(BF)
    gu = (grad_hidden * silu).astype(BF)
    return rows, grads, gate, w_gate, w_up, hidden, expert_out, grad_rows, ga, gu


def expert_kernel(number, rows_ref, g_ref, router_ref, *refs):
    parts, back_ref = refs[:4], refs[4]
    e = number[0] + pl.program_id(0)
    rows, grads, _, w_gate, w_up, _, expert_out, _, ga, gu = expert_steps(
        e, rows_ref, g_ref, router_ref, parts
    )
    grad_gate = jnp.sum(grads * expert_out, axis=1, keepdims=True)
    back = dot(ga, w_gate, NT) + dot(gu, w_up, NT)
    high = grad_gate.astype(BF).astype(F32)
    lane = lanes_of(rows.shape[0])
    tail = jnp.where(lane == e, high, jnp.where(lane == e + EXPERTS, grad_gate - high, 0.0))
    for c in range(rows_ref.shape[0]):
        cut = slice(CAP * c, CAP * (c + 1))
        back_ref[c, 0, :, 0:1024] = back[cut, :].astype(BF)
        back_ref[c, 0, :, 1024:1152] = tail[cut, :].astype(BF)


def weight_grad_kernel(number, rows_ref, g_ref, router_ref, slot_ref, *refs):
    parts, (keep, near, far, sums_ref) = refs[:4], refs[4:]
    e = number[0] + pl.program_id(0)
    rows, _, gate, _, _, hidden, expert_out, grad_rows, ga, gu = expert_steps(
        e, rows_ref, g_ref, router_ref, parts
    )
    line = lax.broadcasted_iota(jnp.int32, (CAP, 128), 0).astype(F32)
    first = pl.program_id(0) == 0
    out_rows = gate * expert_out
    for c in range(rows_ref.shape[0]):
        mask = jnp.where(line == slot_ref[0, c : c + 1, :], 1.0, 0.0).astype(BF)
        part = dot(mask, out_rows[CAP * c : CAP * (c + 1), :].astype(BF), TN)
        before = jnp.where(first, 0.0, sums_ref[c].astype(F32))
        sums_ref[c] = (part + before).astype(BF)
    gate_grad = dot(rows, ga, TN)
    up_grad = dot(rows, gu, TN)
    down_grad = dot(hidden, grad_rows, TN)
    for j, (ref, at) in enumerate([(keep, 0), (far, 0), (near, 0), (far, 1)]):
        cut = slice(128 * j, 128 * (j + 1))
        ref[at, 0, 0:1024, :] = gate_grad[:, cut].astype(BF)
        ref[at, 0, 1024:2048, :] = up_grad[:, cut].astype(BF)
        for n in range(8):
            ref[at, 0, 2048 + 128 * n : 2176 + 128 * n, :] = down_grad[
                cut, 128 * n : 128 * (n + 1)
            ].astype(BF)


def expert_call(kernel, name, number, rows, grads, router, slots, parts, outs, out_specs):
    n_ctx = rows.shape[0]
    n = n_ctx * CAP
    extra = () if slots is None else (slots,)
    return pl.pallas_call(
        kernel,
        grid=(2,),
        out_shape=outs,
        in_specs=[
            SM,
            pl.BlockSpec((n_ctx, 1, CAP, 1024), lambda i: (0, i, 0, 0)),
            pl.BlockSpec((1, n, 1024), lambda i: (i, 0, 0)),
            pl.BlockSpec(router.shape, lambda i: (0, 0)),
        ]
        + [pl.BlockSpec((1,) + v.shape[1:], lambda i: (i, 0, 0)) for v in extra + tuple(parts)],
        out_specs=out_specs,
        compiler_params=pltpu.CompilerParams(vmem_limit_bytes=58 * MIB),
        cost_estimate=pl.CostEstimate(
            flops=24 * n * 1024 * 512, bytes_accessed=20 * 1024 * 1024, transcendentals=2 * n * 512
        ),
        name=name,
    )(number, rows, grads, router, *extra, *parts)


def experts(number, rows, grads, router, parts):
    n_ctx = rows.shape[0]
    return expert_call(
        expert_kernel, "experts", number, rows, grads, router, None, parts,
        like((n_ctx, 2, CAP, 1152), BF),
        pl.BlockSpec((n_ctx, 1, CAP, 1152), lambda i: (0, i, 0, 0)),
    )


def weight_grads(number, rows, grads, router, slots, parts):
    n_ctx = rows.shape[0]
    put = lambda k: pl.BlockSpec((k, 1, 3072, 128), lambda i: (0, i, 0, 0))
    return expert_call(
        weight_grad_kernel, "weight_grads", number, rows, grads, router, slots, parts,
        (
            like((1, 2, 3072, 128), BF),
            like((1, 2, 3072, 128), BF),
            like((2, 2, 3072, 128), BF),
            like((n_ctx, 128, 1024), BF),
        ),
        (put(1), put(1), put(2), pl.BlockSpec((n_ctx, 128, 1024), lambda i: (0, 0, 0))),
    )


def middle_kernel(heads, x_ref, w_out, gain, spot, attended_out, middle_out, second_out, send_out):
    attended = jnp.concatenate(
        [unpack_heads(heads[2 * t], heads[2 * t + 1]) for t in range(HEADS // 2)], axis=1
    ).astype(BF)
    attended_out[...] = attended
    middle = x_ref[...].astype(F32) + dot(attended, w_out[...])
    middle_out[...] = middle
    second = (middle * inverse_rms(middle) * row_of(gain)).astype(BF)
    second_out[...] = second
    send_out[...] = dot(spot[...], second, TN).astype(BF)


def middle_forward(heads, x, w_out, gain, spot):
    rows, width = x.shape
    return call(
        middle_kernel,
        (
            like((rows, width), BF),
            like((rows, width), F32),
            like((rows, width), BF),
            like((spot.shape[1], width), BF),
        ),
        [VM] * 5,
        "middle",
        2 * rows * width * (1024 + 1280),
        6 * 1024 * 1024,
    )(heads, x, w_out, gain, spot)


def middle_back_kernel(
    spot, back, middle_ref, second, router, gain, g_ref, w_out,
    send, grad_out, branch_out,
):
    summed = dot(spot[...], back[...])
    logits = dot(second[...], router[...], NT)
    powers = jnp.exp(logits - jnp.max(logits, axis=1, keepdims=True))
    probs = powers / jnp.sum(powers, axis=1, keepdims=True)
    last = summed[:, 1024:1152]
    grad_sel = (last + pltpu.roll(last, 128 - EXPERTS, 1))[:, :EXPERTS]
    grad_logits = probs * (grad_sel - jnp.sum(probs * grad_sel, axis=1, keepdims=True))
    high = grad_logits.astype(BF)
    rest = (grad_logits - high.astype(F32)).astype(BF)
    upstream = summed[:, :1024] + dot(high, router[...]) + dot(rest, router[...])
    middle = middle_ref[...]
    r = inverse_rms(middle)
    hat = middle * r
    gain_part = jnp.sum(upstream * hat, axis=0, keepdims=True)
    router_part = dot(high, second[...], TN) + dot(rest, second[...], TN)
    low = lanes_of(EXPERTS) < 64
    first_row = lax.broadcasted_iota(jnp.int32, (EXPERTS, 128), 0) == 0
    for d in range(HEADS):
        cut = slice(128 * (d // 2), 128 * (d // 2 + 1))
        tile = router_part[:, cut]
        part = jnp.where(first_row, jnp.broadcast_to(gain_part[:, cut], (EXPERTS, 128)), 0.0)
        if d % 2 == 0:
            misc = jnp.where(low, tile, swap_halves(part))
        else:
            misc = jnp.where(low, swap_halves(tile), part)
        send[d, RUN : RUN + EXPERTS, :] = misc.astype(BF)
    scaled = upstream * row_of(gain)
    grad = (
        r * (scaled - hat * jnp.mean(scaled * hat, axis=1, keepdims=True)) + g_ref[...].astype(F32)
    )
    grad_out[...] = grad
    branch = grad.astype(BF)
    branch_out[...] = branch
    att = dot(branch, w_out[...], NT)
    for d in range(HEADS):
        send[d, 0:RUN, :] = pack_head(att, d).astype(BF)


def middle_back(spot, back, middle, second, router, gain, g_low, w_out):
    rows, width = middle.shape
    return call(
        middle_back_kernel,
        (
            like((HEADS, RUN + EXPERTS, 128), BF),
            like((rows, width), F32),
            like((rows, width), BF),
        ),
        [VM] * 8,
        "middle_back",
        2 * rows * width * (1280 + 1024),
        6 * 1024 * 1024,
    )(spot, back, middle, second, router, gain, g_low, w_out)


def out_grad_kernel(place, attended, branch, mine, far):
    for j in range(8):
        c, y, d = j // 4, j // 2 % 2, j % 2
        block = (
            jnp.bitwise_xor(place[0], d) * 4 + jnp.bitwise_xor(place[1], y) * 2 + jnp.bitwise_xor(place[2], c)
        )
        part = attended[:, pl.ds(pl.multiple_of(block * 128, 128), 128)]
        (far if c else mine)[j % 4] = dot(part, branch[...], TN).astype(BF)


def out_grads(place, attended, branch):
    return call(
        out_grad_kernel,
        (like((4, 128, 1024), BF), like((4, 128, 1024), BF)),
        [SM, VM, VM],
        "out_grads",
        1 << 20,
        1 << 18,
    )(place, attended, branch)


def queries_of(recv):
    return jnp.concatenate(
        [
            unpack_heads(
                recv[2 * t, BASE + 2 * RUN : BASE + 3 * RUN, :],
                recv[2 * t + 1, BASE + 2 * RUN : BASE + 3 * RUN, :],
            )
            for t in range(HEADS // 2)
        ],
        axis=1,
    )


def keys_values_of(recv):
    low = lanes_of(2 * RUN) < 64
    both = [
        recv[2 * j, BASE : BASE + 2 * RUN, :].astype(F32)
        + recv[2 * j + 1, BASE : BASE + 2 * RUN, :].astype(F32)
        for j in range(KV_HEADS)
    ]
    keys, values = [], []
    for t in range(KV_HEADS // 2):
        keys.append(jnp.where(low, both[2 * t], swap_halves(both[2 * t + 1])))
        values.append(jnp.where(low, swap_halves(both[2 * t]), both[2 * t + 1]))
    return jnp.concatenate(keys, axis=1), jnp.concatenate(values, axis=1)


def input_kernel(
    recv, q_ref, k_ref, x_ref, middle, q_gain, k_gain, gain, wq, wk, wv, out_ref, gain_ref
):
    uq = queries_of(recv)
    uk, dv = keys_values_of(recv)
    q, k = q_ref[...], k_ref[...]
    rq, rk = inverse_rms(q), inverse_rms(k)
    qh, kh = q * rq, k * rk
    uq, uk = uq * row_of(q_gain), uk * row_of(k_gain)
    gq = (rq * (uq - qh * jnp.mean(uq * qh, axis=1, keepdims=True))).astype(BF)
    gk = (rk * (uk - kh * jnp.mean(uk * kh, axis=1, keepdims=True))).astype(BF)
    upstream = dot(gq, wq[...], NT) + dot(gk, wk[...], NT) + dot(dv.astype(BF), wv[...], NT)
    x = x_ref[...].astype(F32)
    r = inverse_rms(x)
    hat = x * r
    x_part = jnp.sum(upstream * hat, axis=0, keepdims=True)
    scaled = upstream * row_of(gain)
    out_ref[...] = middle[...] + r * (scaled - hat * jnp.mean(scaled * hat, axis=1, keepdims=True))
    half = jnp.zeros((1, 64), F32)
    rows = [jnp.concatenate([half, x_part[:, 64 * i : 64 * (i + 1)]], axis=1) for i in range(8)]
    none = jnp.zeros((2, 128), F32)
    more = [x_part[:, 512 + 128 * i : 640 + 128 * i] for i in range(4)]
    gain_ref[...] = jnp.concatenate(rows + [none] + more + [none], axis=0)


def input_back(recv, q, k, x, middle, q_gain, k_gain, gain, wq, wk, wv):
    rows, width = x.shape
    return call(
        input_kernel,
        (like((rows, width), F32), like((16, 128), F32)),
        [VM] * 11,
        "input_back",
        2 * rows * width * 2048,
        8 * 1024 * 1024,
    )(recv, q, k, x, middle, q_gain, k_gain, gain, wq, wk, wv)


def head_grad_kernel(
    place, turned, early, later, queries, kv_other, normed, out_parts, sums_ref, branch, gain_ref, out_ref
):
    n = early.shape[0]
    low = lanes_of(128) < 64
    gain = gain_ref[...]
    sums = sums_ref[0].astype(F32)
    others = branch[0].astype(F32)
    for c in range(1, n):
        sums = sums + sums_ref[c].astype(F32)
        others = others + branch[c].astype(F32)
    out_rows = out_parts[0].astype(F32)
    for c in range(1, n):
        out_rows = out_rows + out_parts[c].astype(F32)
    q_means = sums[0:n, :] / (HEADS * HEAD_DIM)
    k_means = sums[n : 2 * n, :] / (KV_HEADS * HEAD_DIM)
    total = None
    gains = None
    for p in range(n // 2):
        parts = []
        for c in (2 * p, 2 * p + 1):
            packed = queries[c].astype(F32)
            uq = jnp.concatenate([packed, swap_halves(packed)], axis=0)
            both = jnp.concatenate([early[c].astype(F32), later[c].astype(F32)], axis=0)
            other = kv_other[c].astype(F32)
            other = jnp.concatenate([swap_halves(other), other], axis=0)
            keys = swap_halves(both) + other
            upstream = jnp.where(low, uq, keys)
            packed = normed[c, 2 * RUN : 3 * RUN, :].astype(F32)
            qn = jnp.concatenate([packed, swap_halves(packed)], axis=0) * HEAD_DIM**0.5
            hat = jnp.where(low, qn, swap_halves(normed[c, 0 : 2 * RUN, :])) / gain
            factors = normed[c, 3 * RUN : 3 * RUN + 16, :].astype(F32)
            factors = factors[8:10, :] + factors[10:12, :]
            rows = jnp.concatenate(
                [factors, q_means[c : c + 1, :], k_means[c : c + 1, :], jnp.zeros((4, 128), F32)], axis=0
            )
            cols = jnp.transpose(jnp.concatenate([rows] * 16, axis=0))
            r = jnp.where(low, cols[:, 0:1], cols[:, 1:2])
            m = jnp.where(low, cols[:, 2:3], cols[:, 3:4])
            grad = r * (upstream * gain - hat * m)
            part = jnp.sum(upstream * hat, axis=0, keepdims=True)
            gains = part if gains is None else gains + part
            parts.append(jnp.where(low | (place[3] == 1), grad, both + other).astype(BF))
        left = jnp.concatenate([turned[2 * p], turned[2 * p + 1]], axis=1)
        step = dot(left, jnp.concatenate(parts, axis=0))
        total = step if total is None else total + step
    low_row = low[0:1, :]
    gains = jnp.where(low_row | (place[3] == 1), gains, 0.0)
    ffn = jnp.where(low_row, swap_halves(others[0:8, :])[0:1, :], 0.0)
    rows = jnp.concatenate([gains, ffn, jnp.zeros((6, 128), F32)], axis=0)
    some = lanes_of(8) < 64
    for s in range(8):
        out_ref[s, 0:128, :] = total[128 * s : 128 * (s + 1), :].astype(BF)
        kept = jnp.where(some, others[8 * (s // 2) : 8 * (s // 2) + 8, :], 0.0)
        out_ref[s, 128:144, :] = jnp.concatenate(
            [kept, rows if s == 0 else jnp.zeros((8, 128), F32)], axis=0
        ).astype(BF)
        out_ref[s, 144:PART, :] = jnp.zeros((64, 128), BF)
    for j in range(4):
        at = jnp.bitwise_xor(place[0], j % 2) * 4 + jnp.bitwise_xor(place[1], j // 2) * 2 + place[2]
        out_ref[pl.ds(at, 1), 144:PART, :] = out_rows[64 * j : 64 * j + 64, :].astype(BF)[None]


def head_grads(place, turned, own, kv_other, normed, grads, branch, gain):
    whole = lambda v: pl.BlockSpec(v.shape, lambda i: (0,) * v.ndim)
    n = own.shape[0]
    part = lambda rows, at: pl.BlockSpec((n, rows, 128), lambda i: (0, at // rows, 0))
    return pl.pallas_call(
        head_grad_kernel,
        grid=(1,),
        out_shape=like((8, PART, 128), BF),
        in_specs=[
            SM,
            whole(turned),
            part(RUN, BASE),
            part(RUN, BASE + RUN),
            part(RUN, BASE + 2 * RUN),
            whole(kv_other),
            whole(normed),
            part(BASE, 0),
            part(2 * n, BASE + 3 * RUN),
            part(EXPERTS, RUN),
            whole(gain),
        ],
        out_specs=pl.BlockSpec((8, PART, 128), lambda i: (0, 0, 0)),
        compiler_params=pltpu.CompilerParams(vmem_limit_bytes=56 * MIB),
        cost_estimate=pl.CostEstimate(
            flops=2 * 2048 * 1024 * 128, bytes_accessed=8 * 1024 * 1024, transcendentals=0
        ),
        name="head_grads",
    )(place, turned, own, own, own, kv_other, normed, grads, grads, branch, gain)


def share_kernel(shares, gain_ref, out_ref):
    total = shares[0].astype(F32)
    for s in range(1, shares.shape[0]):
        total = total + shares[s].astype(F32)
    total = jnp.concatenate([total[0:128], total[128:144] + gain_ref[...], total[144:PART]], axis=0)
    total = total.astype(BF)
    for c in range(out_ref.shape[0]):
        out_ref[c] = total


def share_out(shares, gain, chips):
    return call(
        share_kernel,
        like((chips, PART, 128), BF),
        [VM, VM],
        "share_out",
        1 << 18,
        4 * 1024 * 1024,
    )(shares, gain)


def spread_kernel(place, block_ref, *refs):
    wq, wk, wv, wo, router, x_gain, q_gain, k_gain, f_gain = refs[-9:]
    n = block_ref.shape[1]
    low = lanes_of(128) < 64
    some = lanes_of(8) < 64
    total = None
    kept = None
    queries, keys, seconds = [], [], []
    for c in range(0, n, 2):
        even, odd = block_ref[0, c, 0].astype(F32), block_ref[0, c + 1, 0].astype(F32)
        wide = slice(64 * c, 64 * c + 128)
        wq[0, 0, :, wide] = jnp.where(low, even[:128], swap_halves(odd[:128]))
        key, value = even[:128], odd[:128]
        if c % 4 == 0:
            kept = (swap_halves(key), swap_halves(value))
        else:
            half = slice(32 * c - 64, 32 * c + 64)
            wk[0, 0, :, half] = jnp.where(low, kept[0], key)
            wv[0, 0, :, half] = jnp.where(low, kept[1], value)
        router[:, wide] = jnp.where(some, even[128:136], swap_halves(odd[128:136]))
        sums = even[128:144] + odd[128:144]
        total = sums if total is None else total + sums
        pairs = jnp.where(some, even[136:144], swap_halves(odd[136:144]))
        queries.append(pairs[0:1])
        seconds.append(pairs[1:2])
        if c % 4 == 0:
            key_gain = swap_halves(even[136:144])
        else:
            keys.append(jnp.where(some, key_gain, even[136:144])[0:1])
        for d, block in ((c, even), (c + 1, odd)):
            for m in range(8):
                wo[0, 0, 8 * d : 8 * d + 8, 128 * m : 128 * (m + 1)] = block[144 + 8 * m : 152 + 8 * m]
    turned = swap_halves(total)
    firsts = [
        jnp.where(some[0:1], turned[2 * t : 2 * t + 1], total[2 * t + 1 : 2 * t + 2]) for t in range(4)
    ]
    firsts = jnp.concatenate(firsts + [total[10 + t : 11 + t] for t in range(4)], axis=1)

    @pl.when(pl.program_id(0) == 0)
    def _():
        ours = place[0] == 0
        given = refs[4:8] if len(refs) > 9 else None
        for i, (ref, made) in enumerate([(x_gain, None), (q_gain, queries), (k_gain, keys), (f_gain, seconds)]):
            old = jnp.zeros(ref.shape, F32) if given is None else given[i][...]
            ref[...] = old if made is None else jnp.where(ours, jnp.concatenate(made, axis=1), old)

    x_gain[...] += firsts


def spread(place, block, before=None):
    dp, n, y = block.shape[:3]
    steps = dp * y
    put = lambda rows, width: pl.BlockSpec((1, 1, rows, width), lambda i, at: (i, at[0], 0, 0))
    sizes = [(128, 1024), (128, 512), (128, 512), (128, 1024)]
    widths = [1024, 1024, 512, 1024]
    small = [pl.BlockSpec((1, w), lambda i, at: (0, 0)) for w in widths]
    given = () if before is None else tuple(before)
    return pl.pallas_call(
        spread_kernel,
        grid_spec=pltpu.PrefetchScalarGridSpec(
            num_scalar_prefetch=1,
            grid=(steps,),
            in_specs=[pl.BlockSpec((1, n, 1, PART, 128), lambda i, at: (i // y, 0, i % y, 0, 0))]
            + ([pl.BlockSpec(memory_space=pl.ANY)] * 4 + small if given else []),
            out_specs=[put(*size) for size in sizes]
            + [pl.BlockSpec((8, 1024), lambda i, at: (i, 0))]
            + small,
        ),
        out_shape=[like((steps, 2) + size, F32) for size in sizes]
        + [like((8 * steps, 1024), F32)]
        + [like((1, w), F32) for w in widths],
        input_output_aliases={2 + i: i for i in range(4 if given else 0)},
        compiler_params=pltpu.CompilerParams(vmem_limit_bytes=56 * MIB),
        name="spread",
    )(place, block, *given)


def by_ctx(value):
    return lax.all_to_all(value, "ctx", split_axis=0, concat_axis=0, tiled=True)


def swap(value, axis, bit):
    n = lax.axis_size(axis)
    return lax.ppermute(value, axis, [(i, i ^ bit) for i in range(n)])


def swap_y(value):
    n = lax.axis_size("dp") * lax.axis_size("exp")
    return lax.ppermute(value, ("dp", "exp"), [(i, i ^ 6) for i in range(n)])


def held(value):
    return lax.optimization_barrier(value)


def across_chips(value):
    axes = ("dp", "ctx", "exp")
    dp, ctx, exp = (lax.axis_size(a) for a in axes)
    groups = [
        [(d * ctx + c) * exp + 2 * y + core for d in range(dp) for c in range(ctx) for y in range(exp // 2)]
        for core in range(2)
    ]
    return lax.all_to_all(
        value, axes, split_axis=0, concat_axis=0, tiled=True, axis_index_groups=groups
    )


def per_device(
    tokens,
    places,
    choices,
    cotangent,
    attn_gain,
    w_query,
    w_key,
    w_value,
    query_gain,
    key_gain,
    w_out,
    ffn_gain,
    w_router,
    w_gate,
    w_up,
    w_down,
):
    x_low = tokens[0]
    rows = x_low.shape[0]
    ctx = lax.axis_index("ctx")
    exp = lax.axis_index("exp")
    n_ctx = lax.axis_size("ctx")
    n_dp = lax.axis_size("dp")
    core = jnp.bitwise_and(exp, 1).astype(jnp.int32)
    picked = choices[0]
    g_low = cotangent[0]

    inv = places[0, ::RUN] // RUN
    runs = jnp.arange(inv.shape[0], dtype=jnp.int32)
    order = jnp.sum(jnp.where(inv[None, :] == runs[:, None], runs[None, :], 0), axis=1)
    table = jnp.asarray(turn_tables(places.shape[1]))

    chosen = jnp.any(picked[:, :, None] == jnp.arange(EXPERTS, dtype=jnp.int32), axis=1)
    tri = jnp.asarray(np.tril(np.ones((rows, rows), np.float32), -1), BF)
    slot = dot(tri, chosen.astype(BF))
    slot = jnp.where(chosen, slot, -1.0).astype(BF)
    column = np.arange(EXPERTS * CAP)
    named = (np.arange(EXPERTS)[:, None] == (column // CAP)[None, :]).astype(np.float32)
    at = dot(slot, jnp.asarray(named, BF))
    spot = (at == jnp.asarray(column % CAP, F32)[None, :]).astype(BF)

    send, first_low, first_turned, q_proj, k_proj = pre(
        x_low, attn_gain, w_query, w_key, w_value, query_gain, key_gain, picked.T
    )
    g_all = lax.all_gather(g_low, "ctx")
    recv = by_ctx(send)
    recv, spot = held((recv, spot))
    kv_all, q_all, att_all, lse_all, att_send = attend(order, inv, recv, table)
    att_send, w_gate, w_up, w_down = held((att_send, w_gate, w_up, w_down))
    down_blocks = w_down.reshape(2, 128, 8, 128).transpose(0, 2, 1, 3).reshape(2, 1024, 128)
    mine = held(jnp.concatenate([w_gate, w_up, down_blocks], axis=1))
    over_y = swap_y(mine)
    over_core = swap(mine, "exp", 1)
    heads = by_ctx(att_send)
    heads, mine, first_turned = held((heads, mine, first_turned))
    turned_all = lax.all_gather(first_turned, "ctx")
    over_both = swap(over_y, "exp", 1)
    router = w_router.T
    attended, middle, second_low, rows_send = middle_forward(heads, x_low, w_out, ffn_gain, spot)
    sent = by_ctx(rows_send.reshape(n_ctx, 2, CAP, -1))
    number = jnp.reshape(2 * ctx, (1,)).astype(jnp.int32)
    g_rows, slots = cotangent_rows(number, recv, g_all)
    sent, over_core, over_both, g_rows = held((sent, over_core, over_both, g_rows))
    parts = (mine, over_core, over_y, over_both)
    back = experts(number, sent, g_rows, router, parts)
    back = by_ctx(back).reshape(EXPERTS * CAP, -1)
    add = lambda *parts: sum(p.astype(F32) for p in parts).astype(BF)
    keep, near, far, out_part = weight_grads(number, sent, g_rows, router, slots, parts)
    back, near, keep, far, out_part, turned_all = held((back, near, keep, far, out_part, turned_all))
    out_part = lax.psum_scatter(out_part, "ctx", scatter_dimension=0, tiled=False)
    far = swap(far, "exp", 1)
    att_grad_send, grad_middle, branch = middle_back(
        spot, back, middle, second_low, router, ffn_gain, g_low, w_out
    )
    grad_recv = by_ctx(att_grad_send)
    even = 1 - jnp.bitwise_and(ctx, 1).astype(jnp.int32)
    place = jnp.stack([lax.axis_index("dp"), exp // 2, core, even]).astype(jnp.int32)
    out_mine, out_far = out_grads(place, attended, branch)
    near_a, near_b = (add(near[0, a], far[1, a]) for a in range(2))
    keep_a, keep_b = (add(keep[0, a], far[0, a]) for a in range(2))
    grad_recv, near_a, near_b, keep_a, keep_b, out_mine, out_far = held(
        (grad_recv, near_a, near_b, keep_a, keep_b, out_mine, out_far)
    )
    near_a = swap_y(near_a)
    near_b = swap_y(near_b)
    out_far = swap(out_far, "exp", 1)
    grad_send, kv_own = attend_back(
        order, inv, place[3:], grad_recv, kv_all, q_all, att_all, lse_all, table
    )
    kv_other = swap(kv_own, "ctx", 1)
    grad_send = join(grad_send, out_mine, out_far)
    grads = by_ctx(grad_send)
    keep_a = held(add(keep_a, near_a))
    dp_a = swap(keep_a, "dp", 1)
    keep_b = held(add(keep_b, near_b))
    dp_b = swap(keep_b, "dp", 1)
    grads, keep_a, keep_b, kv_other, dp_a = held((grads, keep_a, keep_b, kv_other, dp_a))
    own_gain = jnp.concatenate(
        [
            lax.dynamic_slice_in_dim(query_gain, ctx * HEAD_DIM, HEAD_DIM),
            lax.dynamic_slice_in_dim(key_gain, ctx // 2 * HEAD_DIM, HEAD_DIM),
        ]
    ).astype(F32)[None]
    shares = head_grads(
        place, turned_all, grad_send, kv_other, recv, grads, grad_recv, own_gain
    )
    shares, dp_b = held((shares, dp_b))
    shares = lax.all_to_all(shares, ("dp", "exp"), split_axis=0, concat_axis=0, tiled=True)
    input_grad, gain_part = input_back(
        grads, q_proj, k_proj, x_low, grad_middle, query_gain, key_gain, attn_gain, w_query, w_key, w_value
    )
    shares, gain_part, input_grad = held((shares, gain_part, input_grad))
    chips = n_dp * n_ctx * 2
    whole = across_chips(share_out(shares, gain_part, chips))
    sums = [k.astype(F32) + d.astype(F32) for k, d in ((keep_a, dp_a), (keep_b, dp_b))]
    grad_gate_w = jnp.stack([v[:1024] for v in sums])
    grad_up_w = jnp.stack([v[1024:2048] for v in sums])
    grad_down_w = jnp.stack(
        [v[2048:].reshape(8, 128, 128).transpose(1, 0, 2).reshape(128, 1024) for v in sums]
    )
    outputs = (middle + out_part.astype(F32)).astype(BF)
    whole, outputs, grad_gate_w, grad_up_w, grad_down_w = held(
        (whole, outputs, grad_gate_w, grad_up_w, grad_down_w)
    )
    other = swap(whole, "exp", 1)
    shape = (n_dp, n_ctx, 2, PART, 128)
    done = spread(jnp.reshape(core, (1,)), whole.reshape(shape))
    done = spread(jnp.reshape(1 - core, (1,)), other.reshape(shape), done[:4] + done[5:])
    wq, wk, wv, wo = (v.reshape(1024, -1) for v in done[:4])
    router_grad = done[4].T
    x_gain, q_gain, k_gain, f_gain = (v.reshape(-1) for v in done[5:])
    return (
        outputs[None],
        input_grad[None],
        x_gain,
        wq,
        wk,
        wv,
        q_gain,
        k_gain,
        wo,
        f_gain,
        router_grad,
        grad_gate_w,
        grad_up_w,
        grad_down_w,
    )


def solution(mesh):
    seqs = ("dp", "exp")
    row_spec = P(seqs, "ctx", None)
    in_specs = (row_spec, P(seqs, None), row_spec, row_spec) + (P(),) * 9
    in_specs += (P("ctx", None, "exp"), P("ctx", None, "exp"), P("ctx", "exp", None))
    out_specs = (row_spec, row_spec) + (P(),) * 9
    out_specs += (P("ctx", None, "exp"), P("ctx", None, "exp"), P("ctx", "exp", None))
    return jax.shard_map(
        per_device, mesh=mesh, in_specs=in_specs, out_specs=out_specs, check_vma=False
    )
```

```python
import jax
import jax.numpy as jnp
import numpy as np
from jax import lax
from jax.experimental import pallas as pl
from jax.experimental.pallas import tpu as pltpu
from jax.sharding import PartitionSpec as P

HEADS = 16
KV_HEADS = 8
HEAD_DIM = 64
EXPERTS = 32
CAP = 40
EPSILON = 1e-06
MASKED = -1e30
BF = jnp.bfloat16
F32 = jnp.float32
RUN = 64
QB = 512
QB_BACK = 256
PART = 208
BASE = 256
MIB = 1024 * 1024
NT = ((1,), (1,))
TN = ((0,), (0,))
VM = pl.BlockSpec(memory_space=pltpu.VMEM)
SM = pl.BlockSpec(memory_space=pltpu.SMEM)


def dot(a, b, dims=((1,), (0,))):
    return lax.dot_general(a, b, (dims, ((), ())), preferred_element_type=F32)


def call(kernel, outs, ins, name, flops, moved, scratch=(), transcendentals=0, vmem=62):
    return pl.pallas_call(
        kernel,
        out_shape=outs,
        in_specs=ins,
        out_specs=jax.tree.map(lambda _: VM, outs),
        scratch_shapes=list(scratch),
        compiler_params=pltpu.CompilerParams(vmem_limit_bytes=vmem * MIB),
        cost_estimate=pl.CostEstimate(
            flops=flops, bytes_accessed=moved, transcendentals=transcendentals
        ),
        name=name,
    )


def like(shape, dtype):
    return jax.ShapeDtypeStruct(shape, dtype)


def inverse_rms(value):
    return lax.rsqrt(jnp.mean(value * value, axis=-1, keepdims=True) + EPSILON)


def row_of(ref):
    return ref[...].astype(F32).reshape(1, -1)


def lanes_of(rows):
    return lax.broadcasted_iota(jnp.int32, (rows, 128), 1)


def swap_halves(tile):
    return pltpu.roll(tile.astype(F32), 64, 1)


def pack_head(wide, head):
    tile = wide[:, 128 * (head // 2) : 128 * (head // 2 + 1)]
    low = lanes_of(RUN) < 64
    if head % 2 == 0:
        return jnp.where(low, tile[:RUN], swap_halves(tile[RUN:]))
    return jnp.where(low, swap_halves(tile[:RUN]), tile[RUN:])


def unpack_heads(even, odd):
    low = lanes_of(RUN) < 64
    even, odd = even.astype(F32), odd.astype(F32)
    return jnp.concatenate(
        [jnp.where(low, even, swap_halves(odd)), jnp.where(low, swap_halves(even), odd)], axis=0
    )


def turn_tables(seq):
    half = HEAD_DIM // 2
    frequency = (10000.0 ** (-np.arange(half) * 2.0 / HEAD_DIM)).astype(np.float32)
    angles = (np.arange(seq, dtype=np.float32)[:, None] * frequency[None, :]).astype(np.float64)
    cosine, sine = np.cos(angles), np.sin(angles)
    return np.concatenate([cosine, cosine, -sine, sine], axis=1).astype(np.float32)


def split_table(table):
    low = lanes_of(table.shape[0]) < 64
    return jnp.where(low, table, 1.0), jnp.where(low, pltpu.roll(table, 64, 1), 0.0)


def turn(tile, cosine, sine):
    other = jnp.where(lanes_of(tile.shape[0]) < 32, pltpu.roll(tile, 96, 1), pltpu.roll(tile, 32, 1))
    return tile * cosine + other * sine


def pre_kernel(x_ref, gain, wq, wk, wv, q_gain, k_gain, picks, send, first_out, turned_out, q_out, k_out):
    x = x_ref[...].astype(F32)
    wide = x * inverse_rms(x) * row_of(gain)
    first = wide.astype(BF)
    first_out[...] = first
    q = dot(first, wq[...])
    k = dot(first, wk[...])
    v = dot(first, wv[...])
    q_out[...] = q
    k_out[...] = k
    qn = q * inverse_rms(q) * (row_of(q_gain) * HEAD_DIM ** (-0.5))
    kn = k * inverse_rms(k) * row_of(k_gain)
    low = lanes_of(x.shape[0]) < 64
    for h in range(KV_HEADS):
        cut = slice(128 * (h // 2), 128 * (h // 2 + 1))
        kt, vt = kn[:, cut], v[:, cut]
        if h % 2 == 0:
            both = jnp.where(low, kt, swap_halves(vt))
        else:
            both = jnp.where(low, swap_halves(kt), vt)
        both = both.astype(BF)
        send[2 * h, 0 : 2 * RUN, :] = both
        send[2 * h + 1, 0 : 2 * RUN, :] = both
    lane = lanes_of(x.shape[0])
    rows = jnp.transpose(jnp.where(lane == 0, inverse_rms(q), inverse_rms(k)))[0:2, :]
    high = rows.astype(BF).astype(F32)
    named = jnp.concatenate(
        [picks[...].astype(F32), high, rows - high, jnp.zeros((4, 128), F32)], axis=0
    ).astype(BF)
    for d in range(HEADS):
        send[d, 2 * RUN : 3 * RUN, :] = pack_head(qn, d).astype(BF)
        send[d, 3 * RUN : 3 * RUN + 16, :] = named
    turned_out[...] = jnp.transpose(first.astype(F32)).astype(BF)


def pre(x, gain, wq, wk, wv, q_gain, k_gain, picks):
    rows, width = x.shape
    return call(
        pre_kernel,
        (
            like((HEADS, 3 * RUN + 16, 128), BF),
            like((rows, width), BF),
            like((width, rows), BF),
            like((rows, wq.shape[1]), F32),
            like((rows, wk.shape[1]), F32),
        ),
        [VM] * 8,
        "pre",
        2 * rows * width * 2048,
        6 * 1024 * 1024,
    )(x, gain, wq, wk, wv, q_gain, k_gain, picks)


def turn_over(source, target):
    for i in range(source.shape[0] // 128):
        cut = slice(128 * i, 128 * (i + 1))
        target[:, cut] = jnp.transpose(source[cut, :].astype(F32)).astype(BF)


def masked_scores(kv, q, block):
    scores = dot(kv, q, NT)
    end = scores.shape[0]
    row = lax.broadcasted_iota(jnp.int32, (block, block), 0)
    col = lax.broadcasted_iota(jnp.int32, (block, block), 1)
    last = jnp.where(row <= col, scores[end - block :, :], MASKED)
    return last if end == block else jnp.concatenate([scores[: end - block, :], last], axis=0)


def attend_kernel(order, inv, recv, table, kv_out, q_out, att_out, lse_out, send_out, turned):
    seq = kv_out.shape[0]
    lane = lanes_of(RUN)

    def gather(b, carry):
        s = order[b]
        c = lax.shift_right_logical(s, 1)
        half = jnp.bitwise_and(s, 1)
        rows = pl.ds(pl.multiple_of(b * RUN, RUN), RUN)
        cos, sin = split_table(table[rows, :])
        kv = recv[c, pl.ds(pl.multiple_of(half * RUN, RUN), RUN), :].astype(F32)
        kv_out[rows, :] = turn(kv, cos, sin).astype(BF)
        tile = recv[c, pl.ds(2 * RUN, RUN), :].astype(F32)
        q = jnp.where(lane < 64, jnp.where(half == 0, tile, swap_halves(tile)), 0.0)
        q_out[rows, :] = turn(q, cos, sin).astype(BF)
        return carry

    lax.fori_loop(0, seq // RUN, gather, 0, unroll=32)
    turn_over(kv_out, turned)
    for i in range(seq // QB):
        here = slice(i * QB, (i + 1) * QB)
        end = (i + 1) * QB
        scores = masked_scores(kv_out[:end, :], q_out[here, :], QB)
        top = jnp.max(scores, axis=0, keepdims=True)
        weights = jnp.exp(scores - top)
        total = jnp.sum(weights, axis=0, keepdims=True)
        att = jnp.transpose(dot(turned[:, :end], weights.astype(BF)) / total)
        att_out[here, :] = att.astype(BF)
        lse_out[:, here] = jnp.broadcast_to(top + jnp.log(total), (8, QB))

    def place(c, carry):
        b0, b1 = inv[2 * c], inv[2 * c + 1]
        first = att_out[pl.ds(pl.multiple_of(b0 * RUN, RUN), RUN), :]
        second = att_out[pl.ds(pl.multiple_of(b1 * RUN, RUN), RUN), :]
        send_out[c] = jnp.where(lane < 64, swap_halves(first), second.astype(F32)).astype(BF)
        return carry

    lax.fori_loop(0, send_out.shape[0], place, 0, unroll=16)


def attend(order, inv, recv, table):
    n = recv.shape[0]
    seq = n * 128
    return call(
        attend_kernel,
        (
            like((seq, 128), BF),
            like((seq, 128), BF),
            like((seq, 128), BF),
            like((8, seq), F32),
            like((n, RUN, 128), BF),
        ),
        [SM, SM, VM, VM],
        "attend",
        4 * seq * seq * 128 // 2,
        14 * seq * 128,
        [pltpu.VMEM((128, seq), BF)],
        transcendentals=seq * seq // 2,
    )(order, inv, recv, table)


def attend_back_kernel(
    order, inv, even, recv, kv_in, q_in, att_in, lse_in, table,
    send_hbm, kv_grad_out, g_all, dq_all, dkv_all, sums, turned, send_out, sem,
):
    seq = kv_in.shape[0]
    lane = lanes_of(RUN)

    def gather(b, carry):
        s = order[b]
        c = lax.shift_right_logical(s, 1)
        half = jnp.bitwise_and(s, 1)
        tile = recv[c, 0:RUN, :].astype(F32)
        g_all[pl.ds(pl.multiple_of(b * RUN, RUN), RUN), :] = jnp.where(
            lane >= 64, jnp.where(half == 1, tile, swap_halves(tile)), 0.0
        ).astype(BF)
        return carry

    lax.fori_loop(0, seq // RUN, gather, 0, unroll=32)
    turn_over(kv_in, turned)
    steps = seq // QB_BACK
    for i in reversed(range(steps)):
        here = slice(i * QB_BACK, (i + 1) * QB_BACK)
        end = (i + 1) * QB_BACK
        kv, q, g = kv_in[:end, :], q_in[here, :], g_all[here, :]
        offset = jnp.sum(jnp.transpose(att_in[here, :].astype(F32) * g.astype(F32)), axis=0, keepdims=True)
        weights = jnp.exp(masked_scores(kv, q, QB_BACK) - lse_in[0:1, here])
        grad_scores = (weights * (dot(kv, g, NT) - offset)).astype(BF)
        dq_all[here, :] = jnp.transpose(dot(turned[:, :end], grad_scores))
        step = dot(grad_scores, q) + dot(weights.astype(BF), g)
        if i == steps - 1:
            dkv_all[...] = step
        else:
            dkv_all[:end, :] += step

    def place(c, carry):
        b0, b1 = inv[2 * c], inv[2 * c + 1]
        r0 = pl.ds(pl.multiple_of(b0 * RUN, RUN), RUN)
        r1 = pl.ds(pl.multiple_of(b1 * RUN, RUN), RUN)
        cos0, sin0 = split_table(table[r0, :])
        cos1, sin1 = split_table(table[r1, :])
        kv0 = turn(dkv_all[r0, :], cos0, -sin0).astype(BF)
        kv1 = turn(dkv_all[r1, :], cos1, -sin1).astype(BF)
        send_out[c, 0 : RUN, :] = kv0
        send_out[c, RUN : 2 * RUN, :] = kv1
        kv0, kv1 = kv0.astype(F32), kv1.astype(F32)
        values = jnp.where(lane < 64, swap_halves(kv0), kv1)
        keys = jnp.where(lane < 64, kv0, swap_halves(kv1))
        kv_grad_out[c] = jnp.where(even[0] == 1, values, keys).astype(BF)
        both_q = jnp.concatenate([dq_all[r0, :], dq_all[r1, :]], axis=0)
        both_q = both_q * jnp.concatenate([q_in[r0, :], q_in[r1, :]], axis=0).astype(F32)
        both_k = jnp.concatenate([dkv_all[r0, :], dkv_all[r1, :]], axis=0)
        both_k = both_k * jnp.concatenate([kv_in[r0, :], kv_in[r1, :]], axis=0).astype(F32)
        some = jnp.where(lanes_of(8) < 64, 1.0, 0.0).astype(BF)
        sums[pl.ds(c, 1), :] = dot(some, both_q.astype(BF), NT)[0:1, :]
        sums[pl.ds(n + c, 1), :] = dot(some, both_k.astype(BF), NT)[0:1, :]
        q0 = turn(dq_all[r0, :], cos0, -sin0)
        q1 = turn(dq_all[r1, :], cos1, -sin1)
        both = jnp.where(lane < 64, q0, swap_halves(q1))
        send_out[c, 2 * RUN : 3 * RUN, :] = (both * HEAD_DIM ** (-0.5)).astype(BF)
        return carry

    n = send_out.shape[0]
    lax.fori_loop(0, n, place, 0, unroll=16)
    for c in range(n):
        send_out[c, 3 * RUN : 3 * RUN + 2 * n, :] = sums[...].astype(BF)
    copy = pltpu.make_async_copy(send_out, send_hbm.at[:, pl.ds(BASE, 3 * RUN + 2 * n), :], sem)
    copy.start()
    copy.wait()


def attend_back(order, inv, even, recv, kv, q, att, lse, table):
    n = recv.shape[0]
    seq = n * 128
    whole = lambda v: pl.BlockSpec(v.shape, lambda i: (0,) * v.ndim)
    return pl.pallas_call(
        attend_back_kernel,
        grid=(1,),
        out_shape=(like((n, BASE + 3 * RUN + 2 * n, 128), BF), like((n, RUN, 128), BF)),
        in_specs=[SM, SM, SM] + [whole(v) for v in (recv, kv, q, att, lse, table)],
        out_specs=(
            pl.BlockSpec(memory_space=pl.ANY),
            pl.BlockSpec((n, RUN, 128), lambda i: (0, 0, 0)),
        ),
        scratch_shapes=[
            pltpu.VMEM((seq, 128), BF),
            pltpu.VMEM((seq, 128), F32),
            pltpu.VMEM((seq, 128), F32),
            pltpu.VMEM((2 * n, 128), F32),
            pltpu.VMEM((128, seq), BF),
            pltpu.VMEM((n, 3 * RUN + 2 * n, 128), BF),
            pltpu.SemaphoreType.DMA,
        ],
        compiler_params=pltpu.CompilerParams(vmem_limit_bytes=62 * MIB),
        cost_estimate=pl.CostEstimate(
            flops=10 * seq * seq * 128 // 2, bytes_accessed=20 * seq * 128, transcendentals=seq * seq // 2
        ),
        name="attend_back",
    )(order, inv, even, recv, kv, q, att, lse, table)


def join_kernel(send, mine, far, out_ref):
    for c in range(out_ref.shape[0]):
        for j in range(4):
            rows = slice(8 * c, 8 * c + 8)
            both = mine[j, rows, :].astype(F32) + far[j, rows, :].astype(F32)
            for m in range(0, 8, 2):
                at = 64 * j + 8 * m
                pair = (both[:, 128 * m : 128 * m + 128], both[:, 128 * m + 128 : 128 * m + 256])
                out_ref[c, at : at + 16, :] = jnp.concatenate(pair, axis=0).astype(BF)


def join(send, mine, far):
    whole = pl.BlockSpec(mine.shape, lambda i: (0, 0, 0))
    return pl.pallas_call(
        join_kernel,
        grid=(1,),
        out_shape=like(send.shape, BF),
        in_specs=[pl.BlockSpec(memory_space=pl.ANY), whole, whole],
        out_specs=pl.BlockSpec((send.shape[0], BASE, 128), lambda i: (0, 0, 0)),
        input_output_aliases={0: 0},
        compiler_params=pltpu.CompilerParams(vmem_limit_bytes=62 * MIB),
        cost_estimate=pl.CostEstimate(flops=1 << 20, bytes_accessed=1 << 20, transcendentals=0),
        name="join",
    )(send, mine, far)


def slot_masks(slot, pair):
    line = lax.broadcasted_iota(jnp.int32, (2 * CAP, 128), 0).astype(F32)
    left = (line < CAP) & (line == slot[2 * pair : 2 * pair + 1, :])
    right = (line >= CAP) & (line - CAP == slot[2 * pair + 1 : 2 * pair + 2, :])
    return jnp.where(left, 1.0, 0.0).astype(BF), jnp.where(right, 1.0, 0.0).astype(BF)


def cotangent_kernel(number, picks_ref, g_ref, rows_ref, slot_ref):
    n_ctx = g_ref.shape[0]
    picks = picks_ref[...].astype(F32)[:, :8, :]
    before = lax.broadcasted_iota(jnp.int32, (128, 128), 0) < lax.broadcasted_iota(
        jnp.int32, (128, 128), 1
    )
    before = jnp.where(before, 1.0, 0.0).astype(BF)
    for a in range(2):
        e = (number[0] + a).astype(F32)
        named = jnp.max(jnp.where(picks == e, 1.0, 0.0), axis=1)
        slot = jnp.where(named > 0.0, dot(named.astype(BF), before), -1.0)
        slot_ref[a] = slot
        for p in range(n_ctx // 2):
            left, right = slot_masks(slot, p)
            rows_ref[a, 2 * CAP * p : 2 * CAP * (p + 1), :] = (
                dot(left, g_ref[2 * p]) + dot(right, g_ref[2 * p + 1])
            ).astype(BF)


def cotangent_rows(number, recv, g_all):
    n_ctx = g_all.shape[0]
    whole = lambda *shape: pl.BlockSpec(shape, lambda i: (0,) * len(shape))
    return pl.pallas_call(
        cotangent_kernel,
        grid=(1,),
        out_shape=(like((2, n_ctx * CAP, 1024), BF), like((2, n_ctx, 128), F32)),
        in_specs=[
            SM,
            pl.BlockSpec((n_ctx, 16, 128), lambda i: (0, 3 * RUN // 16, 0)),
            whole(*g_all.shape),
        ],
        out_specs=(whole(2, n_ctx * CAP, 1024), whole(2, n_ctx, 128)),
        compiler_params=pltpu.CompilerParams(vmem_limit_bytes=62 * MIB),
        cost_estimate=pl.CostEstimate(
            flops=8 * n_ctx * 80 * 128 * 1024, bytes_accessed=8 * 1024 * 1024, transcendentals=0
        ),
        name="cotangent_rows",
    )(number, recv, g_all)


def expert_steps(e, rows_ref, g_ref, router_ref, parts):
    n_ctx = rows_ref.shape[0]
    rows = jnp.concatenate([rows_ref[c, 0].astype(F32) for c in range(n_ctx)], axis=0).astype(BF)
    grads = g_ref[0].astype(F32)
    logits = dot(rows, router_ref[...], NT)
    lane = lax.broadcasted_iota(jnp.int32, logits.shape, 1)
    powers = jnp.exp(logits - jnp.max(logits, axis=1, keepdims=True))
    gate = jnp.sum(jnp.where(lane == e, powers, 0.0), axis=1, keepdims=True) / jnp.sum(
        powers, axis=1, keepdims=True
    )
    w_gate = jnp.concatenate([w[0, 0:1024, :] for w in parts], axis=1)
    w_up = jnp.concatenate([w[0, 1024:2048, :] for w in parts], axis=1)
    w_down = jnp.concatenate(
        [
            jnp.concatenate([w[0, 2048 + 128 * n : 2176 + 128 * n, :] for n in range(8)], axis=1)
            for w in parts
        ],
        axis=0,
    )
    gate_act = dot(rows, w_gate)
    up_act = dot(rows, w_up)
    sig = 1.0 / (1.0 + jnp.exp(-gate_act))
    silu = gate_act * sig
    hidden = (silu * up_act).astype(BF)
    expert_out = dot(hidden, w_down)
    grad_rows = (gate * grads).astype(BF)
    grad_hidden = dot(grad_rows, w_down, NT)
    ga = (grad_hidden * up_act * sig * (1.0 + gate_act * (1.0 - sig))).astype(BF)
    gu = (grad_hidden * silu).astype(BF)
    return rows, grads, gate, w_gate, w_up, hidden, expert_out, grad_rows, ga, gu


def expert_kernel(number, rows_ref, g_ref, router_ref, *refs):
    parts, back_ref = refs[:4], refs[4]
    e = number[0] + pl.program_id(0)
    rows, grads, _, w_gate, w_up, _, expert_out, _, ga, gu = expert_steps(
        e, rows_ref, g_ref, router_ref, parts
    )
    grad_gate = jnp.sum(grads * expert_out, axis=1, keepdims=True)
    back = dot(ga, w_gate, NT) + dot(gu, w_up, NT)
    high = grad_gate.astype(BF).astype(F32)
    lane = lanes_of(rows.shape[0])
    tail = jnp.where(lane == e, high, jnp.where(lane == e + EXPERTS, grad_gate - high, 0.0))
    for c in range(rows_ref.shape[0]):
        cut = slice(CAP * c, CAP * (c + 1))
        back_ref[c, 0, :, 0:1024] = back[cut, :].astype(BF)
        back_ref[c, 0, :, 1024:1152] = tail[cut, :].astype(BF)


def weight_grad_kernel(number, rows_ref, g_ref, router_ref, slot_ref, *refs):
    parts, (keep, near, far, sums_ref) = refs[:4], refs[4:]
    e = number[0] + pl.program_id(0)
    rows, _, gate, _, _, hidden, expert_out, grad_rows, ga, gu = expert_steps(
        e, rows_ref, g_ref, router_ref, parts
    )
    line = lax.broadcasted_iota(jnp.int32, (CAP, 128), 0).astype(F32)
    first = pl.program_id(0) == 0
    out_rows = gate * expert_out
    for c in range(rows_ref.shape[0]):
        mask = jnp.where(line == slot_ref[0, c : c + 1, :], 1.0, 0.0).astype(BF)
        part = dot(mask, out_rows[CAP * c : CAP * (c + 1), :].astype(BF), TN)
        before = jnp.where(first, 0.0, sums_ref[c].astype(F32))
        sums_ref[c] = (part + before).astype(BF)
    gate_grad = dot(rows, ga, TN)
    up_grad = dot(rows, gu, TN)
    down_grad = dot(hidden, grad_rows, TN)
    for j, (ref, at) in enumerate([(keep, 0), (far, 0), (near, 0), (far, 1)]):
        cut = slice(128 * j, 128 * (j + 1))
        ref[at, 0, 0:1024, :] = gate_grad[:, cut].astype(BF)
        ref[at, 0, 1024:2048, :] = up_grad[:, cut].astype(BF)
        for n in range(8):
            ref[at, 0, 2048 + 128 * n : 2176 + 128 * n, :] = down_grad[
                cut, 128 * n : 128 * (n + 1)
            ].astype(BF)


def expert_call(kernel, name, number, rows, grads, router, slots, parts, outs, out_specs):
    n_ctx = rows.shape[0]
    n = n_ctx * CAP
    extra = () if slots is None else (slots,)
    return pl.pallas_call(
        kernel,
        grid=(2,),
        out_shape=outs,
        in_specs=[
            SM,
            pl.BlockSpec((n_ctx, 1, CAP, 1024), lambda i: (0, i, 0, 0)),
            pl.BlockSpec((1, n, 1024), lambda i: (i, 0, 0)),
            pl.BlockSpec(router.shape, lambda i: (0, 0)),
        ]
        + [pl.BlockSpec((1,) + v.shape[1:], lambda i: (i, 0, 0)) for v in extra + tuple(parts)],
        out_specs=out_specs,
        compiler_params=pltpu.CompilerParams(vmem_limit_bytes=62 * MIB),
        cost_estimate=pl.CostEstimate(
            flops=24 * n * 1024 * 512, bytes_accessed=20 * 1024 * 1024, transcendentals=2 * n * 512
        ),
        name=name,
    )(number, rows, grads, router, *extra, *parts)


def experts(number, rows, grads, router, parts):
    n_ctx = rows.shape[0]
    return expert_call(
        expert_kernel, "experts", number, rows, grads, router, None, parts,
        like((n_ctx, 2, CAP, 1152), BF),
        pl.BlockSpec((n_ctx, 1, CAP, 1152), lambda i: (0, i, 0, 0)),
    )


def weight_grads(number, rows, grads, router, slots, parts):
    n_ctx = rows.shape[0]
    put = lambda k: pl.BlockSpec((k, 1, 3072, 128), lambda i: (0, i, 0, 0))
    return expert_call(
        weight_grad_kernel, "weight_grads", number, rows, grads, router, slots, parts,
        (
            like((1, 2, 3072, 128), BF),
            like((1, 2, 3072, 128), BF),
            like((2, 2, 3072, 128), BF),
            like((n_ctx, 128, 1024), BF),
        ),
        (put(1), put(1), put(2), pl.BlockSpec((n_ctx, 128, 1024), lambda i: (0, 0, 0))),
    )


def middle_kernel(heads, x_ref, w_out, gain, spot, attended_out, middle_out, second_out, send_out):
    attended = jnp.concatenate(
        [unpack_heads(heads[2 * t], heads[2 * t + 1]) for t in range(HEADS // 2)], axis=1
    ).astype(BF)
    attended_out[...] = attended
    middle = x_ref[...].astype(F32) + dot(attended, w_out[...])
    middle_out[...] = middle
    second = (middle * inverse_rms(middle) * row_of(gain)).astype(BF)
    second_out[...] = second
    send_out[...] = dot(spot[...], second, TN).astype(BF)


def middle_forward(heads, x, w_out, gain, spot):
    rows, width = x.shape
    return call(
        middle_kernel,
        (
            like((rows, width), BF),
            like((rows, width), F32),
            like((rows, width), BF),
            like((spot.shape[1], width), BF),
        ),
        [VM] * 5,
        "middle",
        2 * rows * width * (1024 + 1280),
        6 * 1024 * 1024,
    )(heads, x, w_out, gain, spot)


def middle_back_kernel(
    spot, back, middle_ref, second, router, gain, g_ref, w_out,
    send, grad_out, branch_out,
):
    summed = dot(spot[...], back[...])
    logits = dot(second[...], router[...], NT)
    powers = jnp.exp(logits - jnp.max(logits, axis=1, keepdims=True))
    probs = powers / jnp.sum(powers, axis=1, keepdims=True)
    last = summed[:, 1024:1152]
    grad_sel = (last + pltpu.roll(last, 128 - EXPERTS, 1))[:, :EXPERTS]
    grad_logits = probs * (grad_sel - jnp.sum(probs * grad_sel, axis=1, keepdims=True))
    high = grad_logits.astype(BF)
    rest = (grad_logits - high.astype(F32)).astype(BF)
    upstream = summed[:, :1024] + dot(high, router[...]) + dot(rest, router[...])
    middle = middle_ref[...]
    r = inverse_rms(middle)
    hat = middle * r
    gain_part = jnp.sum(upstream * hat, axis=0, keepdims=True)
    router_part = dot(high, second[...], TN) + dot(rest, second[...], TN)
    low = lanes_of(EXPERTS) < 64
    first_row = lax.broadcasted_iota(jnp.int32, (EXPERTS, 128), 0) == 0
    for d in range(HEADS):
        cut = slice(128 * (d // 2), 128 * (d // 2 + 1))
        tile = router_part[:, cut]
        part = jnp.where(first_row, jnp.broadcast_to(gain_part[:, cut], (EXPERTS, 128)), 0.0)
        if d % 2 == 0:
            misc = jnp.where(low, tile, swap_halves(part))
        else:
            misc = jnp.where(low, swap_halves(tile), part)
        send[d, RUN : RUN + EXPERTS, :] = misc.astype(BF)
    scaled = upstream * row_of(gain)
    grad = (
        r * (scaled - hat * jnp.mean(scaled * hat, axis=1, keepdims=True)) + g_ref[...].astype(F32)
    )
    grad_out[...] = grad
    branch = grad.astype(BF)
    branch_out[...] = branch
    att = dot(branch, w_out[...], NT)
    for d in range(HEADS):
        send[d, 0:RUN, :] = pack_head(att, d).astype(BF)


def middle_back(spot, back, middle, second, router, gain, g_low, w_out):
    rows, width = middle.shape
    return call(
        middle_back_kernel,
        (
            like((HEADS, RUN + EXPERTS, 128), BF),
            like((rows, width), F32),
            like((rows, width), BF),
        ),
        [VM] * 8,
        "middle_back",
        2 * rows * width * (1280 + 1024),
        6 * 1024 * 1024,
    )(spot, back, middle, second, router, gain, g_low, w_out)


def out_grad_kernel(place, attended, branch, mine, far):
    for j in range(8):
        c, y, d = j // 4, j // 2 % 2, j % 2
        block = (
            jnp.bitwise_xor(place[0], d) * 4 + jnp.bitwise_xor(place[1], y) * 2 + jnp.bitwise_xor(place[2], c)
        )
        part = attended[:, pl.ds(pl.multiple_of(block * 128, 128), 128)]
        (far if c else mine)[j % 4] = dot(part, branch[...], TN).astype(BF)


def out_grads(place, attended, branch):
    return call(
        out_grad_kernel,
        (like((4, 128, 1024), BF), like((4, 128, 1024), BF)),
        [SM, VM, VM],
        "out_grads",
        1 << 20,
        1 << 18,
    )(place, attended, branch)


def queries_of(recv):
    return jnp.concatenate(
        [
            unpack_heads(
                recv[2 * t, BASE + 2 * RUN : BASE + 3 * RUN, :],
                recv[2 * t + 1, BASE + 2 * RUN : BASE + 3 * RUN, :],
            )
            for t in range(HEADS // 2)
        ],
        axis=1,
    )


def keys_values_of(recv):
    low = lanes_of(2 * RUN) < 64
    both = [
        recv[2 * j, BASE : BASE + 2 * RUN, :].astype(F32)
        + recv[2 * j + 1, BASE : BASE + 2 * RUN, :].astype(F32)
        for j in range(KV_HEADS)
    ]
    keys, values = [], []
    for t in range(KV_HEADS // 2):
        keys.append(jnp.where(low, both[2 * t], swap_halves(both[2 * t + 1])))
        values.append(jnp.where(low, swap_halves(both[2 * t]), both[2 * t + 1]))
    return jnp.concatenate(keys, axis=1), jnp.concatenate(values, axis=1)


def input_kernel(
    recv, q_ref, k_ref, x_ref, middle, q_gain, k_gain, gain, wq, wk, wv, out_ref, gain_ref
):
    uq = queries_of(recv)
    uk, dv = keys_values_of(recv)
    q, k = q_ref[...], k_ref[...]
    rq, rk = inverse_rms(q), inverse_rms(k)
    qh, kh = q * rq, k * rk
    uq, uk = uq * row_of(q_gain), uk * row_of(k_gain)
    gq = (rq * (uq - qh * jnp.mean(uq * qh, axis=1, keepdims=True))).astype(BF)
    gk = (rk * (uk - kh * jnp.mean(uk * kh, axis=1, keepdims=True))).astype(BF)
    upstream = dot(gq, wq[...], NT) + dot(gk, wk[...], NT) + dot(dv.astype(BF), wv[...], NT)
    x = x_ref[...].astype(F32)
    r = inverse_rms(x)
    hat = x * r
    x_part = jnp.sum(upstream * hat, axis=0, keepdims=True)
    scaled = upstream * row_of(gain)
    out_ref[...] = middle[...] + r * (scaled - hat * jnp.mean(scaled * hat, axis=1, keepdims=True))
    half = jnp.zeros((1, 64), F32)
    rows = [jnp.concatenate([half, x_part[:, 64 * i : 64 * (i + 1)]], axis=1) for i in range(8)]
    none = jnp.zeros((2, 128), F32)
    more = [x_part[:, 512 + 128 * i : 640 + 128 * i] for i in range(4)]
    gain_ref[...] = jnp.concatenate(rows + [none] + more + [none], axis=0)


def input_back(recv, q, k, x, middle, q_gain, k_gain, gain, wq, wk, wv):
    rows, width = x.shape
    return call(
        input_kernel,
        (like((rows, width), F32), like((16, 128), F32)),
        [VM] * 11,
        "input_back",
        2 * rows * width * 2048,
        8 * 1024 * 1024,
    )(recv, q, k, x, middle, q_gain, k_gain, gain, wq, wk, wv)


def head_grad_kernel(
    place, turned, early, later, queries, kv_other, normed, out_parts, sums_ref, branch, gain_ref, out_ref
):
    n = early.shape[0]
    low = lanes_of(128) < 64
    gain = gain_ref[...]
    sums = sums_ref[0].astype(F32)
    others = branch[0].astype(F32)
    for c in range(1, n):
        sums = sums + sums_ref[c].astype(F32)
        others = others + branch[c].astype(F32)
    out_rows = out_parts[0].astype(F32)
    for c in range(1, n):
        out_rows = out_rows + out_parts[c].astype(F32)
    q_means = sums[0:n, :] / (HEADS * HEAD_DIM)
    k_means = sums[n : 2 * n, :] / (KV_HEADS * HEAD_DIM)
    total = None
    gains = None
    for p in range(n // 2):
        parts = []
        for c in (2 * p, 2 * p + 1):
            packed = queries[c].astype(F32)
            uq = jnp.concatenate([packed, swap_halves(packed)], axis=0)
            both = jnp.concatenate([early[c].astype(F32), later[c].astype(F32)], axis=0)
            other = kv_other[c].astype(F32)
            other = jnp.concatenate([swap_halves(other), other], axis=0)
            keys = swap_halves(both) + other
            upstream = jnp.where(low, uq, keys)
            packed = normed[c, 2 * RUN : 3 * RUN, :].astype(F32)
            qn = jnp.concatenate([packed, swap_halves(packed)], axis=0) * HEAD_DIM**0.5
            hat = jnp.where(low, qn, swap_halves(normed[c, 0 : 2 * RUN, :])) / gain
            factors = normed[c, 3 * RUN : 3 * RUN + 16, :].astype(F32)
            factors = factors[8:10, :] + factors[10:12, :]
            rows = jnp.concatenate(
                [factors, q_means[c : c + 1, :], k_means[c : c + 1, :], jnp.zeros((4, 128), F32)], axis=0
            )
            cols = jnp.transpose(jnp.concatenate([rows] * 16, axis=0))
            r = jnp.where(low, cols[:, 0:1], cols[:, 1:2])
            m = jnp.where(low, cols[:, 2:3], cols[:, 3:4])
            grad = r * (upstream * gain - hat * m)
            part = jnp.sum(upstream * hat, axis=0, keepdims=True)
            gains = part if gains is None else gains + part
            parts.append(jnp.where(low | (place[3] == 1), grad, both + other).astype(BF))
        left = jnp.concatenate([turned[2 * p], turned[2 * p + 1]], axis=1)
        step = dot(left, jnp.concatenate(parts, axis=0))
        total = step if total is None else total + step
    low_row = low[0:1, :]
    gains = jnp.where(low_row | (place[3] == 1), gains, 0.0)
    ffn = jnp.where(low_row, swap_halves(others[0:8, :])[0:1, :], 0.0)
    rows = jnp.concatenate([gains, ffn, jnp.zeros((6, 128), F32)], axis=0)
    some = lanes_of(8) < 64
    for s in range(8):
        out_ref[s, 0:128, :] = total[128 * s : 128 * (s + 1), :].astype(BF)
        kept = jnp.where(some, others[8 * (s // 2) : 8 * (s // 2) + 8, :], 0.0)
        out_ref[s, 128:144, :] = jnp.concatenate(
            [kept, rows if s == 0 else jnp.zeros((8, 128), F32)], axis=0
        ).astype(BF)
        out_ref[s, 144:PART, :] = jnp.zeros((64, 128), BF)
    for j in range(4):
        at = jnp.bitwise_xor(place[0], j % 2) * 4 + jnp.bitwise_xor(place[1], j // 2) * 2 + place[2]
        out_ref[pl.ds(at, 1), 144:PART, :] = out_rows[64 * j : 64 * j + 64, :].astype(BF)[None]


def head_grads(place, turned, own, kv_other, normed, grads, branch, gain):
    whole = lambda v: pl.BlockSpec(v.shape, lambda i: (0,) * v.ndim)
    n = own.shape[0]
    part = lambda rows, at: pl.BlockSpec((n, rows, 128), lambda i: (0, at // rows, 0))
    return pl.pallas_call(
        head_grad_kernel,
        grid=(1,),
        out_shape=like((8, PART, 128), BF),
        in_specs=[
            SM,
            whole(turned),
            part(RUN, BASE),
            part(RUN, BASE + RUN),
            part(RUN, BASE + 2 * RUN),
            whole(kv_other),
            whole(normed),
            part(BASE, 0),
            part(2 * n, BASE + 3 * RUN),
            part(EXPERTS, RUN),
            whole(gain),
        ],
        out_specs=pl.BlockSpec((8, PART, 128), lambda i: (0, 0, 0)),
        compiler_params=pltpu.CompilerParams(vmem_limit_bytes=62 * MIB),
        cost_estimate=pl.CostEstimate(
            flops=2 * 2048 * 1024 * 128, bytes_accessed=8 * 1024 * 1024, transcendentals=0
        ),
        name="head_grads",
    )(place, turned, own, own, own, kv_other, normed, grads, grads, branch, gain)


def share_kernel(shares, gain_ref, out_ref):
    total = shares[0].astype(F32)
    for s in range(1, shares.shape[0]):
        total = total + shares[s].astype(F32)
    total = jnp.concatenate([total[0:128], total[128:144] + gain_ref[...], total[144:PART]], axis=0)
    total = total.astype(BF)
    for c in range(out_ref.shape[0]):
        out_ref[c] = total


def share_out(shares, gain, chips):
    return call(
        share_kernel,
        like((chips, PART, 128), BF),
        [VM, VM],
        "share_out",
        1 << 18,
        4 * 1024 * 1024,
    )(shares, gain)


def spread_kernel(place, block_ref, *refs):
    wq, wk, wv, wo, router, x_gain, q_gain, k_gain, f_gain = refs[-9:]
    n = block_ref.shape[1]
    low = lanes_of(128) < 64
    some = lanes_of(8) < 64
    total = None
    kept = None
    queries, keys, seconds = [], [], []
    for c in range(0, n, 2):
        even, odd = block_ref[0, c, 0].astype(F32), block_ref[0, c + 1, 0].astype(F32)
        wide = slice(64 * c, 64 * c + 128)
        wq[0, 0, :, wide] = jnp.where(low, even[:128], swap_halves(odd[:128]))
        key, value = even[:128], odd[:128]
        if c % 4 == 0:
            kept = (swap_halves(key), swap_halves(value))
        else:
            half = slice(32 * c - 64, 32 * c + 64)
            wk[0, 0, :, half] = jnp.where(low, kept[0], key)
            wv[0, 0, :, half] = jnp.where(low, kept[1], value)
        router[:, wide] = jnp.where(some, even[128:136], swap_halves(odd[128:136]))
        sums = even[128:144] + odd[128:144]
        total = sums if total is None else total + sums
        pairs = jnp.where(some, even[136:144], swap_halves(odd[136:144]))
        queries.append(pairs[0:1])
        seconds.append(pairs[1:2])
        if c % 4 == 0:
            key_gain = swap_halves(even[136:144])
        else:
            keys.append(jnp.where(some, key_gain, even[136:144])[0:1])
        for d, block in ((c, even), (c + 1, odd)):
            for m in range(8):
                wo[0, 0, 8 * d : 8 * d + 8, 128 * m : 128 * (m + 1)] = block[144 + 8 * m : 152 + 8 * m]
    turned = swap_halves(total)
    firsts = [
        jnp.where(some[0:1], turned[2 * t : 2 * t + 1], total[2 * t + 1 : 2 * t + 2]) for t in range(4)
    ]
    firsts = jnp.concatenate(firsts + [total[10 + t : 11 + t] for t in range(4)], axis=1)

    @pl.when(pl.program_id(0) == 0)
    def _():
        ours = place[0] == 0
        given = refs[4:8] if len(refs) > 9 else None
        for i, (ref, made) in enumerate([(x_gain, None), (q_gain, queries), (k_gain, keys), (f_gain, seconds)]):
            old = jnp.zeros(ref.shape, F32) if given is None else given[i][...]
            ref[...] = old if made is None else jnp.where(ours, jnp.concatenate(made, axis=1), old)

    x_gain[...] += firsts


def spread(place, block, before=None):
    dp, n, y = block.shape[:3]
    steps = dp * y
    put = lambda rows, width: pl.BlockSpec((1, 1, rows, width), lambda i, at: (i, at[0], 0, 0))
    sizes = [(128, 1024), (128, 512), (128, 512), (128, 1024)]
    widths = [1024, 1024, 512, 1024]
    small = [pl.BlockSpec((1, w), lambda i, at: (0, 0)) for w in widths]
    given = () if before is None else tuple(before)
    return pl.pallas_call(
        spread_kernel,
        grid_spec=pltpu.PrefetchScalarGridSpec(
            num_scalar_prefetch=1,
            grid=(steps,),
            in_specs=[pl.BlockSpec((1, n, 1, PART, 128), lambda i, at: (i // y, 0, i % y, 0, 0))]
            + ([pl.BlockSpec(memory_space=pl.ANY)] * 4 + small if given else []),
            out_specs=[put(*size) for size in sizes]
            + [pl.BlockSpec((8, 1024), lambda i, at: (i, 0))]
            + small,
        ),
        out_shape=[like((steps, 2) + size, F32) for size in sizes]
        + [like((8 * steps, 1024), F32)]
        + [like((1, w), F32) for w in widths],
        input_output_aliases={2 + i: i for i in range(4 if given else 0)},
        compiler_params=pltpu.CompilerParams(vmem_limit_bytes=62 * MIB),
        name="spread",
    )(place, block, *given)


def by_ctx(value):
    return lax.all_to_all(value, "ctx", split_axis=0, concat_axis=0, tiled=True)


def swap(value, axis, bit):
    n = lax.axis_size(axis)
    return lax.ppermute(value, axis, [(i, i ^ bit) for i in range(n)])


def swap_y(value):
    n = lax.axis_size("dp") * lax.axis_size("exp")
    return lax.ppermute(value, ("dp", "exp"), [(i, i ^ 6) for i in range(n)])


def held(value):
    return lax.optimization_barrier(value)


def across_chips(value):
    axes = ("dp", "ctx", "exp")
    dp, ctx, exp = (lax.axis_size(a) for a in axes)
    groups = [
        [(d * ctx + c) * exp + 2 * y + core for d in range(dp) for c in range(ctx) for y in range(exp // 2)]
        for core in range(2)
    ]
    return lax.all_to_all(
        value, axes, split_axis=0, concat_axis=0, tiled=True, axis_index_groups=groups
    )


def per_device(
    tokens,
    places,
    choices,
    cotangent,
    attn_gain,
    w_query,
    w_key,
    w_value,
    query_gain,
    key_gain,
    w_out,
    ffn_gain,
    w_router,
    w_gate,
    w_up,
    w_down,
):
    x_low = tokens[0]
    rows = x_low.shape[0]
    ctx = lax.axis_index("ctx")
    exp = lax.axis_index("exp")
    n_ctx = lax.axis_size("ctx")
    n_dp = lax.axis_size("dp")
    core = jnp.bitwise_and(exp, 1).astype(jnp.int32)
    picked = choices[0]
    g_low = cotangent[0]

    inv = places[0, ::RUN] // RUN
    runs = jnp.arange(inv.shape[0], dtype=jnp.int32)
    order = jnp.sum(jnp.where(inv[None, :] == runs[:, None], runs[None, :], 0), axis=1)
    table = jnp.asarray(turn_tables(places.shape[1]))

    chosen = jnp.any(picked[:, :, None] == jnp.arange(EXPERTS, dtype=jnp.int32), axis=1)
    tri = jnp.asarray(np.tril(np.ones((rows, rows), np.float32), -1), BF)
    slot = dot(tri, chosen.astype(BF))
    slot = jnp.where(chosen, slot, -1.0).astype(BF)
    column = np.arange(EXPERTS * CAP)
    named = (np.arange(EXPERTS)[:, None] == (column // CAP)[None, :]).astype(np.float32)
    at = dot(slot, jnp.asarray(named, BF))
    spot = (at == jnp.asarray(column % CAP, F32)[None, :]).astype(BF)

    send, first_low, first_turned, q_proj, k_proj = pre(
        x_low, attn_gain, w_query, w_key, w_value, query_gain, key_gain, picked.T
    )
    g_all = lax.all_gather(g_low, "ctx")
    recv = by_ctx(send)
    recv, spot = held((recv, spot))
    kv_all, q_all, att_all, lse_all, att_send = attend(order, inv, recv, table)
    att_send, w_gate, w_up, w_down = held((att_send, w_gate, w_up, w_down))
    down_blocks = w_down.reshape(2, 128, 8, 128).transpose(0, 2, 1, 3).reshape(2, 1024, 128)
    mine = held(jnp.concatenate([w_gate, w_up, down_blocks], axis=1))
    over_y = swap_y(mine)
    over_core = swap(mine, "exp", 1)
    heads = by_ctx(att_send)
    heads, mine, first_turned = held((heads, mine, first_turned))
    turned_all = lax.all_gather(first_turned, "ctx")
    over_both = swap(over_y, "exp", 1)
    router = w_router.T
    attended, middle, second_low, rows_send = middle_forward(heads, x_low, w_out, ffn_gain, spot)
    sent = by_ctx(rows_send.reshape(n_ctx, 2, CAP, -1))
    number = jnp.reshape(2 * ctx, (1,)).astype(jnp.int32)
    g_rows, slots = cotangent_rows(number, recv, g_all)
    sent, over_core, over_both, g_rows = held((sent, over_core, over_both, g_rows))
    parts = (mine, over_core, over_y, over_both)
    back = experts(number, sent, g_rows, router, parts)
    back = by_ctx(back).reshape(EXPERTS * CAP, -1)
    add = lambda *parts: sum(p.astype(F32) for p in parts).astype(BF)
    keep, near, far, out_part = weight_grads(number, sent, g_rows, router, slots, parts)
    back, near, keep, far, out_part, turned_all = held((back, near, keep, far, out_part, turned_all))
    out_part = lax.psum_scatter(out_part, "ctx", scatter_dimension=0, tiled=False)
    far = swap(far, "exp", 1)
    att_grad_send, grad_middle, branch = middle_back(
        spot, back, middle, second_low, router, ffn_gain, g_low, w_out
    )
    grad_recv = by_ctx(att_grad_send)
    even = 1 - jnp.bitwise_and(ctx, 1).astype(jnp.int32)
    place = jnp.stack([lax.axis_index("dp"), exp // 2, core, even]).astype(jnp.int32)
    out_mine, out_far = out_grads(place, attended, branch)
    near_a, near_b = (add(near[0, a], far[1, a]) for a in range(2))
    keep_a, keep_b = (add(keep[0, a], far[0, a]) for a in range(2))
    grad_recv, near_a, near_b, keep_a, keep_b, out_mine, out_far = held(
        (grad_recv, near_a, near_b, keep_a, keep_b, out_mine, out_far)
    )
    near_a = swap_y(near_a)
    near_b = swap_y(near_b)
    out_far = swap(out_far, "exp", 1)
    grad_send, kv_own = attend_back(
        order, inv, place[3:], grad_recv, kv_all, q_all, att_all, lse_all, table
    )
    kv_other = swap(kv_own, "ctx", 1)
    grad_send = join(grad_send, out_mine, out_far)
    grads = by_ctx(grad_send)
    keep_a = held(add(keep_a, near_a))
    dp_a = swap(keep_a, "dp", 1)
    keep_b = held(add(keep_b, near_b))
    dp_b = swap(keep_b, "dp", 1)
    grads, keep_a, keep_b, kv_other, dp_a = held((grads, keep_a, keep_b, kv_other, dp_a))
    own_gain = jnp.concatenate(
        [
            lax.dynamic_slice_in_dim(query_gain, ctx * HEAD_DIM, HEAD_DIM),
            lax.dynamic_slice_in_dim(key_gain, ctx // 2 * HEAD_DIM, HEAD_DIM),
        ]
    ).astype(F32)[None]
    shares = head_grads(
        place, turned_all, grad_send, kv_other, recv, grads, grad_recv, own_gain
    )
    shares, dp_b = held((shares, dp_b))
    shares = lax.all_to_all(shares, ("dp", "exp"), split_axis=0, concat_axis=0, tiled=True)
    input_grad, gain_part = input_back(
        grads, q_proj, k_proj, x_low, grad_middle, query_gain, key_gain, attn_gain, w_query, w_key, w_value
    )
    shares, gain_part, input_grad = held((shares, gain_part, input_grad))
    chips = n_dp * n_ctx * 2
    whole = across_chips(share_out(shares, gain_part, chips))
    sums = [k.astype(F32) + d.astype(F32) for k, d in ((keep_a, dp_a), (keep_b, dp_b))]
    grad_gate_w = jnp.stack([v[:1024] for v in sums])
    grad_up_w = jnp.stack([v[1024:2048] for v in sums])
    grad_down_w = jnp.stack(
        [v[2048:].reshape(8, 128, 128).transpose(1, 0, 2).reshape(128, 1024) for v in sums]
    )
    outputs = (middle + out_part.astype(F32)).astype(BF)
    whole, outputs, grad_gate_w, grad_up_w, grad_down_w = held(
        (whole, outputs, grad_gate_w, grad_up_w, grad_down_w)
    )
    other = swap(whole, "exp", 1)
    shape = (n_dp, n_ctx, 2, PART, 128)
    done = spread(jnp.reshape(core, (1,)), whole.reshape(shape))
    done = spread(jnp.reshape(1 - core, (1,)), other.reshape(shape), done[:4] + done[5:])
    wq, wk, wv, wo = (v.reshape(1024, -1) for v in done[:4])
    router_grad = done[4].T
    x_gain, q_gain, k_gain, f_gain = (v.reshape(-1) for v in done[5:])
    return (
        outputs[None],
        input_grad[None],
        x_gain,
        wq,
        wk,
        wv,
        q_gain,
        k_gain,
        wo,
        f_gain,
        router_grad,
        grad_gate_w,
        grad_up_w,
        grad_down_w,
    )


def solution(mesh):
    seqs = ("dp", "exp")
    row_spec = P(seqs, "ctx", None)
    in_specs = (row_spec, P(seqs, None), row_spec, row_spec) + (P(),) * 9
    in_specs += (P("ctx", None, "exp"), P("ctx", None, "exp"), P("ctx", "exp", None))
    out_specs = (row_spec, row_spec) + (P(),) * 9
    out_specs += (P("ctx", None, "exp"), P("ctx", None, "exp"), P("ctx", "exp", None))
    return jax.shard_map(
        per_device, mesh=mesh, in_specs=in_specs, out_specs=out_specs, check_vma=False
    )
```

```python
import jax
import jax.numpy as jnp
import numpy as np
from jax import lax
from jax.experimental import pallas as pl
from jax.experimental.pallas import tpu as pltpu
from jax.sharding import PartitionSpec as P

HEADS = 16
KV_HEADS = 8
HEAD_DIM = 64
EXPERTS = 32
CAP = 40
EPSILON = 1e-06
MASKED = -1e30
BF = jnp.bfloat16
F32 = jnp.float32
RUN = 64
QB = 512
QB_BACK = 256
PART = 208
BASE = 256
MIB = 1024 * 1024
NT = ((1,), (1,))
TN = ((0,), (0,))
VM = pl.BlockSpec(memory_space=pltpu.VMEM)
SM = pl.BlockSpec(memory_space=pltpu.SMEM)


def dot(a, b, dims=((1,), (0,))):
    return lax.dot_general(a, b, (dims, ((), ())), preferred_element_type=F32)


def call(kernel, outs, ins, name, flops, moved, scratch=(), transcendentals=0, vmem=62):
    return pl.pallas_call(
        kernel,
        out_shape=outs,
        in_specs=ins,
        out_specs=jax.tree.map(lambda _: VM, outs),
        scratch_shapes=list(scratch),
        compiler_params=pltpu.CompilerParams(vmem_limit_bytes=vmem * MIB),
        cost_estimate=pl.CostEstimate(
            flops=flops, bytes_accessed=moved, transcendentals=transcendentals
        ),
        name=name,
    )


def like(shape, dtype):
    return jax.ShapeDtypeStruct(shape, dtype)


def inverse_rms(value):
    return lax.rsqrt(jnp.mean(value * value, axis=-1, keepdims=True) + EPSILON)


def row_of(ref):
    return ref[...].astype(F32).reshape(1, -1)


def lanes_of(rows):
    return lax.broadcasted_iota(jnp.int32, (rows, 128), 1)


def swap_halves(tile):
    return pltpu.roll(tile.astype(F32), 64, 1)


def pack_head(wide, head):
    tile = wide[:, 128 * (head // 2) : 128 * (head // 2 + 1)]
    low = lanes_of(RUN) < 64
    if head % 2 == 0:
        return jnp.where(low, tile[:RUN], swap_halves(tile[RUN:]))
    return jnp.where(low, swap_halves(tile[:RUN]), tile[RUN:])


def unpack_heads(even, odd):
    low = lanes_of(RUN) < 64
    even, odd = even.astype(F32), odd.astype(F32)
    return jnp.concatenate(
        [jnp.where(low, even, swap_halves(odd)), jnp.where(low, swap_halves(even), odd)], axis=0
    )


def turn_tables(seq):
    half = HEAD_DIM // 2
    frequency = (10000.0 ** (-np.arange(half) * 2.0 / HEAD_DIM)).astype(np.float32)
    angles = (np.arange(seq, dtype=np.float32)[:, None] * frequency[None, :]).astype(np.float64)
    cosine, sine = np.cos(angles), np.sin(angles)
    return np.concatenate([cosine, cosine, -sine, sine], axis=1).astype(np.float32)


def split_table(table):
    low = lanes_of(table.shape[0]) < 64
    return jnp.where(low, table, 1.0), jnp.where(low, pltpu.roll(table, 64, 1), 0.0)


def turn(tile, cosine, sine):
    other = jnp.where(lanes_of(tile.shape[0]) < 32, pltpu.roll(tile, 96, 1), pltpu.roll(tile, 32, 1))
    return tile * cosine + other * sine


def pre_kernel(x_ref, gain, wq, wk, wv, q_gain, k_gain, picks, send, first_out, turned_out, q_out, k_out):
    x = x_ref[...].astype(F32)
    wide = x * inverse_rms(x) * row_of(gain)
    first = wide.astype(BF)
    first_out[...] = first
    q = dot(first, wq[...])
    k = dot(first, wk[...])
    v = dot(first, wv[...])
    q_out[...] = q
    k_out[...] = k
    qn = q * inverse_rms(q) * (row_of(q_gain) * HEAD_DIM ** (-0.5))
    kn = k * inverse_rms(k) * row_of(k_gain)
    low = lanes_of(x.shape[0]) < 64
    for h in range(KV_HEADS):
        cut = slice(128 * (h // 2), 128 * (h // 2 + 1))
        kt, vt = kn[:, cut], v[:, cut]
        if h % 2 == 0:
            both = jnp.where(low, kt, swap_halves(vt))
        else:
            both = jnp.where(low, swap_halves(kt), vt)
        both = both.astype(BF)
        send[2 * h, 0 : 2 * RUN, :] = both
        send[2 * h + 1, 0 : 2 * RUN, :] = both
    lane = lanes_of(x.shape[0])
    rows = jnp.transpose(jnp.where(lane == 0, inverse_rms(q), inverse_rms(k)))[0:2, :]
    high = rows.astype(BF).astype(F32)
    named = jnp.concatenate(
        [picks[...].astype(F32), high, rows - high, jnp.zeros((4, 128), F32)], axis=0
    ).astype(BF)
    for d in range(HEADS):
        send[d, 2 * RUN : 3 * RUN, :] = pack_head(qn, d).astype(BF)
        send[d, 3 * RUN : 3 * RUN + 16, :] = named
    turned_out[...] = jnp.transpose(first.astype(F32)).astype(BF)


def pre(x, gain, wq, wk, wv, q_gain, k_gain, picks):
    rows, width = x.shape
    return call(
        pre_kernel,
        (
            like((HEADS, 3 * RUN + 16, 128), BF),
            like((rows, width), BF),
            like((width, rows), BF),
            like((rows, wq.shape[1]), F32),
            like((rows, wk.shape[1]), F32),
        ),
        [VM] * 8,
        "pre",
        2 * rows * width * 2048,
        6 * 1024 * 1024,
    )(x, gain, wq, wk, wv, q_gain, k_gain, picks)


def turn_over(source, target):
    for i in range(source.shape[0] // 128):
        cut = slice(128 * i, 128 * (i + 1))
        target[:, cut] = jnp.transpose(source[cut, :].astype(F32)).astype(BF)


def masked_scores(kv, q, block):
    scores = dot(kv, q, NT)
    end = scores.shape[0]
    row = lax.broadcasted_iota(jnp.int32, (block, block), 0)
    col = lax.broadcasted_iota(jnp.int32, (block, block), 1)
    last = jnp.where(row <= col, scores[end - block :, :], MASKED)
    return last if end == block else jnp.concatenate([scores[: end - block, :], last], axis=0)


def attend_kernel(order, inv, recv, table, kv_out, q_out, att_out, lse_out, send_out, turned):
    seq = kv_out.shape[0]
    lane = lanes_of(RUN)

    def gather(b, carry):
        s = order[b]
        c = lax.shift_right_logical(s, 1)
        half = jnp.bitwise_and(s, 1)
        rows = pl.ds(pl.multiple_of(b * RUN, RUN), RUN)
        cos, sin = split_table(table[rows, :])
        kv = recv[c, pl.ds(pl.multiple_of(half * RUN, RUN), RUN), :].astype(F32)
        kv_out[rows, :] = turn(kv, cos, sin).astype(BF)
        tile = recv[c, pl.ds(2 * RUN, RUN), :].astype(F32)
        q = jnp.where(lane < 64, jnp.where(half == 0, tile, swap_halves(tile)), 0.0)
        q_out[rows, :] = turn(q, cos, sin).astype(BF)
        return carry

    lax.fori_loop(0, seq // RUN, gather, 0, unroll=32)
    turn_over(kv_out, turned)
    for i in range(seq // QB):
        here = slice(i * QB, (i + 1) * QB)
        end = (i + 1) * QB
        scores = masked_scores(kv_out[:end, :], q_out[here, :], QB)
        top = jnp.max(scores, axis=0, keepdims=True)
        weights = jnp.exp(scores - top)
        total = jnp.sum(weights, axis=0, keepdims=True)
        att = jnp.transpose(dot(turned[:, :end], weights.astype(BF)) / total)
        att_out[here, :] = att.astype(BF)
        lse_out[:, here] = jnp.broadcast_to(top + jnp.log(total), (8, QB))

    def place(c, carry):
        b0, b1 = inv[2 * c], inv[2 * c + 1]
        first = att_out[pl.ds(pl.multiple_of(b0 * RUN, RUN), RUN), :]
        second = att_out[pl.ds(pl.multiple_of(b1 * RUN, RUN), RUN), :]
        send_out[c] = jnp.where(lane < 64, swap_halves(first), second.astype(F32)).astype(BF)
        return carry

    lax.fori_loop(0, send_out.shape[0], place, 0, unroll=16)


def attend(order, inv, recv, table):
    n = recv.shape[0]
    seq = n * 128
    return call(
        attend_kernel,
        (
            like((seq, 128), BF),
            like((seq, 128), BF),
            like((seq, 128), BF),
            like((8, seq), F32),
            like((n, RUN, 128), BF),
        ),
        [SM, SM, VM, VM],
        "attend",
        4 * seq * seq * 128 // 2,
        14 * seq * 128,
        [pltpu.VMEM((128, seq), BF)],
        transcendentals=seq * seq // 2,
    )(order, inv, recv, table)


def attend_back_kernel(
    order, inv, even, recv, kv_in, q_in, att_in, lse_in, table, _,
    send_hbm, kv_grad_out, g_all, dq_all, dkv_all, sums, turned, send_out, sem,
):
    seq = kv_in.shape[0]
    lane = lanes_of(RUN)

    def gather(b, carry):
        s = order[b]
        c = lax.shift_right_logical(s, 1)
        half = jnp.bitwise_and(s, 1)
        tile = recv[c, 0:RUN, :].astype(F32)
        g_all[pl.ds(pl.multiple_of(b * RUN, RUN), RUN), :] = jnp.where(
            lane >= 64, jnp.where(half == 1, tile, swap_halves(tile)), 0.0
        ).astype(BF)
        return carry

    lax.fori_loop(0, seq // RUN, gather, 0, unroll=32)
    turn_over(kv_in, turned)
    steps = seq // QB_BACK
    for i in reversed(range(steps)):
        here = slice(i * QB_BACK, (i + 1) * QB_BACK)
        end = (i + 1) * QB_BACK
        kv, q, g = kv_in[:end, :], q_in[here, :], g_all[here, :]
        offset = jnp.sum(jnp.transpose(att_in[here, :].astype(F32) * g.astype(F32)), axis=0, keepdims=True)
        weights = jnp.exp(masked_scores(kv, q, QB_BACK) - lse_in[0:1, here])
        grad_scores = (weights * (dot(kv, g, NT) - offset)).astype(BF)
        dq_all[here, :] = jnp.transpose(dot(turned[:, :end], grad_scores))
        step = dot(grad_scores, q) + dot(weights.astype(BF), g)
        if i == steps - 1:
            dkv_all[...] = step
        else:
            dkv_all[:end, :] += step

    def place(c, carry):
        b0, b1 = inv[2 * c], inv[2 * c + 1]
        r0 = pl.ds(pl.multiple_of(b0 * RUN, RUN), RUN)
        r1 = pl.ds(pl.multiple_of(b1 * RUN, RUN), RUN)
        cos0, sin0 = split_table(table[r0, :])
        cos1, sin1 = split_table(table[r1, :])
        kv0 = turn(dkv_all[r0, :], cos0, -sin0).astype(BF)
        kv1 = turn(dkv_all[r1, :], cos1, -sin1).astype(BF)
        send_out[c, 0 : RUN, :] = kv0
        send_out[c, RUN : 2 * RUN, :] = kv1
        kv0, kv1 = kv0.astype(F32), kv1.astype(F32)
        values = jnp.where(lane < 64, swap_halves(kv0), kv1)
        keys = jnp.where(lane < 64, kv0, swap_halves(kv1))
        kv_grad_out[c] = jnp.where(even[0] == 1, values, keys).astype(BF)
        both_q = jnp.concatenate([dq_all[r0, :], dq_all[r1, :]], axis=0)
        both_q = both_q * jnp.concatenate([q_in[r0, :], q_in[r1, :]], axis=0).astype(F32)
        both_k = jnp.concatenate([dkv_all[r0, :], dkv_all[r1, :]], axis=0)
        both_k = both_k * jnp.concatenate([kv_in[r0, :], kv_in[r1, :]], axis=0).astype(F32)
        some = jnp.where(lanes_of(8) < 64, 1.0, 0.0).astype(BF)
        sums[pl.ds(c, 1), :] = dot(some, both_q.astype(BF), NT)[0:1, :]
        sums[pl.ds(n + c, 1), :] = dot(some, both_k.astype(BF), NT)[0:1, :]
        q0 = turn(dq_all[r0, :], cos0, -sin0)
        q1 = turn(dq_all[r1, :], cos1, -sin1)
        both = jnp.where(lane < 64, q0, swap_halves(q1))
        send_out[c, 2 * RUN : 3 * RUN, :] = (both * HEAD_DIM ** (-0.5)).astype(BF)
        return carry

    n = send_out.shape[0]
    lax.fori_loop(0, n, place, 0, unroll=16)
    for c in range(n):
        send_out[c, 3 * RUN : 3 * RUN + 2 * n, :] = sums[...].astype(BF)
    copy = pltpu.make_async_copy(send_out, send_hbm.at[:, pl.ds(BASE, 3 * RUN + 2 * n), :], sem)
    copy.start()
    copy.wait()


def attend_back(order, inv, even, recv, kv, q, att, lse, table, begun):
    n = recv.shape[0]
    seq = n * 128
    whole = lambda v: pl.BlockSpec(v.shape, lambda i: (0,) * v.ndim)
    return pl.pallas_call(
        attend_back_kernel,
        grid=(1,),
        out_shape=(like((n, BASE + 3 * RUN + 2 * n, 128), BF), like((n, RUN, 128), BF)),
        in_specs=[SM, SM, SM]
        + [whole(v) for v in (recv, kv, q, att, lse, table)]
        + [pl.BlockSpec(memory_space=pl.ANY)],
        input_output_aliases={9: 0},
        out_specs=(
            pl.BlockSpec(memory_space=pl.ANY),
            pl.BlockSpec((n, RUN, 128), lambda i: (0, 0, 0)),
        ),
        scratch_shapes=[
            pltpu.VMEM((seq, 128), BF),
            pltpu.VMEM((seq, 128), F32),
            pltpu.VMEM((seq, 128), F32),
            pltpu.VMEM((2 * n, 128), F32),
            pltpu.VMEM((128, seq), BF),
            pltpu.VMEM((n, 3 * RUN + 2 * n, 128), BF),
            pltpu.SemaphoreType.DMA,
        ],
        compiler_params=pltpu.CompilerParams(vmem_limit_bytes=62 * MIB),
        cost_estimate=pl.CostEstimate(
            flops=10 * seq * seq * 128 // 2, bytes_accessed=20 * seq * 128, transcendentals=seq * seq // 2
        ),
        name="attend_back",
    )(order, inv, even, recv, kv, q, att, lse, table, begun)


def slot_masks(slot, pair):
    line = lax.broadcasted_iota(jnp.int32, (2 * CAP, 128), 0).astype(F32)
    left = (line < CAP) & (line == slot[2 * pair : 2 * pair + 1, :])
    right = (line >= CAP) & (line - CAP == slot[2 * pair + 1 : 2 * pair + 2, :])
    return jnp.where(left, 1.0, 0.0).astype(BF), jnp.where(right, 1.0, 0.0).astype(BF)


def cotangent_kernel(number, picks_ref, g_ref, rows_ref, slot_ref):
    n_ctx = g_ref.shape[0]
    picks = picks_ref[...].astype(F32)[:, :8, :]
    before = lax.broadcasted_iota(jnp.int32, (128, 128), 0) < lax.broadcasted_iota(
        jnp.int32, (128, 128), 1
    )
    before = jnp.where(before, 1.0, 0.0).astype(BF)
    for a in range(2):
        e = (number[0] + a).astype(F32)
        named = jnp.max(jnp.where(picks == e, 1.0, 0.0), axis=1)
        slot = jnp.where(named > 0.0, dot(named.astype(BF), before), -1.0)
        slot_ref[a] = slot
        for p in range(n_ctx // 2):
            left, right = slot_masks(slot, p)
            rows_ref[a, 2 * CAP * p : 2 * CAP * (p + 1), :] = (
                dot(left, g_ref[2 * p]) + dot(right, g_ref[2 * p + 1])
            ).astype(BF)


def cotangent_rows(number, recv, g_all):
    n_ctx = g_all.shape[0]
    whole = lambda *shape: pl.BlockSpec(shape, lambda i: (0,) * len(shape))
    return pl.pallas_call(
        cotangent_kernel,
        grid=(1,),
        out_shape=(like((2, n_ctx * CAP, 1024), BF), like((2, n_ctx, 128), F32)),
        in_specs=[
            SM,
            pl.BlockSpec((n_ctx, 16, 128), lambda i: (0, 3 * RUN // 16, 0)),
            whole(*g_all.shape),
        ],
        out_specs=(whole(2, n_ctx * CAP, 1024), whole(2, n_ctx, 128)),
        compiler_params=pltpu.CompilerParams(vmem_limit_bytes=62 * MIB),
        cost_estimate=pl.CostEstimate(
            flops=8 * n_ctx * 80 * 128 * 1024, bytes_accessed=8 * 1024 * 1024, transcendentals=0
        ),
        name="cotangent_rows",
    )(number, recv, g_all)


def expert_steps(e, rows_ref, g_ref, router_ref, parts):
    n_ctx = rows_ref.shape[0]
    rows = jnp.concatenate([rows_ref[c, 0].astype(F32) for c in range(n_ctx)], axis=0).astype(BF)
    grads = g_ref[0].astype(F32)
    logits = dot(rows, router_ref[...], NT)
    lane = lax.broadcasted_iota(jnp.int32, logits.shape, 1)
    powers = jnp.exp(logits - jnp.max(logits, axis=1, keepdims=True))
    gate = jnp.sum(jnp.where(lane == e, powers, 0.0), axis=1, keepdims=True) / jnp.sum(
        powers, axis=1, keepdims=True
    )
    w_gate = jnp.concatenate([w[0, 0:1024, :] for w in parts], axis=1)
    w_up = jnp.concatenate([w[0, 1024:2048, :] for w in parts], axis=1)
    w_down = jnp.concatenate(
        [
            jnp.concatenate([w[0, 2048 + 128 * n : 2176 + 128 * n, :] for n in range(8)], axis=1)
            for w in parts
        ],
        axis=0,
    )
    gate_act = dot(rows, w_gate)
    up_act = dot(rows, w_up)
    sig = 1.0 / (1.0 + jnp.exp(-gate_act))
    silu = gate_act * sig
    hidden = (silu * up_act).astype(BF)
    expert_out = dot(hidden, w_down)
    grad_rows = (gate * grads).astype(BF)
    grad_hidden = dot(grad_rows, w_down, NT)
    ga = (grad_hidden * up_act * sig * (1.0 + gate_act * (1.0 - sig))).astype(BF)
    gu = (grad_hidden * silu).astype(BF)
    return rows, grads, gate, w_gate, w_up, hidden, expert_out, grad_rows, ga, gu


def expert_kernel(number, rows_ref, g_ref, router_ref, *refs):
    parts, back_ref = refs[:4], refs[4]
    e = number[0] + pl.program_id(0)
    rows, grads, _, w_gate, w_up, _, expert_out, _, ga, gu = expert_steps(
        e, rows_ref, g_ref, router_ref, parts
    )
    grad_gate = jnp.sum(grads * expert_out, axis=1, keepdims=True)
    back = dot(ga, w_gate, NT) + dot(gu, w_up, NT)
    high = grad_gate.astype(BF).astype(F32)
    lane = lanes_of(rows.shape[0])
    tail = jnp.where(lane == e, high, jnp.where(lane == e + EXPERTS, grad_gate - high, 0.0))
    for c in range(rows_ref.shape[0]):
        cut = slice(CAP * c, CAP * (c + 1))
        back_ref[c, 0, :, 0:1024] = back[cut, :].astype(BF)
        back_ref[c, 0, :, 1024:1152] = tail[cut, :].astype(BF)


def weight_grad_kernel(number, rows_ref, g_ref, router_ref, slot_ref, *refs):
    parts, (keep, near, far, sums_ref) = refs[:4], refs[4:]
    e = number[0] + pl.program_id(0)
    rows, _, gate, _, _, hidden, expert_out, grad_rows, ga, gu = expert_steps(
        e, rows_ref, g_ref, router_ref, parts
    )
    line = lax.broadcasted_iota(jnp.int32, (CAP, 128), 0).astype(F32)
    first = pl.program_id(0) == 0
    out_rows = gate * expert_out
    for c in range(rows_ref.shape[0]):
        mask = jnp.where(line == slot_ref[0, c : c + 1, :], 1.0, 0.0).astype(BF)
        part = dot(mask, out_rows[CAP * c : CAP * (c + 1), :].astype(BF), TN)
        before = jnp.where(first, 0.0, sums_ref[c].astype(F32))
        sums_ref[c] = (part + before).astype(BF)
    gate_grad = dot(rows, ga, TN)
    up_grad = dot(rows, gu, TN)
    down_grad = dot(hidden, grad_rows, TN)
    for j, (ref, at) in enumerate([(keep, 0), (far, 0), (near, 0), (far, 1)]):
        cut = slice(128 * j, 128 * (j + 1))
        ref[at, 0, 0:1024, :] = gate_grad[:, cut].astype(BF)
        ref[at, 0, 1024:2048, :] = up_grad[:, cut].astype(BF)
        for n in range(8):
            ref[at, 0, 2048 + 128 * n : 2176 + 128 * n, :] = down_grad[
                cut, 128 * n : 128 * (n + 1)
            ].astype(BF)


def expert_call(kernel, name, number, rows, grads, router, slots, parts, outs, out_specs):
    n_ctx = rows.shape[0]
    n = n_ctx * CAP
    extra = () if slots is None else (slots,)
    return pl.pallas_call(
        kernel,
        grid=(2,),
        out_shape=outs,
        in_specs=[
            SM,
            pl.BlockSpec((n_ctx, 1, CAP, 1024), lambda i: (0, i, 0, 0)),
            pl.BlockSpec((1, n, 1024), lambda i: (i, 0, 0)),
            pl.BlockSpec(router.shape, lambda i: (0, 0)),
        ]
        + [pl.BlockSpec((1,) + v.shape[1:], lambda i: (i, 0, 0)) for v in extra + tuple(parts)],
        out_specs=out_specs,
        compiler_params=pltpu.CompilerParams(vmem_limit_bytes=62 * MIB),
        cost_estimate=pl.CostEstimate(
            flops=24 * n * 1024 * 512, bytes_accessed=20 * 1024 * 1024, transcendentals=2 * n * 512
        ),
        name=name,
    )(number, rows, grads, router, *extra, *parts)


def experts(number, rows, grads, router, parts):
    n_ctx = rows.shape[0]
    return expert_call(
        expert_kernel, "experts", number, rows, grads, router, None, parts,
        like((n_ctx, 2, CAP, 1152), BF),
        pl.BlockSpec((n_ctx, 1, CAP, 1152), lambda i: (0, i, 0, 0)),
    )


def weight_grads(number, rows, grads, router, slots, parts):
    n_ctx = rows.shape[0]
    put = lambda k: pl.BlockSpec((k, 1, 3072, 128), lambda i: (0, i, 0, 0))
    return expert_call(
        weight_grad_kernel, "weight_grads", number, rows, grads, router, slots, parts,
        (
            like((1, 2, 3072, 128), BF),
            like((1, 2, 3072, 128), BF),
            like((2, 2, 3072, 128), BF),
            like((n_ctx, 128, 1024), BF),
        ),
        (put(1), put(1), put(2), pl.BlockSpec((n_ctx, 128, 1024), lambda i: (0, 0, 0))),
    )


def middle_kernel(heads, x_ref, w_out, gain, spot, attended_out, middle_out, second_out, send_out):
    attended = jnp.concatenate(
        [unpack_heads(heads[2 * t], heads[2 * t + 1]) for t in range(HEADS // 2)], axis=1
    ).astype(BF)
    attended_out[...] = attended
    middle = x_ref[...].astype(F32) + dot(attended, w_out[...])
    middle_out[...] = middle
    second = (middle * inverse_rms(middle) * row_of(gain)).astype(BF)
    second_out[...] = second
    send_out[...] = dot(spot[...], second, TN).astype(BF)


def middle_forward(heads, x, w_out, gain, spot):
    rows, width = x.shape
    return call(
        middle_kernel,
        (
            like((rows, width), BF),
            like((rows, width), F32),
            like((rows, width), BF),
            like((spot.shape[1], width), BF),
        ),
        [VM] * 5,
        "middle",
        2 * rows * width * (1024 + 1280),
        6 * 1024 * 1024,
    )(heads, x, w_out, gain, spot)


def middle_back_kernel(
    spot, back, middle_ref, second, router, gain, g_ref, w_out,
    send, grad_out, branch_out,
):
    summed = dot(spot[...], back[...])
    logits = dot(second[...], router[...], NT)
    powers = jnp.exp(logits - jnp.max(logits, axis=1, keepdims=True))
    probs = powers / jnp.sum(powers, axis=1, keepdims=True)
    last = summed[:, 1024:1152]
    grad_sel = (last + pltpu.roll(last, 128 - EXPERTS, 1))[:, :EXPERTS]
    grad_logits = probs * (grad_sel - jnp.sum(probs * grad_sel, axis=1, keepdims=True))
    high = grad_logits.astype(BF)
    rest = (grad_logits - high.astype(F32)).astype(BF)
    upstream = summed[:, :1024] + dot(high, router[...]) + dot(rest, router[...])
    middle = middle_ref[...]
    r = inverse_rms(middle)
    hat = middle * r
    gain_part = jnp.sum(upstream * hat, axis=0, keepdims=True)
    router_part = dot(high, second[...], TN) + dot(rest, second[...], TN)
    low = lanes_of(EXPERTS) < 64
    first_row = lax.broadcasted_iota(jnp.int32, (EXPERTS, 128), 0) == 0
    for d in range(HEADS):
        cut = slice(128 * (d // 2), 128 * (d // 2 + 1))
        tile = router_part[:, cut]
        part = jnp.where(first_row, jnp.broadcast_to(gain_part[:, cut], (EXPERTS, 128)), 0.0)
        if d % 2 == 0:
            misc = jnp.where(low, tile, swap_halves(part))
        else:
            misc = jnp.where(low, swap_halves(tile), part)
        send[d, RUN : RUN + EXPERTS, :] = misc.astype(BF)
    scaled = upstream * row_of(gain)
    grad = (
        r * (scaled - hat * jnp.mean(scaled * hat, axis=1, keepdims=True)) + g_ref[...].astype(F32)
    )
    grad_out[...] = grad
    branch = grad.astype(BF)
    branch_out[...] = branch
    att = dot(branch, w_out[...], NT)
    for d in range(HEADS):
        send[d, 0:RUN, :] = pack_head(att, d).astype(BF)


def middle_back(spot, back, middle, second, router, gain, g_low, w_out):
    rows, width = middle.shape
    return call(
        middle_back_kernel,
        (
            like((HEADS, RUN + EXPERTS, 128), BF),
            like((rows, width), F32),
            like((rows, width), BF),
        ),
        [VM] * 8,
        "middle_back",
        2 * rows * width * (1280 + 1024),
        6 * 1024 * 1024,
    )(spot, back, middle, second, router, gain, g_low, w_out)


def out_grad_kernel(place, attended, other, branch, other_branch, send_hbm, rows, sem):
    for j in range(4):
        pair = jnp.bitwise_xor(place[0], j % 2) * 2 + jnp.bitwise_xor(place[1], j // 2)
        own = attended[:, pl.ds(pl.multiple_of((2 * pair + place[2]) * 128, 128), 128)]
        far = other[:, pl.ds(pl.multiple_of(pair * 128, 128), 128)]
        part = dot(own, branch[...], TN) + dot(far, other_branch[...], TN)
        for c in range(rows.shape[0]):
            both = part[8 * c : 8 * c + 8, :]
            for m in range(0, 8, 2):
                two = (both[:, 128 * m : 128 * m + 128], both[:, 128 * m + 128 : 128 * m + 256])
                at = 64 * j + 8 * m
                rows[c, at : at + 16, :] = jnp.concatenate(two, axis=0).astype(BF)
    copy = pltpu.make_async_copy(rows, send_hbm.at[:, pl.ds(0, BASE), :], sem)
    copy.start()
    copy.wait()


def out_grads(place, attended, other, branch, other_branch):
    n = HEADS
    whole = lambda v: pl.BlockSpec(v.shape, lambda i: (0,) * v.ndim)
    return pl.pallas_call(
        out_grad_kernel,
        grid=(1,),
        out_shape=like((n, BASE + 3 * RUN + 2 * n, 128), BF),
        in_specs=[SM] + [whole(v) for v in (attended, other, branch, other_branch)],
        out_specs=pl.BlockSpec(memory_space=pl.ANY),
        scratch_shapes=[pltpu.VMEM((n, BASE, 128), BF), pltpu.SemaphoreType.DMA],
        compiler_params=pltpu.CompilerParams(vmem_limit_bytes=62 * MIB),
        cost_estimate=pl.CostEstimate(flops=1 << 20, bytes_accessed=1 << 18, transcendentals=0),
        name="out_grads",
    )(place, attended, other, branch, other_branch)


def queries_of(recv):
    return jnp.concatenate(
        [
            unpack_heads(
                recv[2 * t, BASE + 2 * RUN : BASE + 3 * RUN, :],
                recv[2 * t + 1, BASE + 2 * RUN : BASE + 3 * RUN, :],
            )
            for t in range(HEADS // 2)
        ],
        axis=1,
    )


def keys_values_of(recv):
    low = lanes_of(2 * RUN) < 64
    both = [
        recv[2 * j, BASE : BASE + 2 * RUN, :].astype(F32)
        + recv[2 * j + 1, BASE : BASE + 2 * RUN, :].astype(F32)
        for j in range(KV_HEADS)
    ]
    keys, values = [], []
    for t in range(KV_HEADS // 2):
        keys.append(jnp.where(low, both[2 * t], swap_halves(both[2 * t + 1])))
        values.append(jnp.where(low, swap_halves(both[2 * t]), both[2 * t + 1]))
    return jnp.concatenate(keys, axis=1), jnp.concatenate(values, axis=1)


def input_kernel(
    recv, q_ref, k_ref, x_ref, middle, q_gain, k_gain, gain, wq, wk, wv, out_ref, gain_ref
):
    uq = queries_of(recv)
    uk, dv = keys_values_of(recv)
    q, k = q_ref[...], k_ref[...]
    rq, rk = inverse_rms(q), inverse_rms(k)
    qh, kh = q * rq, k * rk
    uq, uk = uq * row_of(q_gain), uk * row_of(k_gain)
    gq = (rq * (uq - qh * jnp.mean(uq * qh, axis=1, keepdims=True))).astype(BF)
    gk = (rk * (uk - kh * jnp.mean(uk * kh, axis=1, keepdims=True))).astype(BF)
    upstream = dot(gq, wq[...], NT) + dot(gk, wk[...], NT) + dot(dv.astype(BF), wv[...], NT)
    x = x_ref[...].astype(F32)
    r = inverse_rms(x)
    hat = x * r
    x_part = jnp.sum(upstream * hat, axis=0, keepdims=True)
    scaled = upstream * row_of(gain)
    out_ref[...] = middle[...] + r * (scaled - hat * jnp.mean(scaled * hat, axis=1, keepdims=True))
    half = jnp.zeros((1, 64), F32)
    rows = [jnp.concatenate([half, x_part[:, 64 * i : 64 * (i + 1)]], axis=1) for i in range(8)]
    none = jnp.zeros((2, 128), F32)
    more = [x_part[:, 512 + 128 * i : 640 + 128 * i] for i in range(4)]
    gain_ref[...] = jnp.concatenate(rows + [none] + more + [none], axis=0)


def input_back(recv, q, k, x, middle, q_gain, k_gain, gain, wq, wk, wv):
    rows, width = x.shape
    return call(
        input_kernel,
        (like((rows, width), F32), like((16, 128), F32)),
        [VM] * 11,
        "input_back",
        2 * rows * width * 2048,
        8 * 1024 * 1024,
    )(recv, q, k, x, middle, q_gain, k_gain, gain, wq, wk, wv)


def head_grad_kernel(
    place, turned, early, later, queries, kv_other, normed, out_parts, sums_ref, branch, gain_ref, out_ref
):
    n = early.shape[0]
    low = lanes_of(128) < 64
    gain = gain_ref[...]
    sums = sums_ref[0].astype(F32)
    others = branch[0].astype(F32)
    for c in range(1, n):
        sums = sums + sums_ref[c].astype(F32)
        others = others + branch[c].astype(F32)
    out_rows = out_parts[0].astype(F32)
    for c in range(1, n):
        out_rows = out_rows + out_parts[c].astype(F32)
    q_means = sums[0:n, :] / (HEADS * HEAD_DIM)
    k_means = sums[n : 2 * n, :] / (KV_HEADS * HEAD_DIM)
    total = None
    gains = None
    for p in range(n // 2):
        parts = []
        for c in (2 * p, 2 * p + 1):
            packed = queries[c].astype(F32)
            uq = jnp.concatenate([packed, swap_halves(packed)], axis=0)
            both = jnp.concatenate([early[c].astype(F32), later[c].astype(F32)], axis=0)
            other = kv_other[c].astype(F32)
            other = jnp.concatenate([swap_halves(other), other], axis=0)
            keys = swap_halves(both) + other
            upstream = jnp.where(low, uq, keys)
            packed = normed[c, 2 * RUN : 3 * RUN, :].astype(F32)
            qn = jnp.concatenate([packed, swap_halves(packed)], axis=0) * HEAD_DIM**0.5
            hat = jnp.where(low, qn, swap_halves(normed[c, 0 : 2 * RUN, :])) / gain
            factors = normed[c, 3 * RUN : 3 * RUN + 16, :].astype(F32)
            factors = factors[8:10, :] + factors[10:12, :]
            rows = jnp.concatenate(
                [factors, q_means[c : c + 1, :], k_means[c : c + 1, :], jnp.zeros((4, 128), F32)], axis=0
            )
            cols = jnp.transpose(jnp.concatenate([rows] * 16, axis=0))
            r = jnp.where(low, cols[:, 0:1], cols[:, 1:2])
            m = jnp.where(low, cols[:, 2:3], cols[:, 3:4])
            grad = r * (upstream * gain - hat * m)
            part = jnp.sum(upstream * hat, axis=0, keepdims=True)
            gains = part if gains is None else gains + part
            parts.append(jnp.where(low | (place[3] == 1), grad, both + other).astype(BF))
        left = jnp.concatenate([turned[2 * p], turned[2 * p + 1]], axis=1)
        step = dot(left, jnp.concatenate(parts, axis=0))
        total = step if total is None else total + step
    low_row = low[0:1, :]
    gains = jnp.where(low_row | (place[3] == 1), gains, 0.0)
    ffn = jnp.where(low_row, swap_halves(others[0:8, :])[0:1, :], 0.0)
    rows = jnp.concatenate([gains, ffn, jnp.zeros((6, 128), F32)], axis=0)
    some = lanes_of(8) < 64
    for s in range(8):
        out_ref[s, 0:128, :] = total[128 * s : 128 * (s + 1), :].astype(BF)
        kept = jnp.where(some, others[8 * (s // 2) : 8 * (s // 2) + 8, :], 0.0)
        out_ref[s, 128:144, :] = jnp.concatenate(
            [kept, rows if s == 0 else jnp.zeros((8, 128), F32)], axis=0
        ).astype(BF)
        out_ref[s, 144:PART, :] = jnp.zeros((64, 128), BF)
    for j in range(4):
        at = jnp.bitwise_xor(place[0], j % 2) * 4 + jnp.bitwise_xor(place[1], j // 2) * 2 + place[2]
        out_ref[pl.ds(at, 1), 144:PART, :] = out_rows[64 * j : 64 * j + 64, :].astype(BF)[None]


def head_grads(place, turned, own, kv_other, normed, grads, branch, gain):
    whole = lambda v: pl.BlockSpec(v.shape, lambda i: (0,) * v.ndim)
    n = own.shape[0]
    part = lambda rows, at: pl.BlockSpec((n, rows, 128), lambda i: (0, at // rows, 0))
    return pl.pallas_call(
        head_grad_kernel,
        grid=(1,),
        out_shape=like((8, PART, 128), BF),
        in_specs=[
            SM,
            whole(turned),
            part(RUN, BASE),
            part(RUN, BASE + RUN),
            part(RUN, BASE + 2 * RUN),
            whole(kv_other),
            whole(normed),
            part(BASE, 0),
            part(2 * n, BASE + 3 * RUN),
            part(EXPERTS, RUN),
            whole(gain),
        ],
        out_specs=pl.BlockSpec((8, PART, 128), lambda i: (0, 0, 0)),
        compiler_params=pltpu.CompilerParams(vmem_limit_bytes=62 * MIB),
        cost_estimate=pl.CostEstimate(
            flops=2 * 2048 * 1024 * 128, bytes_accessed=8 * 1024 * 1024, transcendentals=0
        ),
        name="head_grads",
    )(place, turned, own, own, own, kv_other, normed, grads, grads, branch, gain)


def share_kernel(shares, gain_ref, out_ref):
    total = shares[0].astype(F32)
    for s in range(1, shares.shape[0]):
        total = total + shares[s].astype(F32)
    total = jnp.concatenate([total[0:128], total[128:144] + gain_ref[...], total[144:PART]], axis=0)
    total = total.astype(BF)
    for c in range(out_ref.shape[0]):
        out_ref[c] = total


def share_out(shares, gain, chips):
    return call(
        share_kernel,
        like((chips, PART, 128), BF),
        [VM, VM],
        "share_out",
        1 << 18,
        4 * 1024 * 1024,
    )(shares, gain)


def spread_kernel(place, block_ref, *refs):
    wq, wk, wv, wo, router, x_gain, q_gain, k_gain, f_gain = refs[-9:]
    n = block_ref.shape[1]
    low = lanes_of(128) < 64
    some = lanes_of(8) < 64
    total = None
    kept = None
    queries, keys, seconds = [], [], []
    for c in range(0, n, 2):
        even, odd = block_ref[0, c, 0].astype(F32), block_ref[0, c + 1, 0].astype(F32)
        wide = slice(64 * c, 64 * c + 128)
        wq[0, 0, :, wide] = jnp.where(low, even[:128], swap_halves(odd[:128]))
        key, value = even[:128], odd[:128]
        if c % 4 == 0:
            kept = (swap_halves(key), swap_halves(value))
        else:
            half = slice(32 * c - 64, 32 * c + 64)
            wk[0, 0, :, half] = jnp.where(low, kept[0], key)
            wv[0, 0, :, half] = jnp.where(low, kept[1], value)
        router[:, wide] = jnp.where(some, even[128:136], swap_halves(odd[128:136]))
        sums = even[128:144] + odd[128:144]
        total = sums if total is None else total + sums
        pairs = jnp.where(some, even[136:144], swap_halves(odd[136:144]))
        queries.append(pairs[0:1])
        seconds.append(pairs[1:2])
        if c % 4 == 0:
            key_gain = swap_halves(even[136:144])
        else:
            keys.append(jnp.where(some, key_gain, even[136:144])[0:1])
        for d, block in ((c, even), (c + 1, odd)):
            for m in range(8):
                wo[0, 0, 8 * d : 8 * d + 8, 128 * m : 128 * (m + 1)] = block[144 + 8 * m : 152 + 8 * m]
    turned = swap_halves(total)
    firsts = [
        jnp.where(some[0:1], turned[2 * t : 2 * t + 1], total[2 * t + 1 : 2 * t + 2]) for t in range(4)
    ]
    firsts = jnp.concatenate(firsts + [total[10 + t : 11 + t] for t in range(4)], axis=1)

    @pl.when(pl.program_id(0) == 0)
    def _():
        ours = place[0] == 0
        given = refs[4:8] if len(refs) > 9 else None
        for i, (ref, made) in enumerate([(x_gain, None), (q_gain, queries), (k_gain, keys), (f_gain, seconds)]):
            old = jnp.zeros(ref.shape, F32) if given is None else given[i][...]
            ref[...] = old if made is None else jnp.where(ours, jnp.concatenate(made, axis=1), old)

    x_gain[...] += firsts


def spread(place, block, before=None):
    dp, n, y = block.shape[:3]
    steps = dp * y
    put = lambda rows, width: pl.BlockSpec((1, 1, rows, width), lambda i, at: (i, at[0], 0, 0))
    sizes = [(128, 1024), (128, 512), (128, 512), (128, 1024)]
    widths = [1024, 1024, 512, 1024]
    small = [pl.BlockSpec((1, w), lambda i, at: (0, 0)) for w in widths]
    given = () if before is None else tuple(before)
    return pl.pallas_call(
        spread_kernel,
        grid_spec=pltpu.PrefetchScalarGridSpec(
            num_scalar_prefetch=1,
            grid=(steps,),
            in_specs=[pl.BlockSpec((1, n, 1, PART, 128), lambda i, at: (i // y, 0, i % y, 0, 0))]
            + ([pl.BlockSpec(memory_space=pl.ANY)] * 4 + small if given else []),
            out_specs=[put(*size) for size in sizes]
            + [pl.BlockSpec((8, 1024), lambda i, at: (i, 0))]
            + small,
        ),
        out_shape=[like((steps, 2) + size, F32) for size in sizes]
        + [like((8 * steps, 1024), F32)]
        + [like((1, w), F32) for w in widths],
        input_output_aliases={2 + i: i for i in range(4 if given else 0)},
        compiler_params=pltpu.CompilerParams(vmem_limit_bytes=62 * MIB),
        name="spread",
    )(place, block, *given)


def by_ctx(value):
    return lax.all_to_all(value, "ctx", split_axis=0, concat_axis=0, tiled=True)


def swap(value, axis, bit):
    n = lax.axis_size(axis)
    return lax.ppermute(value, axis, [(i, i ^ bit) for i in range(n)])


def swap_y(value):
    n = lax.axis_size("dp") * lax.axis_size("exp")
    return lax.ppermute(value, ("dp", "exp"), [(i, i ^ 6) for i in range(n)])


def held(value):
    return lax.optimization_barrier(value)


def across_chips(value):
    axes = ("dp", "ctx", "exp")
    dp, ctx, exp = (lax.axis_size(a) for a in axes)
    groups = [
        [(d * ctx + c) * exp + 2 * y + core for d in range(dp) for c in range(ctx) for y in range(exp // 2)]
        for core in range(2)
    ]
    return lax.all_to_all(
        value, axes, split_axis=0, concat_axis=0, tiled=True, axis_index_groups=groups
    )


def per_device(
    tokens,
    places,
    choices,
    cotangent,
    attn_gain,
    w_query,
    w_key,
    w_value,
    query_gain,
    key_gain,
    w_out,
    ffn_gain,
    w_router,
    w_gate,
    w_up,
    w_down,
):
    x_low = tokens[0]
    rows = x_low.shape[0]
    ctx = lax.axis_index("ctx")
    exp = lax.axis_index("exp")
    n_ctx = lax.axis_size("ctx")
    n_dp = lax.axis_size("dp")
    core = jnp.bitwise_and(exp, 1).astype(jnp.int32)
    picked = choices[0]
    g_low = cotangent[0]

    inv = places[0, ::RUN] // RUN
    runs = jnp.arange(inv.shape[0], dtype=jnp.int32)
    order = jnp.sum(jnp.where(inv[None, :] == runs[:, None], runs[None, :], 0), axis=1)
    table = jnp.asarray(turn_tables(places.shape[1]))

    chosen = jnp.any(picked[:, :, None] == jnp.arange(EXPERTS, dtype=jnp.int32), axis=1)
    tri = jnp.asarray(np.tril(np.ones((rows, rows), np.float32), -1), BF)
    slot = dot(tri, chosen.astype(BF))
    slot = jnp.where(chosen, slot, -1.0).astype(BF)
    column = np.arange(EXPERTS * CAP)
    named = (np.arange(EXPERTS)[:, None] == (column // CAP)[None, :]).astype(np.float32)
    at = dot(slot, jnp.asarray(named, BF))
    spot = (at == jnp.asarray(column % CAP, F32)[None, :]).astype(BF)

    send, first_low, first_turned, q_proj, k_proj = pre(
        x_low, attn_gain, w_query, w_key, w_value, query_gain, key_gain, picked.T
    )
    g_all = lax.all_gather(g_low, "ctx")
    recv = by_ctx(send)
    recv, spot = held((recv, spot))
    kv_all, q_all, att_all, lse_all, att_send = attend(order, inv, recv, table)
    att_send, w_gate, w_up, w_down = held((att_send, w_gate, w_up, w_down))
    down_blocks = w_down.reshape(2, 128, 8, 128).transpose(0, 2, 1, 3).reshape(2, 1024, 128)
    mine = held(jnp.concatenate([w_gate, w_up, down_blocks], axis=1))
    over_y = swap_y(mine)
    over_core = swap(mine, "exp", 1)
    heads = by_ctx(att_send)
    heads, mine, first_turned = held((heads, mine, first_turned))
    turned_all = lax.all_gather(first_turned, "ctx")
    over_both = swap(over_y, "exp", 1)
    router = w_router.T
    attended, middle, second_low, rows_send = middle_forward(heads, x_low, w_out, ffn_gain, spot)
    sent = by_ctx(rows_send.reshape(n_ctx, 2, CAP, -1))
    number = jnp.reshape(2 * ctx, (1,)).astype(jnp.int32)
    g_rows, slots = cotangent_rows(number, recv, g_all)
    halves = attended.reshape(rows, 4, 2, 128)
    halves = lax.dynamic_index_in_dim(halves, 1 - core, axis=2, keepdims=False).reshape(rows, 512)
    halves = swap(halves, "exp", 1)
    sent, over_core, over_both, g_rows, halves = held((sent, over_core, over_both, g_rows, halves))
    parts = (mine, over_core, over_y, over_both)
    back = experts(number, sent, g_rows, router, parts)
    back = by_ctx(back).reshape(EXPERTS * CAP, -1)
    add = lambda *parts: sum(p.astype(F32) for p in parts).astype(BF)
    keep, near, far, out_part = weight_grads(number, sent, g_rows, router, slots, parts)
    back, near, keep, far, out_part, turned_all = held((back, near, keep, far, out_part, turned_all))
    out_part = lax.psum_scatter(out_part, "ctx", scatter_dimension=0, tiled=False)
    far = swap(far, "exp", 1)
    att_grad_send, grad_middle, branch = middle_back(
        spot, back, middle, second_low, router, ffn_gain, g_low, w_out
    )
    grad_recv = by_ctx(att_grad_send)
    even = 1 - jnp.bitwise_and(ctx, 1).astype(jnp.int32)
    place = jnp.stack([lax.axis_index("dp"), exp // 2, core, even]).astype(jnp.int32)
    begun = out_grads(place, attended, halves, branch, swap(branch, "exp", 1))
    near_a, near_b = (add(near[0, a], far[1, a]) for a in range(2))
    keep_a, keep_b = (add(keep[0, a], far[0, a]) for a in range(2))
    grad_recv, near_a, near_b, keep_a, keep_b, begun = held(
        (grad_recv, near_a, near_b, keep_a, keep_b, begun)
    )
    near_a = swap_y(near_a)
    near_b = swap_y(near_b)
    grad_send, kv_own = attend_back(
        order, inv, place[3:], grad_recv, kv_all, q_all, att_all, lse_all, table, begun
    )
    kv_other = swap(kv_own, "ctx", 1)
    grads = by_ctx(grad_send)
    keep_a = held(add(keep_a, near_a))
    dp_a = swap(keep_a, "dp", 1)
    keep_b = held(add(keep_b, near_b))
    dp_b = swap(keep_b, "dp", 1)
    grads, keep_a, keep_b, kv_other, dp_a = held((grads, keep_a, keep_b, kv_other, dp_a))
    own_gain = jnp.concatenate(
        [
            lax.dynamic_slice_in_dim(query_gain, ctx * HEAD_DIM, HEAD_DIM),
            lax.dynamic_slice_in_dim(key_gain, ctx // 2 * HEAD_DIM, HEAD_DIM),
        ]
    ).astype(F32)[None]
    shares = head_grads(
        place, turned_all, grad_send, kv_other, recv, grads, grad_recv, own_gain
    )
    shares, dp_b = held((shares, dp_b))
    shares = lax.all_to_all(shares, ("dp", "exp"), split_axis=0, concat_axis=0, tiled=True)
    input_grad, gain_part = input_back(
        grads, q_proj, k_proj, x_low, grad_middle, query_gain, key_gain, attn_gain, w_query, w_key, w_value
    )
    shares, gain_part, input_grad = held((shares, gain_part, input_grad))
    chips = n_dp * n_ctx * 2
    whole = across_chips(share_out(shares, gain_part, chips))
    sums = [k.astype(F32) + d.astype(F32) for k, d in ((keep_a, dp_a), (keep_b, dp_b))]
    grad_gate_w = jnp.stack([v[:1024] for v in sums])
    grad_up_w = jnp.stack([v[1024:2048] for v in sums])
    grad_down_w = jnp.stack(
        [v[2048:].reshape(8, 128, 128).transpose(1, 0, 2).reshape(128, 1024) for v in sums]
    )
    outputs = (middle + out_part.astype(F32)).astype(BF)
    whole, outputs, grad_gate_w, grad_up_w, grad_down_w = held(
        (whole, outputs, grad_gate_w, grad_up_w, grad_down_w)
    )
    other = swap(whole, "exp", 1)
    shape = (n_dp, n_ctx, 2, PART, 128)
    done = spread(jnp.reshape(core, (1,)), whole.reshape(shape))
    done = spread(jnp.reshape(1 - core, (1,)), other.reshape(shape), done[:4] + done[5:])
    wq, wk, wv, wo = (v.reshape(1024, -1) for v in done[:4])
    router_grad = done[4].T
    x_gain, q_gain, k_gain, f_gain = (v.reshape(-1) for v in done[5:])
    return (
        outputs[None],
        input_grad[None],
        x_gain,
        wq,
        wk,
        wv,
        q_gain,
        k_gain,
        wo,
        f_gain,
        router_grad,
        grad_gate_w,
        grad_up_w,
        grad_down_w,
    )


def solution(mesh):
    seqs = ("dp", "exp")
    row_spec = P(seqs, "ctx", None)
    in_specs = (row_spec, P(seqs, None), row_spec, row_spec) + (P(),) * 9
    in_specs += (P("ctx", None, "exp"), P("ctx", None, "exp"), P("ctx", "exp", None))
    out_specs = (row_spec, row_spec) + (P(),) * 9
    out_specs += (P("ctx", None, "exp"), P("ctx", None, "exp"), P("ctx", "exp", None))
    return jax.shard_map(
        per_device, mesh=mesh, in_specs=in_specs, out_specs=out_specs, check_vma=False
    )
```

```python
import jax
import jax.numpy as jnp
import numpy as np
from jax import lax
from jax.experimental import pallas as pl
from jax.experimental.pallas import tpu as pltpu
from jax.sharding import PartitionSpec as P

HEADS = 16
KV_HEADS = 8
HEAD_DIM = 64
EXPERTS = 32
CAP = 40
EPSILON = 1e-06
MASKED = -1e30
BF = jnp.bfloat16
F32 = jnp.float32
RUN = 64
QB = 512
QB_BACK = 256
PART = 208
BASE = 256
MIB = 1024 * 1024
NT = ((1,), (1,))
TN = ((0,), (0,))
VM = pl.BlockSpec(memory_space=pltpu.VMEM)
SM = pl.BlockSpec(memory_space=pltpu.SMEM)


def dot(a, b, dims=((1,), (0,))):
    return lax.dot_general(a, b, (dims, ((), ())), preferred_element_type=F32)


def call(kernel, outs, ins, name, flops, moved, scratch=(), transcendentals=0, vmem=62):
    return pl.pallas_call(
        kernel,
        out_shape=outs,
        in_specs=ins,
        out_specs=jax.tree.map(lambda _: VM, outs),
        scratch_shapes=list(scratch),
        compiler_params=pltpu.CompilerParams(vmem_limit_bytes=vmem * MIB),
        cost_estimate=pl.CostEstimate(
            flops=flops, bytes_accessed=moved, transcendentals=transcendentals
        ),
        name=name,
    )


def like(shape, dtype):
    return jax.ShapeDtypeStruct(shape, dtype)


def inverse_rms(value):
    return lax.rsqrt(jnp.mean(value * value, axis=-1, keepdims=True) + EPSILON)


def row_of(ref):
    return ref[...].astype(F32).reshape(1, -1)


def lanes_of(rows):
    return lax.broadcasted_iota(jnp.int32, (rows, 128), 1)


def swap_halves(tile):
    return pltpu.roll(tile.astype(F32), 64, 1)


def pack_head(wide, head):
    tile = wide[:, 128 * (head // 2) : 128 * (head // 2 + 1)]
    low = lanes_of(RUN) < 64
    if head % 2 == 0:
        return jnp.where(low, tile[:RUN], swap_halves(tile[RUN:]))
    return jnp.where(low, swap_halves(tile[:RUN]), tile[RUN:])


def unpack_heads(even, odd):
    low = lanes_of(RUN) < 64
    even, odd = even.astype(F32), odd.astype(F32)
    return jnp.concatenate(
        [jnp.where(low, even, swap_halves(odd)), jnp.where(low, swap_halves(even), odd)], axis=0
    )


def turn_tables(seq):
    half = HEAD_DIM // 2
    frequency = (10000.0 ** (-np.arange(half) * 2.0 / HEAD_DIM)).astype(np.float32)
    angles = (np.arange(seq, dtype=np.float32)[:, None] * frequency[None, :]).astype(np.float64)
    cosine, sine = np.cos(angles), np.sin(angles)
    return np.concatenate([cosine, cosine, -sine, sine], axis=1).astype(np.float32)


def split_table(table):
    low = lanes_of(table.shape[0]) < 64
    return jnp.where(low, table, 1.0), jnp.where(low, pltpu.roll(table, 64, 1), 0.0)


def turn(tile, cosine, sine):
    other = jnp.where(lanes_of(tile.shape[0]) < 32, pltpu.roll(tile, 96, 1), pltpu.roll(tile, 32, 1))
    return tile * cosine + other * sine


def pre_kernel(x_ref, gain, wq, wk, wv, q_gain, k_gain, picks, send, first_out, turned_out, q_out, k_out):
    x = x_ref[...].astype(F32)
    wide = x * inverse_rms(x) * row_of(gain)
    first = wide.astype(BF)
    first_out[...] = first
    q = dot(first, wq[...])
    k = dot(first, wk[...])
    v = dot(first, wv[...])
    q_out[...] = q
    k_out[...] = k
    qn = q * inverse_rms(q) * (row_of(q_gain) * HEAD_DIM ** (-0.5))
    kn = k * inverse_rms(k) * row_of(k_gain)
    low = lanes_of(x.shape[0]) < 64
    for h in range(KV_HEADS):
        cut = slice(128 * (h // 2), 128 * (h // 2 + 1))
        kt, vt = kn[:, cut], v[:, cut]
        if h % 2 == 0:
            both = jnp.where(low, kt, swap_halves(vt))
        else:
            both = jnp.where(low, swap_halves(kt), vt)
        both = both.astype(BF)
        send[2 * h, 0 : 2 * RUN, :] = both
        send[2 * h + 1, 0 : 2 * RUN, :] = both
    lane = lanes_of(x.shape[0])
    rows = jnp.transpose(jnp.where(lane == 0, inverse_rms(q), inverse_rms(k)))[0:2, :]
    high = rows.astype(BF).astype(F32)
    named = jnp.concatenate(
        [picks[...].astype(F32), high, rows - high, jnp.zeros((4, 128), F32)], axis=0
    ).astype(BF)
    for d in range(HEADS):
        send[d, 2 * RUN : 3 * RUN, :] = pack_head(qn, d).astype(BF)
        send[d, 3 * RUN : 3 * RUN + 16, :] = named
    turned_out[...] = jnp.transpose(first.astype(F32)).astype(BF)


def pre(x, gain, wq, wk, wv, q_gain, k_gain, picks):
    rows, width = x.shape
    return call(
        pre_kernel,
        (
            like((HEADS, 3 * RUN + 16, 128), BF),
            like((rows, width), BF),
            like((width, rows), BF),
            like((rows, wq.shape[1]), F32),
            like((rows, wk.shape[1]), F32),
        ),
        [VM] * 8,
        "pre",
        2 * rows * width * 2048,
        6 * 1024 * 1024,
    )(x, gain, wq, wk, wv, q_gain, k_gain, picks)


def turn_over(source, target):
    for i in range(source.shape[0] // 128):
        cut = slice(128 * i, 128 * (i + 1))
        target[:, cut] = jnp.transpose(source[cut, :].astype(F32)).astype(BF)


def masked_scores(kv, q, block):
    scores = dot(kv, q, NT)
    end = scores.shape[0]
    row = lax.broadcasted_iota(jnp.int32, (block, block), 0)
    col = lax.broadcasted_iota(jnp.int32, (block, block), 1)
    last = jnp.where(row <= col, scores[end - block :, :], MASKED)
    return last if end == block else jnp.concatenate([scores[: end - block, :], last], axis=0)


def attend_kernel(order, inv, recv, table, kv_out, q_out, att_out, lse_out, send_out, turned):
    seq = kv_out.shape[0]
    lane = lanes_of(RUN)

    def gather(b, carry):
        s = order[b]
        c = lax.shift_right_logical(s, 1)
        half = jnp.bitwise_and(s, 1)
        rows = pl.ds(pl.multiple_of(b * RUN, RUN), RUN)
        cos, sin = split_table(table[rows, :])
        kv = recv[c, pl.ds(pl.multiple_of(half * RUN, RUN), RUN), :].astype(F32)
        kv_out[rows, :] = turn(kv, cos, sin).astype(BF)
        tile = recv[c, pl.ds(2 * RUN, RUN), :].astype(F32)
        q = jnp.where(lane < 64, jnp.where(half == 0, tile, swap_halves(tile)), 0.0)
        q_out[rows, :] = turn(q, cos, sin).astype(BF)
        return carry

    lax.fori_loop(0, seq // RUN, gather, 0, unroll=32)
    turn_over(kv_out, turned)
    for i in range(seq // QB):
        here = slice(i * QB, (i + 1) * QB)
        end = (i + 1) * QB
        scores = masked_scores(kv_out[:end, :], q_out[here, :], QB)
        top = jnp.max(scores, axis=0, keepdims=True)
        weights = jnp.exp(scores - top)
        total = jnp.sum(weights, axis=0, keepdims=True)
        att = jnp.transpose(dot(turned[:, :end], weights.astype(BF)) / total)
        att_out[here, :] = att.astype(BF)
        lse_out[:, here] = jnp.broadcast_to(top + jnp.log(total), (8, QB))

    def place(c, carry):
        b0, b1 = inv[2 * c], inv[2 * c + 1]
        first = att_out[pl.ds(pl.multiple_of(b0 * RUN, RUN), RUN), :]
        second = att_out[pl.ds(pl.multiple_of(b1 * RUN, RUN), RUN), :]
        send_out[c] = jnp.where(lane < 64, swap_halves(first), second.astype(F32)).astype(BF)
        return carry

    lax.fori_loop(0, send_out.shape[0], place, 0, unroll=16)


def attend(order, inv, recv, table):
    n = recv.shape[0]
    seq = n * 128
    return call(
        attend_kernel,
        (
            like((seq, 128), BF),
            like((seq, 128), BF),
            like((seq, 128), BF),
            like((8, seq), F32),
            like((n, RUN, 128), BF),
        ),
        [SM, SM, VM, VM],
        "attend",
        4 * seq * seq * 128 // 2,
        14 * seq * 128,
        [pltpu.VMEM((128, seq), BF)],
        transcendentals=seq * seq // 2,
    )(order, inv, recv, table)


def attend_back_kernel(
    order, inv, even, recv, kv_in, q_in, att_in, lse_in, table, _,
    send_hbm, kv_grad_out, g_all, dq_all, dkv_all, sums, turned, send_out, sem,
):
    seq = kv_in.shape[0]
    lane = lanes_of(RUN)

    def gather(b, carry):
        s = order[b]
        c = lax.shift_right_logical(s, 1)
        half = jnp.bitwise_and(s, 1)
        tile = recv[c, 0:RUN, :].astype(F32)
        g_all[pl.ds(pl.multiple_of(b * RUN, RUN), RUN), :] = jnp.where(
            lane >= 64, jnp.where(half == 1, tile, swap_halves(tile)), 0.0
        ).astype(BF)
        return carry

    lax.fori_loop(0, seq // RUN, gather, 0, unroll=32)
    turn_over(kv_in, turned)
    steps = seq // QB_BACK
    for i in reversed(range(steps)):
        here = slice(i * QB_BACK, (i + 1) * QB_BACK)
        end = (i + 1) * QB_BACK
        kv, q, g = kv_in[:end, :], q_in[here, :], g_all[here, :]
        offset = jnp.sum(jnp.transpose(att_in[here, :].astype(F32) * g.astype(F32)), axis=0, keepdims=True)
        weights = jnp.exp(masked_scores(kv, q, QB_BACK) - lse_in[0:1, here])
        grad_scores = (weights * (dot(kv, g, NT) - offset)).astype(BF)
        dq_all[here, :] = jnp.transpose(dot(turned[:, :end], grad_scores))
        step = dot(grad_scores, q) + dot(weights.astype(BF), g)
        if i == steps - 1:
            dkv_all[...] = step
        else:
            dkv_all[:end, :] += step

    def place(c, carry):
        b0, b1 = inv[2 * c], inv[2 * c + 1]
        r0 = pl.ds(pl.multiple_of(b0 * RUN, RUN), RUN)
        r1 = pl.ds(pl.multiple_of(b1 * RUN, RUN), RUN)
        cos0, sin0 = split_table(table[r0, :])
        cos1, sin1 = split_table(table[r1, :])
        kv0 = turn(dkv_all[r0, :], cos0, -sin0).astype(BF)
        kv1 = turn(dkv_all[r1, :], cos1, -sin1).astype(BF)
        send_out[c, 0 : RUN, :] = kv0
        send_out[c, RUN : 2 * RUN, :] = kv1
        kv0, kv1 = kv0.astype(F32), kv1.astype(F32)
        values = jnp.where(lane < 64, swap_halves(kv0), kv1)
        keys = jnp.where(lane < 64, kv0, swap_halves(kv1))
        kv_grad_out[c] = jnp.where(even[0] == 1, values, keys).astype(BF)
        both_q = jnp.concatenate([dq_all[r0, :], dq_all[r1, :]], axis=0)
        both_q = both_q * jnp.concatenate([q_in[r0, :], q_in[r1, :]], axis=0).astype(F32)
        both_k = jnp.concatenate([dkv_all[r0, :], dkv_all[r1, :]], axis=0)
        both_k = both_k * jnp.concatenate([kv_in[r0, :], kv_in[r1, :]], axis=0).astype(F32)
        some = jnp.where(lanes_of(8) < 64, 1.0, 0.0).astype(BF)
        sums[pl.ds(c, 1), :] = dot(some, both_q.astype(BF), NT)[0:1, :]
        sums[pl.ds(n + c, 1), :] = dot(some, both_k.astype(BF), NT)[0:1, :]
        q0 = turn(dq_all[r0, :], cos0, -sin0)
        q1 = turn(dq_all[r1, :], cos1, -sin1)
        both = jnp.where(lane < 64, q0, swap_halves(q1))
        send_out[c, 2 * RUN : 3 * RUN, :] = (both * HEAD_DIM ** (-0.5)).astype(BF)
        return carry

    n = send_out.shape[0]
    lax.fori_loop(0, n, place, 0, unroll=16)
    for c in range(n):
        send_out[c, 3 * RUN : 3 * RUN + 2 * n, :] = sums[...].astype(BF)
    copy = pltpu.make_async_copy(send_out, send_hbm.at[:, pl.ds(BASE, 3 * RUN + 2 * n), :], sem)
    copy.start()
    copy.wait()


def attend_back(order, inv, even, recv, kv, q, att, lse, table, begun):
    n = recv.shape[0]
    seq = n * 128
    whole = lambda v: pl.BlockSpec(v.shape, lambda i: (0,) * v.ndim)
    return pl.pallas_call(
        attend_back_kernel,
        grid=(1,),
        out_shape=(like((n, BASE + 3 * RUN + 2 * n, 128), BF), like((n, RUN, 128), BF)),
        in_specs=[SM, SM, SM]
        + [whole(v) for v in (recv, kv, q, att, lse, table)]
        + [pl.BlockSpec(memory_space=pl.ANY)],
        input_output_aliases={9: 0},
        out_specs=(
            pl.BlockSpec(memory_space=pl.ANY),
            pl.BlockSpec((n, RUN, 128), lambda i: (0, 0, 0)),
        ),
        scratch_shapes=[
            pltpu.VMEM((seq, 128), BF),
            pltpu.VMEM((seq, 128), F32),
            pltpu.VMEM((seq, 128), F32),
            pltpu.VMEM((2 * n, 128), F32),
            pltpu.VMEM((128, seq), BF),
            pltpu.VMEM((n, 3 * RUN + 2 * n, 128), BF),
            pltpu.SemaphoreType.DMA,
        ],
        compiler_params=pltpu.CompilerParams(vmem_limit_bytes=62 * MIB),
        cost_estimate=pl.CostEstimate(
            flops=10 * seq * seq * 128 // 2, bytes_accessed=20 * seq * 128, transcendentals=seq * seq // 2
        ),
        name="attend_back",
    )(order, inv, even, recv, kv, q, att, lse, table, begun)


def slot_masks(slot, pair):
    line = lax.broadcasted_iota(jnp.int32, (2 * CAP, 128), 0).astype(F32)
    left = (line < CAP) & (line == slot[2 * pair : 2 * pair + 1, :])
    right = (line >= CAP) & (line - CAP == slot[2 * pair + 1 : 2 * pair + 2, :])
    return jnp.where(left, 1.0, 0.0).astype(BF), jnp.where(right, 1.0, 0.0).astype(BF)


def cotangent_kernel(number, picks_ref, g_ref, rows_ref, slot_ref):
    n_ctx = g_ref.shape[0]
    picks = picks_ref[...].astype(F32)[:, :8, :]
    before = lax.broadcasted_iota(jnp.int32, (128, 128), 0) < lax.broadcasted_iota(
        jnp.int32, (128, 128), 1
    )
    before = jnp.where(before, 1.0, 0.0).astype(BF)
    for a in range(2):
        e = (number[0] + a).astype(F32)
        named = jnp.max(jnp.where(picks == e, 1.0, 0.0), axis=1)
        slot = jnp.where(named > 0.0, dot(named.astype(BF), before), -1.0)
        slot_ref[a] = slot
        for p in range(n_ctx // 2):
            left, right = slot_masks(slot, p)
            rows_ref[a, 2 * CAP * p : 2 * CAP * (p + 1), :] = (
                dot(left, g_ref[2 * p]) + dot(right, g_ref[2 * p + 1])
            ).astype(BF)


def cotangent_rows(number, recv, g_all):
    n_ctx = g_all.shape[0]
    whole = lambda *shape: pl.BlockSpec(shape, lambda i: (0,) * len(shape))
    return pl.pallas_call(
        cotangent_kernel,
        grid=(1,),
        out_shape=(like((2, n_ctx * CAP, 1024), BF), like((2, n_ctx, 128), F32)),
        in_specs=[
            SM,
            pl.BlockSpec((n_ctx, 16, 128), lambda i: (0, 3 * RUN // 16, 0)),
            whole(*g_all.shape),
        ],
        out_specs=(whole(2, n_ctx * CAP, 1024), whole(2, n_ctx, 128)),
        compiler_params=pltpu.CompilerParams(vmem_limit_bytes=62 * MIB),
        cost_estimate=pl.CostEstimate(
            flops=8 * n_ctx * 80 * 128 * 1024, bytes_accessed=8 * 1024 * 1024, transcendentals=0
        ),
        name="cotangent_rows",
    )(number, recv, g_all)


def expert_steps(e, rows_ref, g_ref, router_ref, parts):
    n_ctx = rows_ref.shape[0]
    rows = jnp.concatenate([rows_ref[c, 0].astype(F32) for c in range(n_ctx)], axis=0).astype(BF)
    grads = g_ref[0].astype(F32)
    logits = dot(rows, router_ref[...], NT)
    lane = lax.broadcasted_iota(jnp.int32, logits.shape, 1)
    powers = jnp.exp(logits - jnp.max(logits, axis=1, keepdims=True))
    gate = jnp.sum(jnp.where(lane == e, powers, 0.0), axis=1, keepdims=True) / jnp.sum(
        powers, axis=1, keepdims=True
    )
    w_gate = jnp.concatenate([w[0, 0:1024, :] for w in parts], axis=1)
    w_up = jnp.concatenate([w[0, 1024:2048, :] for w in parts], axis=1)
    w_down = jnp.concatenate(
        [
            jnp.concatenate([w[0, 2048 + 128 * n : 2176 + 128 * n, :] for n in range(8)], axis=1)
            for w in parts
        ],
        axis=0,
    )
    gate_act = dot(rows, w_gate)
    up_act = dot(rows, w_up)
    sig = 1.0 / (1.0 + jnp.exp(-gate_act))
    silu = gate_act * sig
    hidden = (silu * up_act).astype(BF)
    expert_out = dot(hidden, w_down)
    grad_rows = (gate * grads).astype(BF)
    grad_hidden = dot(grad_rows, w_down, NT)
    ga = (grad_hidden * up_act * sig * (1.0 + gate_act * (1.0 - sig))).astype(BF)
    gu = (grad_hidden * silu).astype(BF)
    return rows, grads, gate, w_gate, w_up, hidden, expert_out, grad_rows, ga, gu


def expert_kernel(number, rows_ref, g_ref, router_ref, *refs):
    parts, back_ref = refs[:4], refs[4]
    e = number[0] + pl.program_id(0)
    rows, grads, _, w_gate, w_up, _, expert_out, _, ga, gu = expert_steps(
        e, rows_ref, g_ref, router_ref, parts
    )
    grad_gate = jnp.sum(grads * expert_out, axis=1, keepdims=True)
    back = dot(ga, w_gate, NT) + dot(gu, w_up, NT)
    high = grad_gate.astype(BF).astype(F32)
    lane = lanes_of(rows.shape[0])
    tail = jnp.where(lane == e, high, jnp.where(lane == e + EXPERTS, grad_gate - high, 0.0))
    for c in range(rows_ref.shape[0]):
        cut = slice(CAP * c, CAP * (c + 1))
        back_ref[c, 0, :, 0:1024] = back[cut, :].astype(BF)
        back_ref[c, 0, :, 1024:1152] = tail[cut, :].astype(BF)


def weight_grad_kernel(number, rows_ref, g_ref, router_ref, slot_ref, *refs):
    parts, (keep, near, far, sums_ref) = refs[:4], refs[4:]
    e = number[0] + pl.program_id(0)
    rows, _, gate, _, _, hidden, expert_out, grad_rows, ga, gu = expert_steps(
        e, rows_ref, g_ref, router_ref, parts
    )
    line = lax.broadcasted_iota(jnp.int32, (CAP, 128), 0).astype(F32)
    first = pl.program_id(0) == 0
    out_rows = gate * expert_out
    for c in range(rows_ref.shape[0]):
        mask = jnp.where(line == slot_ref[0, c : c + 1, :], 1.0, 0.0).astype(BF)
        part = dot(mask, out_rows[CAP * c : CAP * (c + 1), :].astype(BF), TN)
        before = jnp.where(first, 0.0, sums_ref[c].astype(F32))
        sums_ref[c] = (part + before).astype(BF)
    gate_grad = dot(rows, ga, TN)
    up_grad = dot(rows, gu, TN)
    down_grad = dot(hidden, grad_rows, TN)
    for j, (ref, at) in enumerate([(keep, 0), (far, 0), (near, 0), (far, 1)]):
        cut = slice(128 * j, 128 * (j + 1))
        ref[at, 0, 0:1024, :] = gate_grad[:, cut].astype(BF)
        ref[at, 0, 1024:2048, :] = up_grad[:, cut].astype(BF)
        for n in range(8):
            ref[at, 0, 2048 + 128 * n : 2176 + 128 * n, :] = down_grad[
                cut, 128 * n : 128 * (n + 1)
            ].astype(BF)


def expert_call(kernel, name, number, rows, grads, router, slots, parts, outs, out_specs):
    n_ctx = rows.shape[0]
    n = n_ctx * CAP
    extra = () if slots is None else (slots,)
    return pl.pallas_call(
        kernel,
        grid=(2,),
        out_shape=outs,
        in_specs=[
            SM,
            pl.BlockSpec((n_ctx, 1, CAP, 1024), lambda i: (0, i, 0, 0)),
            pl.BlockSpec((1, n, 1024), lambda i: (i, 0, 0)),
            pl.BlockSpec(router.shape, lambda i: (0, 0)),
        ]
        + [pl.BlockSpec((1,) + v.shape[1:], lambda i: (i, 0, 0)) for v in extra + tuple(parts)],
        out_specs=out_specs,
        compiler_params=pltpu.CompilerParams(vmem_limit_bytes=62 * MIB),
        cost_estimate=pl.CostEstimate(
            flops=24 * n * 1024 * 512, bytes_accessed=20 * 1024 * 1024, transcendentals=2 * n * 512
        ),
        name=name,
    )(number, rows, grads, router, *extra, *parts)


def experts(number, rows, grads, router, parts):
    n_ctx = rows.shape[0]
    return expert_call(
        expert_kernel, "experts", number, rows, grads, router, None, parts,
        like((n_ctx, 2, CAP, 1152), BF),
        pl.BlockSpec((n_ctx, 1, CAP, 1152), lambda i: (0, i, 0, 0)),
    )


def weight_grads(number, rows, grads, router, slots, parts):
    n_ctx = rows.shape[0]
    put = lambda k: pl.BlockSpec((k, 1, 3072, 128), lambda i: (0, i, 0, 0))
    return expert_call(
        weight_grad_kernel, "weight_grads", number, rows, grads, router, slots, parts,
        (
            like((1, 2, 3072, 128), BF),
            like((1, 2, 3072, 128), BF),
            like((2, 2, 3072, 128), BF),
            like((n_ctx, 128, 1024), BF),
        ),
        (put(1), put(1), put(2), pl.BlockSpec((n_ctx, 128, 1024), lambda i: (0, 0, 0))),
    )


def middle_kernel(heads, x_ref, w_out, gain, spot, attended_out, middle_out, second_out, send_out):
    attended = jnp.concatenate(
        [unpack_heads(heads[2 * t], heads[2 * t + 1]) for t in range(HEADS // 2)], axis=1
    ).astype(BF)
    attended_out[...] = attended
    middle = x_ref[...].astype(F32) + dot(attended, w_out[...])
    middle_out[...] = middle
    second = (middle * inverse_rms(middle) * row_of(gain)).astype(BF)
    second_out[...] = second
    send_out[...] = dot(spot[...], second, TN).astype(BF)


def middle_forward(heads, x, w_out, gain, spot):
    rows, width = x.shape
    return call(
        middle_kernel,
        (
            like((rows, width), BF),
            like((rows, width), F32),
            like((rows, width), BF),
            like((spot.shape[1], width), BF),
        ),
        [VM] * 5,
        "middle",
        2 * rows * width * (1024 + 1280),
        6 * 1024 * 1024,
    )(heads, x, w_out, gain, spot)


def middle_back_kernel(
    spot, back, middle_ref, second, router, gain, g_ref, w_out,
    send, grad_out, branch_out,
):
    summed = dot(spot[...], back[...])
    logits = dot(second[...], router[...], NT)
    powers = jnp.exp(logits - jnp.max(logits, axis=1, keepdims=True))
    probs = powers / jnp.sum(powers, axis=1, keepdims=True)
    last = summed[:, 1024:1152]
    grad_sel = (last + pltpu.roll(last, 128 - EXPERTS, 1))[:, :EXPERTS]
    grad_logits = probs * (grad_sel - jnp.sum(probs * grad_sel, axis=1, keepdims=True))
    high = grad_logits.astype(BF)
    rest = (grad_logits - high.astype(F32)).astype(BF)
    upstream = summed[:, :1024] + dot(high, router[...]) + dot(rest, router[...])
    middle = middle_ref[...]
    r = inverse_rms(middle)
    hat = middle * r
    gain_part = jnp.sum(upstream * hat, axis=0, keepdims=True)
    router_part = dot(high, second[...], TN) + dot(rest, second[...], TN)
    low = lanes_of(EXPERTS) < 64
    first_row = lax.broadcasted_iota(jnp.int32, (EXPERTS, 128), 0) == 0
    for d in range(HEADS):
        cut = slice(128 * (d // 2), 128 * (d // 2 + 1))
        tile = router_part[:, cut]
        part = jnp.where(first_row, jnp.broadcast_to(gain_part[:, cut], (EXPERTS, 128)), 0.0)
        if d % 2 == 0:
            misc = jnp.where(low, tile, swap_halves(part))
        else:
            misc = jnp.where(low, swap_halves(tile), part)
        send[d, RUN : RUN + EXPERTS, :] = misc.astype(BF)
    scaled = upstream * row_of(gain)
    grad = (
        r * (scaled - hat * jnp.mean(scaled * hat, axis=1, keepdims=True)) + g_ref[...].astype(F32)
    )
    grad_out[...] = grad
    branch = grad.astype(BF)
    branch_out[...] = branch
    att = dot(branch, w_out[...], NT)
    for d in range(HEADS):
        send[d, 0:RUN, :] = pack_head(att, d).astype(BF)


def middle_back(spot, back, middle, second, router, gain, g_low, w_out):
    rows, width = middle.shape
    return call(
        middle_back_kernel,
        (
            like((HEADS, RUN + EXPERTS, 128), BF),
            like((rows, width), F32),
            like((rows, width), BF),
        ),
        [VM] * 8,
        "middle_back",
        2 * rows * width * (1280 + 1024),
        6 * 1024 * 1024,
    )(spot, back, middle, second, router, gain, g_low, w_out)


def out_grad_kernel(place, attended, other, branch, other_branch, send_hbm, rows, sem):
    for j in range(4):
        pair = jnp.bitwise_xor(place[0], j % 2) * 2 + jnp.bitwise_xor(place[1], j // 2)
        own = attended[:, pl.ds(pl.multiple_of((2 * pair + place[2]) * 128, 128), 128)]
        far = other[:, pl.ds(pl.multiple_of(pair * 128, 128), 128)]
        part = dot(own, branch[...], TN) + dot(far, other_branch[...], TN)
        for c in range(rows.shape[0]):
            both = part[8 * c : 8 * c + 8, :]
            for m in range(0, 8, 2):
                two = (both[:, 128 * m : 128 * m + 128], both[:, 128 * m + 128 : 128 * m + 256])
                at = 64 * j + 8 * m
                rows[c, at : at + 16, :] = jnp.concatenate(two, axis=0).astype(BF)
    copy = pltpu.make_async_copy(rows, send_hbm.at[:, pl.ds(0, BASE), :], sem)
    copy.start()
    copy.wait()


def out_grads(place, attended, other, branch, other_branch):
    n = HEADS
    whole = lambda v: pl.BlockSpec(v.shape, lambda i: (0,) * v.ndim)
    return pl.pallas_call(
        out_grad_kernel,
        grid=(1,),
        out_shape=like((n, BASE + 3 * RUN + 2 * n, 128), BF),
        in_specs=[SM] + [whole(v) for v in (attended, other, branch, other_branch)],
        out_specs=pl.BlockSpec(memory_space=pl.ANY),
        scratch_shapes=[pltpu.VMEM((n, BASE, 128), BF), pltpu.SemaphoreType.DMA],
        compiler_params=pltpu.CompilerParams(vmem_limit_bytes=62 * MIB),
        cost_estimate=pl.CostEstimate(flops=1 << 20, bytes_accessed=1 << 18, transcendentals=0),
        name="out_grads",
    )(place, attended, other, branch, other_branch)


def queries_of(recv):
    return jnp.concatenate(
        [
            unpack_heads(
                recv[2 * t, BASE + 2 * RUN : BASE + 3 * RUN, :],
                recv[2 * t + 1, BASE + 2 * RUN : BASE + 3 * RUN, :],
            )
            for t in range(HEADS // 2)
        ],
        axis=1,
    )


def keys_values_of(recv):
    low = lanes_of(2 * RUN) < 64
    both = [
        recv[2 * j, BASE : BASE + 2 * RUN, :].astype(F32)
        + recv[2 * j + 1, BASE : BASE + 2 * RUN, :].astype(F32)
        for j in range(KV_HEADS)
    ]
    keys, values = [], []
    for t in range(KV_HEADS // 2):
        keys.append(jnp.where(low, both[2 * t], swap_halves(both[2 * t + 1])))
        values.append(jnp.where(low, swap_halves(both[2 * t]), both[2 * t + 1]))
    return jnp.concatenate(keys, axis=1), jnp.concatenate(values, axis=1)


def input_kernel(
    recv, q_ref, k_ref, x_ref, middle, q_gain, k_gain, gain, wq, wk, wv, out_ref, gain_ref
):
    uq = queries_of(recv)
    uk, dv = keys_values_of(recv)
    q, k = q_ref[...], k_ref[...]
    rq, rk = inverse_rms(q), inverse_rms(k)
    qh, kh = q * rq, k * rk
    uq, uk = uq * row_of(q_gain), uk * row_of(k_gain)
    gq = (rq * (uq - qh * jnp.mean(uq * qh, axis=1, keepdims=True))).astype(BF)
    gk = (rk * (uk - kh * jnp.mean(uk * kh, axis=1, keepdims=True))).astype(BF)
    upstream = dot(gq, wq[...], NT) + dot(gk, wk[...], NT) + dot(dv.astype(BF), wv[...], NT)
    x = x_ref[...].astype(F32)
    r = inverse_rms(x)
    hat = x * r
    x_part = jnp.sum(upstream * hat, axis=0, keepdims=True)
    scaled = upstream * row_of(gain)
    out_ref[...] = middle[...] + r * (scaled - hat * jnp.mean(scaled * hat, axis=1, keepdims=True))
    half = jnp.zeros((1, 64), F32)
    rows = [jnp.concatenate([half, x_part[:, 64 * i : 64 * (i + 1)]], axis=1) for i in range(8)]
    none = jnp.zeros((2, 128), F32)
    more = [x_part[:, 512 + 128 * i : 640 + 128 * i] for i in range(4)]
    gain_ref[...] = jnp.concatenate(rows + [none] + more + [none], axis=0)


def input_back(recv, q, k, x, middle, q_gain, k_gain, gain, wq, wk, wv):
    rows, width = x.shape
    return call(
        input_kernel,
        (like((rows, width), F32), like((16, 128), F32)),
        [VM] * 11,
        "input_back",
        2 * rows * width * 2048,
        8 * 1024 * 1024,
    )(recv, q, k, x, middle, q_gain, k_gain, gain, wq, wk, wv)


def head_grad_kernel(
    place, turned, early, later, queries, kv_other, normed, out_parts, sums_ref, branch, gain_ref, out_ref
):
    n = early.shape[0]
    low = lanes_of(128) < 64
    gain = gain_ref[...]
    sums = sums_ref[0].astype(F32)
    others = branch[0].astype(F32)
    for c in range(1, n):
        sums = sums + sums_ref[c].astype(F32)
        others = others + branch[c].astype(F32)
    out_rows = out_parts[0].astype(F32)
    for c in range(1, n):
        out_rows = out_rows + out_parts[c].astype(F32)
    q_means = sums[0:n, :] / (HEADS * HEAD_DIM)
    k_means = sums[n : 2 * n, :] / (KV_HEADS * HEAD_DIM)
    total = None
    gains = None
    for p in range(n // 2):
        parts = []
        for c in (2 * p, 2 * p + 1):
            packed = queries[c].astype(F32)
            uq = jnp.concatenate([packed, swap_halves(packed)], axis=0)
            both = jnp.concatenate([early[c].astype(F32), later[c].astype(F32)], axis=0)
            other = kv_other[c].astype(F32)
            other = jnp.concatenate([swap_halves(other), other], axis=0)
            keys = swap_halves(both) + other
            upstream = jnp.where(low, uq, keys)
            packed = normed[c, 2 * RUN : 3 * RUN, :].astype(F32)
            qn = jnp.concatenate([packed, swap_halves(packed)], axis=0) * HEAD_DIM**0.5
            hat = jnp.where(low, qn, swap_halves(normed[c, 0 : 2 * RUN, :])) / gain
            factors = normed[c, 3 * RUN : 3 * RUN + 16, :].astype(F32)
            factors = factors[8:10, :] + factors[10:12, :]
            rows = jnp.concatenate(
                [factors, q_means[c : c + 1, :], k_means[c : c + 1, :], jnp.zeros((4, 128), F32)], axis=0
            )
            cols = jnp.transpose(jnp.concatenate([rows] * 16, axis=0))
            r = jnp.where(low, cols[:, 0:1], cols[:, 1:2])
            m = jnp.where(low, cols[:, 2:3], cols[:, 3:4])
            grad = r * (upstream * gain - hat * m)
            part = jnp.sum(upstream * hat, axis=0, keepdims=True)
            gains = part if gains is None else gains + part
            parts.append(jnp.where(low | (place[3] == 1), grad, both + other).astype(BF))
        left = jnp.concatenate([turned[2 * p], turned[2 * p + 1]], axis=1)
        step = dot(left, jnp.concatenate(parts, axis=0))
        total = step if total is None else total + step
    low_row = low[0:1, :]
    gains = jnp.where(low_row | (place[3] == 1), gains, 0.0)
    ffn = jnp.where(low_row, swap_halves(others[0:8, :])[0:1, :], 0.0)
    rows = jnp.concatenate([gains, ffn, jnp.zeros((6, 128), F32)], axis=0)
    some = lanes_of(8) < 64
    for s in range(8):
        out_ref[s, 0:128, :] = total[128 * s : 128 * (s + 1), :].astype(BF)
        kept = jnp.where(some, others[8 * (s // 2) : 8 * (s // 2) + 8, :], 0.0)
        out_ref[s, 128:144, :] = jnp.concatenate(
            [kept, rows if s == 0 else jnp.zeros((8, 128), F32)], axis=0
        ).astype(BF)
        out_ref[s, 144:PART, :] = jnp.zeros((64, 128), BF)
    for j in range(4):
        at = jnp.bitwise_xor(place[0], j % 2) * 4 + jnp.bitwise_xor(place[1], j // 2) * 2 + place[2]
        out_ref[pl.ds(at, 1), 144:PART, :] = out_rows[64 * j : 64 * j + 64, :].astype(BF)[None]


def head_grads(place, turned, own, kv_other, normed, grads, branch, gain):
    whole = lambda v: pl.BlockSpec(v.shape, lambda i: (0,) * v.ndim)
    n = own.shape[0]
    part = lambda rows, at: pl.BlockSpec((n, rows, 128), lambda i: (0, at // rows, 0))
    return pl.pallas_call(
        head_grad_kernel,
        grid=(1,),
        out_shape=like((8, PART, 128), BF),
        in_specs=[
            SM,
            whole(turned),
            part(RUN, BASE),
            part(RUN, BASE + RUN),
            part(RUN, BASE + 2 * RUN),
            whole(kv_other),
            whole(normed),
            part(BASE, 0),
            part(2 * n, BASE + 3 * RUN),
            part(EXPERTS, RUN),
            whole(gain),
        ],
        out_specs=pl.BlockSpec((8, PART, 128), lambda i: (0, 0, 0)),
        compiler_params=pltpu.CompilerParams(vmem_limit_bytes=62 * MIB),
        cost_estimate=pl.CostEstimate(
            flops=2 * 2048 * 1024 * 128, bytes_accessed=8 * 1024 * 1024, transcendentals=0
        ),
        name="head_grads",
    )(place, turned, own, own, own, kv_other, normed, grads, grads, branch, gain)


def share_kernel(shares, gain_ref, out_ref):
    total = shares[0].astype(F32)
    for s in range(1, shares.shape[0]):
        total = total + shares[s].astype(F32)
    total = jnp.concatenate([total[0:128], total[128:144] + gain_ref[...], total[144:PART]], axis=0)
    total = total.astype(BF)
    for c in range(out_ref.shape[0]):
        out_ref[c] = total


def share_out(shares, gain, chips):
    return call(
        share_kernel,
        like((chips, PART, 128), BF),
        [VM, VM],
        "share_out",
        1 << 18,
        4 * 1024 * 1024,
    )(shares, gain)


def spread_kernel(place, block_ref, *refs):
    wq, wk, wv, wo, router, x_gain, q_gain, k_gain, f_gain = refs[-9:]
    n = block_ref.shape[1]
    low = lanes_of(128) < 64
    some = lanes_of(8) < 64
    total = None
    kept = None
    queries, keys, seconds = [], [], []
    for c in range(0, n, 2):
        even, odd = block_ref[0, c, 0].astype(F32), block_ref[0, c + 1, 0].astype(F32)
        wide = slice(64 * c, 64 * c + 128)
        wq[0, 0, :, wide] = jnp.where(low, even[:128], swap_halves(odd[:128]))
        key, value = even[:128], odd[:128]
        if c % 4 == 0:
            kept = (swap_halves(key), swap_halves(value))
        else:
            half = slice(32 * c - 64, 32 * c + 64)
            wk[0, 0, :, half] = jnp.where(low, kept[0], key)
            wv[0, 0, :, half] = jnp.where(low, kept[1], value)
        router[:, wide] = jnp.where(some, even[128:136], swap_halves(odd[128:136]))
        sums = even[128:144] + odd[128:144]
        total = sums if total is None else total + sums
        pairs = jnp.where(some, even[136:144], swap_halves(odd[136:144]))
        queries.append(pairs[0:1])
        seconds.append(pairs[1:2])
        if c % 4 == 0:
            key_gain = swap_halves(even[136:144])
        else:
            keys.append(jnp.where(some, key_gain, even[136:144])[0:1])
        for d, block in ((c, even), (c + 1, odd)):
            for m in range(8):
                wo[0, 0, 8 * d : 8 * d + 8, 128 * m : 128 * (m + 1)] = block[144 + 8 * m : 152 + 8 * m]
    turned = swap_halves(total)
    firsts = [
        jnp.where(some[0:1], turned[2 * t : 2 * t + 1], total[2 * t + 1 : 2 * t + 2]) for t in range(4)
    ]
    firsts = jnp.concatenate(firsts + [total[10 + t : 11 + t] for t in range(4)], axis=1)

    @pl.when(pl.program_id(0) == 0)
    def _():
        ours = place[0] == 0
        given = refs[4:8] if len(refs) > 9 else None
        for i, (ref, made) in enumerate([(x_gain, None), (q_gain, queries), (k_gain, keys), (f_gain, seconds)]):
            old = jnp.zeros(ref.shape, F32) if given is None else given[i][...]
            ref[...] = old if made is None else jnp.where(ours, jnp.concatenate(made, axis=1), old)

    x_gain[...] += firsts


def spread(place, block, before=None):
    dp, n, y = block.shape[:3]
    steps = dp * y
    put = lambda rows, width: pl.BlockSpec((1, 1, rows, width), lambda i, at: (i, at[0], 0, 0))
    sizes = [(128, 1024), (128, 512), (128, 512), (128, 1024)]
    widths = [1024, 1024, 512, 1024]
    small = [pl.BlockSpec((1, w), lambda i, at: (0, 0)) for w in widths]
    given = () if before is None else tuple(before)
    return pl.pallas_call(
        spread_kernel,
        grid_spec=pltpu.PrefetchScalarGridSpec(
            num_scalar_prefetch=1,
            grid=(steps,),
            in_specs=[pl.BlockSpec((1, n, 1, PART, 128), lambda i, at: (i // y, 0, i % y, 0, 0))]
            + ([pl.BlockSpec(memory_space=pl.ANY)] * 4 + small if given else []),
            out_specs=[put(*size) for size in sizes]
            + [pl.BlockSpec((8, 1024), lambda i, at: (i, 0))]
            + small,
        ),
        out_shape=[like((steps, 2) + size, F32) for size in sizes]
        + [like((8 * steps, 1024), F32)]
        + [like((1, w), F32) for w in widths],
        input_output_aliases={2 + i: i for i in range(4 if given else 0)},
        compiler_params=pltpu.CompilerParams(vmem_limit_bytes=62 * MIB),
        name="spread",
    )(place, block, *given)


def by_ctx(value):
    return lax.all_to_all(value, "ctx", split_axis=0, concat_axis=0, tiled=True)


def swap(value, axis, bit):
    n = lax.axis_size(axis)
    return lax.ppermute(value, axis, [(i, i ^ bit) for i in range(n)])


def swap_y(value):
    n = lax.axis_size("dp") * lax.axis_size("exp")
    return lax.ppermute(value, ("dp", "exp"), [(i, i ^ 6) for i in range(n)])


def held(value):
    return lax.optimization_barrier(value)


def across_chips(value):
    axes = ("dp", "ctx", "exp")
    dp, ctx, exp = (lax.axis_size(a) for a in axes)
    groups = [
        [(d * ctx + c) * exp + 2 * y + core for d in range(dp) for c in range(ctx) for y in range(exp // 2)]
        for core in range(2)
    ]
    return lax.all_to_all(
        value, axes, split_axis=0, concat_axis=0, tiled=True, axis_index_groups=groups
    )


def per_device(
    tokens,
    places,
    choices,
    cotangent,
    attn_gain,
    w_query,
    w_key,
    w_value,
    query_gain,
    key_gain,
    w_out,
    ffn_gain,
    w_router,
    w_gate,
    w_up,
    w_down,
):
    x_low = tokens[0]
    rows = x_low.shape[0]
    ctx = lax.axis_index("ctx")
    exp = lax.axis_index("exp")
    n_ctx = lax.axis_size("ctx")
    n_dp = lax.axis_size("dp")
    core = jnp.bitwise_and(exp, 1).astype(jnp.int32)
    picked = choices[0]
    g_low = cotangent[0]

    inv = places[0, ::RUN] // RUN
    runs = jnp.arange(inv.shape[0], dtype=jnp.int32)
    order = jnp.sum(jnp.where(inv[None, :] == runs[:, None], runs[None, :], 0), axis=1)
    table = jnp.asarray(turn_tables(places.shape[1]))

    chosen = jnp.any(picked[:, :, None] == jnp.arange(EXPERTS, dtype=jnp.int32), axis=1)
    tri = jnp.asarray(np.tril(np.ones((rows, rows), np.float32), -1), BF)
    slot = dot(tri, chosen.astype(BF))
    slot = jnp.where(chosen, slot, -1.0).astype(BF)
    column = np.arange(EXPERTS * CAP)
    named = (np.arange(EXPERTS)[:, None] == (column // CAP)[None, :]).astype(np.float32)
    at = dot(slot, jnp.asarray(named, BF))
    spot = (at == jnp.asarray(column % CAP, F32)[None, :]).astype(BF)

    send, first_low, first_turned, q_proj, k_proj = pre(
        x_low, attn_gain, w_query, w_key, w_value, query_gain, key_gain, picked.T
    )
    g_all = lax.all_gather(g_low, "ctx")
    recv = by_ctx(send)
    recv, spot = held((recv, spot))
    kv_all, q_all, att_all, lse_all, att_send = attend(order, inv, recv, table)
    att_send, w_gate, w_up, w_down = held((att_send, w_gate, w_up, w_down))
    down_blocks = w_down.reshape(2, 128, 8, 128).transpose(0, 2, 1, 3).reshape(2, 1024, 128)
    mine = held(jnp.concatenate([w_gate, w_up, down_blocks], axis=1))
    over_y = swap_y(mine)
    over_core = swap(mine, "exp", 1)
    heads = by_ctx(att_send)
    heads, mine, first_turned = held((heads, mine, first_turned))
    turned_all = lax.all_gather(first_turned, "ctx")
    over_both = swap(over_y, "exp", 1)
    router = w_router.T
    attended, middle, second_low, rows_send = middle_forward(heads, x_low, w_out, ffn_gain, spot)
    sent = by_ctx(rows_send.reshape(n_ctx, 2, CAP, -1))
    number = jnp.reshape(2 * ctx, (1,)).astype(jnp.int32)
    g_rows, slots = cotangent_rows(number, recv, g_all)
    halves = attended.reshape(rows, 4, 2, 128)
    halves = lax.dynamic_index_in_dim(halves, 1 - core, axis=2, keepdims=False).reshape(rows, 512)
    halves = swap(halves, "exp", 1)
    sent, over_core, over_both, g_rows, halves = held((sent, over_core, over_both, g_rows, halves))
    parts = (mine, over_core, over_y, over_both)
    back = experts(number, sent, g_rows, router, parts)
    back = by_ctx(back).reshape(EXPERTS * CAP, -1)
    add = lambda *parts: sum(p.astype(F32) for p in parts).astype(BF)
    keep, near, far, out_part = weight_grads(number, sent, g_rows, router, slots, parts)
    back, near, keep, far, out_part, turned_all = held((back, near, keep, far, out_part, turned_all))
    out_part = lax.psum_scatter(out_part, "ctx", scatter_dimension=0, tiled=False)
    far = swap(far, "exp", 1)
    att_grad_send, grad_middle, branch = middle_back(
        spot, back, middle, second_low, router, ffn_gain, g_low, w_out
    )
    grad_recv = by_ctx(att_grad_send)
    even = 1 - jnp.bitwise_and(ctx, 1).astype(jnp.int32)
    place = jnp.stack([lax.axis_index("dp"), exp // 2, core, even]).astype(jnp.int32)
    other_branch = swap(grad_middle.astype(BF), "exp", 1)
    begun = out_grads(place, attended, halves, branch, other_branch)
    near_a, near_b = (add(near[0, a], far[1, a]) for a in range(2))
    keep_a, keep_b = (add(keep[0, a], far[0, a]) for a in range(2))
    grad_recv, near_a, near_b, keep_a, keep_b, begun = held(
        (grad_recv, near_a, near_b, keep_a, keep_b, begun)
    )
    near_a = swap_y(near_a)
    near_b = swap_y(near_b)
    grad_send, kv_own = attend_back(
        order, inv, place[3:], grad_recv, kv_all, q_all, att_all, lse_all, table, begun
    )
    kv_other = swap(kv_own, "ctx", 1)
    grads = by_ctx(grad_send)
    keep_a = held(add(keep_a, near_a))
    dp_a = swap(keep_a, "dp", 1)
    keep_b = held(add(keep_b, near_b))
    dp_b = swap(keep_b, "dp", 1)
    grads, keep_a, keep_b, kv_other, dp_a = held((grads, keep_a, keep_b, kv_other, dp_a))
    own_gain = jnp.concatenate(
        [
            lax.dynamic_slice_in_dim(query_gain, ctx * HEAD_DIM, HEAD_DIM),
            lax.dynamic_slice_in_dim(key_gain, ctx // 2 * HEAD_DIM, HEAD_DIM),
        ]
    ).astype(F32)[None]
    shares = head_grads(
        place, turned_all, grad_send, kv_other, recv, grads, grad_recv, own_gain
    )
    shares, dp_b = held((shares, dp_b))
    shares = lax.all_to_all(shares, ("dp", "exp"), split_axis=0, concat_axis=0, tiled=True)
    input_grad, gain_part = input_back(
        grads, q_proj, k_proj, x_low, grad_middle, query_gain, key_gain, attn_gain, w_query, w_key, w_value
    )
    shares, gain_part, input_grad = held((shares, gain_part, input_grad))
    chips = n_dp * n_ctx * 2
    whole = across_chips(share_out(shares, gain_part, chips))
    sums = [k.astype(F32) + d.astype(F32) for k, d in ((keep_a, dp_a), (keep_b, dp_b))]
    grad_gate_w = jnp.stack([v[:1024] for v in sums])
    grad_up_w = jnp.stack([v[1024:2048] for v in sums])
    grad_down_w = jnp.stack(
        [v[2048:].reshape(8, 128, 128).transpose(1, 0, 2).reshape(128, 1024) for v in sums]
    )
    outputs = (middle + out_part.astype(F32)).astype(BF)
    whole, outputs, grad_gate_w, grad_up_w, grad_down_w = held(
        (whole, outputs, grad_gate_w, grad_up_w, grad_down_w)
    )
    other = swap(whole, "exp", 1)
    shape = (n_dp, n_ctx, 2, PART, 128)
    done = spread(jnp.reshape(core, (1,)), whole.reshape(shape))
    done = spread(jnp.reshape(1 - core, (1,)), other.reshape(shape), done[:4] + done[5:])
    wq, wk, wv, wo = (v.reshape(1024, -1) for v in done[:4])
    router_grad = done[4].T
    x_gain, q_gain, k_gain, f_gain = (v.reshape(-1) for v in done[5:])
    return (
        outputs[None],
        input_grad[None],
        x_gain,
        wq,
        wk,
        wv,
        q_gain,
        k_gain,
        wo,
        f_gain,
        router_grad,
        grad_gate_w,
        grad_up_w,
        grad_down_w,
    )


def solution(mesh):
    seqs = ("dp", "exp")
    row_spec = P(seqs, "ctx", None)
    in_specs = (row_spec, P(seqs, None), row_spec, row_spec) + (P(),) * 9
    in_specs += (P("ctx", None, "exp"), P("ctx", None, "exp"), P("ctx", "exp", None))
    out_specs = (row_spec, row_spec) + (P(),) * 9
    out_specs += (P("ctx", None, "exp"), P("ctx", None, "exp"), P("ctx", "exp", None))
    return jax.shard_map(
        per_device, mesh=mesh, in_specs=in_specs, out_specs=out_specs, check_vma=False
    )
```
